32 devices in a mesh: parts: 2 (over y), gx: 4 (over z), gy: 4 (over x, core).
Axes of the slice: x: 2, y: 2, z: 4, core: 2. Of those that a mesh axis runs over, the one named last changes fastest.
Arguments:
- force: float32 [3, 17, 48, 512], P(None, None, ('parts', 'gx'), 'gy'), parts along dimension 2, may hold values from -6 to 6
- phase: int32 [16, 48, 512], P(None, ('parts', 'gx'), 'gy'), parts along dimension 1, may hold values from 0 to 3
- fixed: int32 [17, 48, 512], P(None, ('parts', 'gx'), 'gy'), parts along dimension 1, may hold values 0 or 1
Outputs:
- displacement: float32 [3, 17, 48, 512], P(None, None, ('parts', 'gx'), 'gy'), parts along dimension 2
- sensitivity: float32 [16, 48, 512], P(None, ('parts', 'gx'), 'gy'), parts along dimension 1
The draws below stay inside these ranges and needn't reach their ends.
There are 2 independent parts, one for each index of `parts`. The reference program is written for one: setup_inputs(seed, part) draws one part's arguments, and reference() takes and returns one part's arrays. A program takes and returns all parts, laid end to end along the dimension named above; each array names one. Nothing has to cross between parts.
All inputs are finite; a program needn't handle non-finite values. No bound on the sum of `fixed` on one device may be relied on, other than what follows from the above.
Results may differ from the reference program's by a relative error of at most 0.0003.
Values sent between devices are 32-bit elements; how exact they have to be, the bound alone decides.
No kernel may reach another device: no remote copies, remote signals or barrier semaphores. Data moves between devices by JAX's collectives and lax.ppermute only.
A program may use at most 64 MiB of HBM per device.

```python
import math
import jax
import jax.numpy as jnp
import numpy as np
from jax import lax

NZ = 16
ITERS = 2
NX = 24
NY = 512


def set_ends(entries, key, smallest, high):
    place = [jax.random.randint(jax.random.fold_in(key, axis), (), 0, length) for axis, length in enumerate(entries.shape)]
    widest = entries.shape.index(max(entries.shape))
    next_to = place[:widest] + [(place[widest] + 1) % entries.shape[widest]] + place[widest + 1:]
    return entries.at[tuple(place)].set(smallest).at[tuple(next_to)].set(high)


def steps_of(key, extent, pieces, smallest, top_value):
    level, own = 1.0, jax.random.fold_in(key, 6)
    for dim, shards_of in pieces:
        draws = jnp.exp(jax.random.uniform(jax.random.fold_in(own, dim), (shards_of,), jnp.float32, smallest / len(pieces), top_value / len(pieces)))
        level = level * jnp.repeat(draws, extent[dim] // shards_of).reshape([-1 if axis == dim else 1 for axis in range(len(extent))])
    return level


def scatter_about(key, extent, width, most, cuts=(), held_as=jnp.bfloat16):
    values = jax.random.normal(key, extent, jnp.float32) * width
    if len(cuts) > 0:
        values = steps_of(key, extent, cuts, -0.22, 0.18) * values
    return jnp.clip(values, min=-most, max=most).astype(held_as)


def setup_inputs(seed: int = 0, part: int = 0) -> dict:
    seeds = jax.random.split(jax.random.key(seed), 4)
    part_splits = jax.random.split(jax.random.fold_in(seeds[3], part), 4)
    force = scatter_about(part_splits[0], (3, NZ + 1, NX, NY), 1.0, 6.0, ((2, 4), (3, 4)), jnp.float32)
    phase = set_ends(jax.random.randint(part_splits[1], (NZ, NX, NY), 0, 4), jax.random.fold_in(part_splits[1], 1), 0, 3).astype(jnp.int32)
    fixed = set_ends((jax.random.randint(part_splits[2], (NZ + 1, NX, NY), 0, 8) < 1).astype(jnp.int32), jax.random.fold_in(part_splits[2], 1), 0, 1)
    return dict(force=force, phase=phase, fixed=fixed)


corner_list = tuple(((a, b, c) for a in (0, 1) for b in (0, 1) for c in (0, 1)))
phase_stiffness = (0.125, 0.343, 0.614, 1.0)
phase_slope = (0.75, 1.47, 2.17, 3.0)

def element_matrix():
    poisson = 0.3
    lame_first = poisson / ((1.0 + poisson) * (1.0 - 2.0 * poisson))
    shear = 1.0 / (2.0 * (1.0 + poisson))
    elastic = np.zeros((6, 6))
    elastic[:3, :3] = lame_first
    for index in range(3):
        elastic[index, index] += 2.0 * shear
        elastic[3 + index, 3 + index] = shear
    gauss_points = (0.5 - 0.5 / math.sqrt(3.0), 0.5 + 0.5 / math.sqrt(3.0))
    stiffness = np.zeros((24, 24))
    for first in gauss_points:
        for second in gauss_points:
            for third in gauss_points:
                point = (first, second, third)
                strain_map = np.zeros((6, 24))
                for node, bits in enumerate(corner_list):
                    grads = []
                    for axis in range(3):
                        factor = 1.0
                        for other in range(3):
                            if other == axis:
                                factor *= 1.0 if bits[other] else -1.0
                            else:
                                factor *= point[other] if bits[other] else 1.0 - point[other]
                        grads.append(factor)
                    for axis in range(3):
                        strain_map[axis, 3 * node + axis] = grads[axis]
                    strain_map[3, 3 * node + 1] = grads[2]
                    strain_map[3, 3 * node + 2] = grads[1]
                    strain_map[4, 3 * node + 0] = grads[2]
                    strain_map[4, 3 * node + 2] = grads[0]
                    strain_map[5, 3 * node + 0] = grads[1]
                    strain_map[5, 3 * node + 1] = grads[0]
                stiffness += strain_map.T @ elastic @ strain_map / 8.0
    return stiffness

def phase_values(phase, table):
    total = jnp.zeros(phase.shape, jnp.float32)
    for index, value in enumerate(table):
        total = total + jnp.where(phase == index, jnp.float32(value), jnp.float32(0.0))
    return total

def layer_corners(slab):
    return jnp.concatenate([jnp.roll(slab[:, a], (-b, -c), (1, 2)) for a, b, c in corner_list], 0)

def layer_spread(terms):
    lower = jnp.zeros(terms[:3].shape, jnp.float32)
    upper = jnp.zeros(terms[:3].shape, jnp.float32)
    for node, (a, b, c) in enumerate(corner_list):
        piece = jnp.roll(terms[3 * node:3 * node + 3], (b, c), (1, 2))
        if a == 0:
            lower = lower + piece
        else:
            upper = upper + piece
    return jnp.stack([lower, upper], 1)

def element_forces(stiff, stacked):
    flat = jnp.dot(stiff, stacked.reshape(24, -1), precision=lax.Precision.HIGHEST)
    return flat.reshape(stacked.shape)

def assemble(make, scale, field_shape):

    def layer(k, total):
        k = k.astype(jnp.int32)
        terms = make(k) * lax.dynamic_index_in_dim(scale, k, 0, keepdims=False)[None]
        now = lax.dynamic_slice_in_dim(total, k, 2, 1)
        return lax.dynamic_update_slice_in_dim(total, now + layer_spread(terms), k, 1)
    return lax.fori_loop(0, scale.shape[0], layer, jnp.zeros(field_shape, jnp.float32))

def reference(force, phase, fixed):
    stiff = jnp.asarray(element_matrix(), jnp.float32)
    free = (1 - fixed).astype(jnp.float32)[None]
    scale = phase_values(phase, phase_stiffness)
    slope = phase_values(phase, phase_slope)
    field_shape = force.shape

    def operate(field):
        masked = free * field

        def make(k):
            slab = lax.dynamic_slice_in_dim(masked, k, 2, 1)
            return element_forces(stiff, layer_corners(slab))
        return free * assemble(make, scale, field_shape) + (1.0 - free) * field
    diag_entries = jnp.diagonal(stiff)[:, None, None]

    def make_diag(k):
        return jnp.broadcast_to(diag_entries, (24,) + scale.shape[1:])
    diag = free * assemble(make_diag, scale, field_shape) + (1.0 - free)
    rhs = free * force
    displacement = jnp.zeros_like(rhs)
    residual = rhs
    direction = residual / diag
    norm_now = jnp.sum(residual * residual / diag)
    for step in range(ITERS):
        image = operate(direction)
        alpha = norm_now / jnp.sum(direction * image)
        displacement = displacement + alpha * direction
        residual = residual - alpha * image
        if step + 1 < ITERS:
            norm_next = jnp.sum(residual * residual / diag)
            direction = residual / diag + norm_next / norm_now * direction
            norm_now = norm_next

    def energy_layer(k):
        slab = lax.dynamic_slice_in_dim(displacement, k, 2, 1)
        stacked = layer_corners(slab)
        return lax.optimization_barrier(jnp.sum(stacked * element_forces(stiff, stacked), 0))
    energies = lax.map(energy_layer, jnp.arange(phase.shape[0], dtype=jnp.int32))
    return (displacement, -slope * energies)
```

```python
import functools

import jax
import jax.numpy as jnp
import numpy as np
from jax import lax
from jax.experimental import pallas as pl
from jax.experimental.pallas import tpu as pltpu
from jax.sharding import PartitionSpec as P

PHASE_STIFFNESS = (0.125, 0.343, 0.614, 1.0)
PHASE_SLOPE = (0.75, 1.47, 2.17, 3.0)
POISSON = 0.3
LAME = POISSON / ((1.0 + POISSON) * (1.0 - 2.0 * POISSON))
SHEAR = 1.0 / (2.0 * (1.0 + POISSON))
KE_DIAGONAL = (LAME + 4.0 * SHEAR) / 9.0

SLOT = 24
LANES = 128
FULL = 168
CORNERS = 152

VMEM = pl.BlockSpec(memory_space=pltpu.VMEM)
PARAMS = pltpu.CompilerParams(vmem_limit_bytes=32 * 1024 * 1024)


def lanes():
    return lax.broadcasted_iota(jnp.int32, (8, LANES), 1)


def sublanes():
    return lax.broadcasted_iota(jnp.int32, (8, LANES), 0)


def table(phase, values):
    out = jnp.full(phase.shape, values[3], jnp.float32)
    for index in (2, 1, 0):
        out = jnp.where(phase == index, jnp.float32(values[index]), out)
    return out


def lane_roll(x, by):
    if isinstance(by, int):
        by = by % LANES
        return x if by == 0 else pltpu.roll(x, by, 1)
    return pltpu.roll(x, lax.rem(by + LANES, LANES), 1)


def is_even(axis):
    return lax.rem(lax.axis_index(axis), 2) == 0


def pack_kernel(paired_x, paired_y, force, phase, fixed, col1, col2, row1, row2, pad):
    comps, nodes, rows, width = force.shape
    layers = nodes - 1
    lane = lanes()
    even_x = is_even("gx") if paired_x else True
    even_y = is_even("gy") if paired_y else True
    zero = jnp.zeros((8, LANES), jnp.float32)
    low = [zero, zero]
    high = [zero, zero]
    pad[...] = jnp.zeros(pad.shape, jnp.float32)

    def place(planes, tile, column, plane, slot, k):
        target = slot * SLOT + k
        planes[plane] = jnp.where(lane == target, lane_roll(tile, target - column), planes[plane])

    def put(at_low, at_high, value_low, value_high):
        if paired_x:
            if value_high is None:
                value_high = jnp.zeros((1, LANES), jnp.float32)
            row1[at_low : at_low + 1, :] = jnp.where(even_x, value_high, value_low)
            row2[at_low : at_low + 1, :] = jnp.where(even_x, value_low, value_high)
        else:
            row1[at_low : at_low + 1, :] = value_low
            row2[at_low : at_low + 1, :] = jnp.zeros((1, LANES), jnp.float32) if value_high is None else value_high

    for k in range(nodes):
        free = (1 - fixed[k]).astype(jnp.float32)
        for c in range(comps):
            q = c * nodes + k
            r0 = free * force[c, k]
            pad[q, 0:rows, :] = r0
            tile = pad[q]
            place(low, tile, 0, 0, c, k)
            place(low, tile, 1, 1, c, k)
            place(high, tile, width - 1, 0, c, k)
            put(q, q, r0[0:1], r0[rows - 1 : rows])
            put(comps * nodes + 2 * layers + q, None, r0[1:2], None)
        pad[comps * nodes, 0:rows, :] = free
        place(low, pad[comps * nodes], 0, 0, 3, k)
        put(2 * comps * nodes + 2 * layers + k, None, free[0:1], None)
        if k < layers:
            scale = table(phase[k], PHASE_STIFFNESS)
            pad[comps * nodes + 1, 0:rows, :] = scale
            tile = pad[comps * nodes + 1]
            place(low, tile, 0, 1, 3, k)
            place(low, tile, 1, 1, 4, k)
            place(high, tile, width - 2, 0, 3, k)
            place(high, tile, width - 1, 0, 4, k)
            put(comps * nodes + k, None, scale[0:1], scale[rows - 2 : rows - 1])
            put(comps * nodes + layers + k, None, scale[1:2], scale[rows - 1 : rows])
    used = 2 * comps * nodes + 2 * layers + nodes
    row1[used:, :] = jnp.zeros((FULL - used, LANES), jnp.float32)
    row2[used:, :] = jnp.zeros((FULL - used, LANES), jnp.float32)
    for plane in range(2):
        if paired_y:
            col1[plane] = jnp.where(even_y, high[plane], low[plane])
            col2[plane] = jnp.where(even_y, low[plane], high[plane])
        else:
            col1[plane] = low[plane]
            col2[plane] = high[plane]


def strip_kernel(paired_x, paired_y, own1, own2, got1, got2, row1, row2, strip, out1, out2):
    lane = lanes()
    even_x = is_even("gx") if paired_x else True
    even_y = is_even("gy") if paired_y else True
    if paired_y:
        own_low = [jnp.where(even_y, own2[p], own1[p]) for p in range(2)]
        own_high = [jnp.where(even_y, own1[p], own2[p]) for p in range(2)]
        from_low = [jnp.where(even_y, got2[p], got1[p]) for p in range(2)]
        from_high = [jnp.where(even_y, got1[p], got2[p]) for p in range(2)]
    else:
        own_low, own_high = [own1[p] for p in range(2)], [own2[p] for p in range(2)]
        from_low, from_high = [got2[p] for p in range(2)], [got1[p] for p in range(2)]

    def build(*items):
        out = jnp.zeros((8, LANES), jnp.float32)
        for planes, plane, source, slot in items:
            inside = (lane >= slot * SLOT) & (lane < slot * SLOT + SLOT)
            out = jnp.where(inside, lane_roll(planes[plane], (slot - source) * SLOT), out)
        return out

    planes = [
        build(
            (from_low, 0, c, 0),
            (own_low, 0, c, 1),
            (own_high, 0, c, 2),
            (from_high, 0, c, 3),
            (from_high, 1, c, 4),
        )
        for c in range(3)
    ]
    planes.append(
        build((from_low, 0, 3, 0), (from_low, 0, 4, 1), (own_high, 0, 3, 2), (own_high, 0, 4, 3), (from_high, 1, 3, 4))
    )
    planes.append(
        build((from_low, 0, 4, 0), (own_low, 1, 3, 1), (own_high, 0, 4, 2), (from_high, 1, 3, 3), (from_high, 1, 4, 4))
    )
    planes.append(build((from_high, 0, 3, 3)))
    rows = 6
    out1[...] = row1[...]
    out2[...] = row2[...]
    for p, plane in enumerate(planes):
        strip[p] = plane
        for which in range(2):
            at = CORNERS + 2 * p + which
            low_row = plane[which : which + 1]
            high_row = plane[rows - 2 + which : rows - 1 + which]
            if paired_x:
                out1[at : at + 1, :] = jnp.where(even_x, high_row, low_row)
                out2[at : at + 1, :] = jnp.where(even_x, low_row, high_row)
            else:
                out1[at : at + 1, :] = low_row
                out2[at : at + 1, :] = high_row


PLANE = ("", "1", "2", "12")


def split_layers(lo, hi):
    sums = [{m: lo[c][m] + hi[c][m] for m in ("1", "2", "12")} for c in range(3)]
    diffs = [{m: hi[c][m] - lo[c][m] for m in PLANE} for c in range(3)]
    u, v, w = range(3)
    return (
        diffs[u][""], sums[v]["1"], sums[w]["2"],
        sums[u]["1"] + diffs[v][""], sums[u]["2"] + diffs[w][""], sums[v]["2"] + sums[w]["1"],
        diffs[u]["1"], sums[w]["12"], diffs[u]["2"], sums[v]["12"], diffs[v]["1"], diffs[w]["2"],
        sums[u]["12"], diffs[v]["2"], diffs[w]["1"],
        diffs[u]["12"], diffs[v]["12"], diffs[w]["12"],
    )


def stress(m):
    one, two, three = 1.0 / 16.0, 1.0 / 48.0, 1.0 / 144.0
    trace = (LAME * one) * (m[0] + m[1] + m[2])
    out = [trace + (2.0 * SHEAR * one) * m[i] for i in range(3)]
    out += [(SHEAR * one) * m[i] for i in (3, 4, 5)]
    own, other = (LAME + 3.0 * SHEAR) * two, LAME * two
    for i in (6, 8, 10):
        out += [own * m[i] + other * m[i + 1], own * m[i + 1] + other * m[i]]
    total = m[12] + m[13] + m[14]
    out += [(SHEAR * two) * (m[i] + total) for i in (12, 13, 14)]
    out += [((LAME + 4.0 * SHEAR) * three) * m[i] for i in (15, 16, 17)]
    return out


def inner(g, m):
    parts = [g[i] * m[i] for i in range(18)]
    while len(parts) > 1:
        parts = [parts[i] + parts[i + 1] if i + 1 < len(parts) else parts[i] for i in range(0, len(parts), 2)]
    return parts[0]


def join_layers(g):
    sums = [
        {"1": g[3], "2": g[4], "12": g[12]},
        {"1": g[1], "2": g[5], "12": g[9]},
        {"1": g[5], "2": g[2], "12": g[7]},
    ]
    diffs = [
        {"": g[0], "1": g[6], "2": g[8], "12": g[15]},
        {"": g[3], "1": g[10], "2": g[13], "12": g[16]},
        {"": g[4], "1": g[14], "2": g[11], "12": g[17]},
    ]
    lower = [{m: (sums[c][m] - diffs[c][m] if m else -diffs[c][m]) for m in PLANE} for c in range(3)]
    upper = [{m: (sums[c][m] + diffs[c][m] if m else diffs[c][m]) for m in PLANE} for c in range(3)]
    return lower, upper


def in_plane(x, right, up):
    y = right(x)
    near, far = x + y, y - x
    near_up, far_up = up(near), up(far)
    return {"": near + near_up, "1": near_up - near, "2": far + far_up, "12": far_up - far}


def out_of_plane(f, right, up):
    plain = (f[""] - f["2"]) + right(f[""] + f["2"])
    steep = (f["1"] - f["12"]) + right(f["1"] + f["12"])
    return (plain - steep) + up(plain + steep)


def operator_kernel(
    paired_x, force, phase, fixed, strip, got1, got2,
    base, second, energy, sums,
    lo, hi, held, modes, residual, inverse,
):
    comps, nodes, rows, width = force.shape
    layers = nodes - 1
    lane, row = lanes(), sublanes()
    last_row, below = row == 6, row == 7
    cn = comps * nodes
    if paired_x:
        even_x = is_even("gx")
        lo[...] = jnp.where(even_x, got2[...], got1[...])
        hi[...] = jnp.where(even_x, got1[...], got2[...])
    else:
        lo[...] = got2[...]
        hi[...] = got1[...]

    def spread(ref, at):
        return jnp.broadcast_to(ref[pl.ds(at, 1), :], (8, LANES))

    def roll_up(x):
        return pltpu.roll(x, 7, 0)

    def roll_down(x):
        return pltpu.roll(x, 1, 0)

    def corner(ref, p, which):
        return spread(ref, CORNERS + 2 * p + which)

    tiles = [
        jnp.where(row < 6, strip[p], jnp.where(last_row, corner(hi, p, 0), corner(lo, p, 1))) for p in range(6)
    ]
    sevens = [corner(hi, p, 1) for p in range(5)]
    left, right = tiles[3], tiles[4]
    around = left + right
    around_7 = sevens[3] + sevens[4]
    around_m2 = corner(lo, 3, 0) + corner(lo, 4, 0)

    def node_rows(x, x_m2):
        return x + jnp.where(below, x_m2, roll_down(x))

    def node_row_7(x, x_7):
        return jnp.broadcast_to(x[6:7], (8, LANES)) + x_7

    def strip_diagonal(x):
        return KE_DIAGONAL * (x + lane_roll(x, 1))

    strip_diag = strip_diagonal(node_rows(around, around_m2))
    strip_diag_7 = strip_diagonal(node_row_7(around, around_7))
    strip_inv = jnp.where(strip_diag > 0.0, 1.0 / strip_diag, 0.0)
    strip_inv_7 = jnp.where(strip_diag_7 > 0.0, 1.0 / strip_diag_7, 0.0)
    strip_base = [tiles[c] * strip_inv for c in range(3)]
    strip_base_7 = [sevens[c] * strip_inv_7 for c in range(3)]
    edge_rows = node_rows(right, corner(lo, 4, 0))
    edge_rows_7 = node_row_7(right, sevens[4])

    slot = lane // SLOT
    live = (slot == 0) | (slot == 2) | (slot == 3)
    strip_scale = jnp.where(live, right, 0.0)

    def strip_modes(c):
        x, x_7 = strip_base[c], strip_base_7[c]
        near, near_7 = x + lane_roll(x, -SLOT), x_7 + lane_roll(x_7, -SLOT)
        far, far_7 = lane_roll(x, -SLOT) - x, lane_roll(x_7, -SLOT) - x_7
        near_up = jnp.where(last_row, near_7, roll_up(near))
        far_up = jnp.where(last_row, far_7, roll_up(far))
        return {"": near + near_up, "1": near_up - near, "2": far + far_up, "12": far_up - far}

    lower = [strip_modes(c) for c in range(3)]
    upper = [{m: lane_roll(lower[c][m], -1) for m in PLANE} for c in range(3)]
    g = [strip_scale * x for x in stress(split_layers(lower, upper))]
    f_low, f_up = join_layers(g)
    f_strip = []
    for c in range(3):
        f = {m: f_low[c][m] + lane_roll(f_up[c][m], 1) for m in PLANE}
        f_strip.append(out_of_plane(f, lambda x: lane_roll(x, SLOT), roll_down))
    strip_second = [jnp.where(tiles[5] > 0.0, (f_strip[c] - tiles[c]) * strip_inv, 0.0) for c in range(3)]

    def scale_of(k):
        held[0, 0:rows, :] = table(phase[k], PHASE_STIFFNESS)
        held[0, 6:7, :] = hi[pl.ds(cn + k, 1), :]
        held[0, 7:8, :] = lo[pl.ds(cn + layers + k, 1), :]
        return held[0], spread(hi, cn + layers + k), spread(lo, cn + k)

    def box(k):
        x, x_7, x_m2 = scale_of(k)
        r, r_7 = node_rows(x, x_m2), node_row_7(x, x_7)
        r = r + jnp.where(lane == 0, lane_roll(edge_rows, -k), lane_roll(r, 1))
        r_7 = r_7 + jnp.where(lane == 0, lane_roll(edge_rows_7, -k), lane_roll(r_7, 1))
        return x, r, r_7

    def first_layer(k, around_node, around_node_7):
        inv = 1.0 / (KE_DIAGONAL * around_node)
        inv_7 = 1.0 / (KE_DIAGONAL * around_node_7)
        inverse[k] = inv
        out = []
        free = (1 - fixed[k]).astype(jnp.float32)
        for c in range(3):
            q = c * nodes + k
            residual[q, 0:rows, :] = free * force[c, k]
            residual[q, 6:7, :] = hi[pl.ds(q, 1), :]
            residual[q, 7:8, :] = lo[pl.ds(q, 1), :]
            x = residual[q] * inv
            x_7 = spread(hi, cn + 2 * layers + q) * inv_7
            base[c, k] = x[0:rows]
            shift = LANES - 1 - (3 * SLOT + k)
            at_end = lane == LANES - 1
            y = jnp.where(at_end, lane_roll(strip_base[c], shift), lane_roll(x, -1))
            y_7 = jnp.where(at_end, lane_roll(strip_base_7[c], shift), lane_roll(x_7, -1))
            near, far, near_7, far_7 = x + y, y - x, x_7 + y_7, y_7 - x_7
            near_up = jnp.where(last_row, near_7, roll_up(near))
            far_up = jnp.where(last_row, far_7, roll_up(far))
            out.append({"": near + near_up, "1": near_up - near, "2": far + far_up, "12": far_up - far})
        return out

    def finish_layer(k, f, totals):
        inv = inverse[k]
        held[1, 0:rows, :] = 1.0 - fixed[k].astype(jnp.float32)
        held[1, 6:7, :] = hi[pl.ds(2 * cn + 2 * layers + k, 1), :]
        free = held[1] > 0.0
        a, b, d = totals
        for c in range(3):
            q = c * nodes + k
            r0 = residual[q]
            image = out_of_plane(f[c], lambda x: jnp.where(lane == 0, 0.0, lane_roll(x, 1)), roll_down)
            image = image + jnp.where(lane == 0, lane_roll(f_strip[c], -(SLOT + k)), 0.0)
            d0 = jnp.where(free, r0 * inv, r0)
            s = jnp.where(free, image, d0) - r0
            v = jnp.where(free, s * inv, s)
            second[c, k] = v[0:rows]
            residual[q] = v
            a, b, d = a + r0 * d0, b + d0 * s, d + s * v
        return a, b, d

    def store_energy(which, k, value):
        energy[which, k] = -table(phase[k], PHASE_SLOPE) * value[0:rows]

    def flat(x):
        return tuple(x[c][m] for c in range(3) for m in PLANE)

    def unflat(x):
        return [{m: x[4 * c + i] for i, m in enumerate(PLANE)} for c in range(3)]

    zero = jnp.zeros((8, LANES), jnp.float32)
    held[1] = zero
    scale_0, box_0, box_0_7 = box(0)
    start = first_layer(0, box_0, box_0_7)

    def element(k, low_modes, high_modes, scale, pending, totals):
        m = split_layers(low_modes, high_modes)
        g = stress(m)
        store_energy(0, k, inner(g, m))
        for i in range(18):
            modes[k, i] = m[i]
        f_lower, f_upper = join_layers([scale * x for x in g])
        done = [{m: pending[c][m] + f_lower[c][m] for m in PLANE} for c in range(3)]
        return f_upper, finish_layer(k, done, totals)

    def forward(k, carry):
        low_modes, pending, totals, scale, b, b_7 = carry
        next_scale, next_b, next_b_7 = box(k + 1)
        high = first_layer(k + 1, b + next_b, b_7 + next_b_7)
        f_upper, totals = element(k, unflat(low_modes), high, scale, unflat(pending), totals)
        return flat(high), flat(f_upper), totals, next_scale, next_b, next_b_7

    carry = (flat(start), (zero,) * 12, (zero,) * 3, scale_0, box_0, box_0_7)
    low_modes, pending, totals, scale, b, b_7 = lax.fori_loop(0, layers - 1, forward, carry)
    high = first_layer(layers, b, b_7)
    f_upper, totals = element(layers - 1, unflat(low_modes), high, scale, unflat(pending), totals)
    totals = finish_layer(layers, f_upper, totals)

    def second_layer(k):
        out = []
        for c in range(3):
            fill = lane_roll(strip_second[c], LANES - 1 - (3 * SLOT + k))
            x = residual[c * nodes + k]
            out.append(in_plane(x, lambda t: jnp.where(lane == LANES - 1, fill, lane_roll(t, -1)), roll_up))
        return out

    def again(k, carry):
        low_modes, total = carry
        high = second_layer(k + 1)
        m = split_layers(unflat(low_modes), high)
        g = stress(m)
        own = inner(g, m)
        store_energy(2, k, own)
        store_energy(1, k, inner(g, [modes[k, i] for i in range(18)]))
        scale = table(phase[k], PHASE_STIFFNESS)
        held[2, 0:rows, :] = scale * own[0:rows]
        return flat(high), total + held[2]

    held[2] = zero
    _, total = lax.fori_loop(0, layers, again, (flat(second_layer(0)), zero))
    for i, x in enumerate(totals + (total,)):
        x = jnp.where(row < rows, x, 0.0)
        x = jnp.sum(jnp.sum(x, axis=0, keepdims=True), axis=1, keepdims=True)
        sums[i : i + 1, :] = jnp.broadcast_to(x, (1, LANES))
    sums[4:, :] = jnp.zeros((4, LANES), jnp.float32)


def combine_kernel(base, second, energy, sums, displacement, sensitivity):
    a, b, d, e = (sums[i : i + 1, :] for i in range(4))
    ratio = b / a
    curve = a + b
    alpha = a / curve
    rest = d - b * ratio
    bend = e - 2.0 * ratio * (b + d) + ratio * ratio * curve
    alpha_next = rest / (bend - rest * rest / curve)
    beta = alpha * alpha * rest / a
    first = alpha + alpha_next * beta + alpha * alpha_next * ratio
    other = -alpha * alpha_next
    displacement[...] = first * base[...] + other * second[...]
    sensitivity[...] = (first * first) * energy[0] + (2.0 * first * other) * energy[1] + (other * other) * energy[2]


def exchange(one, two, axis):
    count = lax.axis_size(axis)
    if count % 2 == 0:
        far = lax.ppermute(two, axis, [(i, (i - 1) % count if i % 2 == 0 else (i + 1) % count) for i in range(count)])
        near = lax.ppermute(one, axis, [(i, i ^ 1) for i in range(count)])
        return near, far
    high = lax.ppermute(one, axis, [((i + 1) % count, i) for i in range(count)])
    low = lax.ppermute(two, axis, [(i, (i + 1) % count) for i in range(count)])
    return high, low


def total_over(x, axis):
    count = lax.axis_size(axis)
    if count & (count - 1):
        return lax.psum(x, axis)
    step = 1
    while step < count:
        x = x + lax.ppermute(x, axis, [(i, i ^ step) for i in range(count)])
        step *= 2
    return x


def body(force, phase, fixed):
    comps, nodes, rows, width = force.shape
    layers = nodes - 1
    f32 = jnp.float32
    paired_x = lax.axis_size("gx") % 2 == 0
    paired_y = lax.axis_size("gy") % 2 == 0
    column = jax.ShapeDtypeStruct((2, 8, LANES), f32)
    message = jax.ShapeDtypeStruct((FULL, LANES), f32)

    def call(kernel, out_shape, scratch=()):
        return pl.pallas_call(
            kernel,
            out_shape=out_shape,
            scratch_shapes=scratch,
            compiler_params=PARAMS,
        )

    col1, col2, row1, row2 = call(
        functools.partial(pack_kernel, paired_x, paired_y),
        (column, column, message, message),
        [pltpu.VMEM((comps * nodes + 2, 8, LANES), f32)],
    )(force, phase, fixed)
    near, far = exchange(col1, col2, "gy")
    strip, row1, row2 = call(
        functools.partial(strip_kernel, paired_x, paired_y),
        (jax.ShapeDtypeStruct((6, 8, LANES), f32), message, message),
    )(col1, col2, near, far, row1, row2)
    near, far = exchange(row1, row2, "gx")
    base, second, energy, sums = call(
        functools.partial(operator_kernel, paired_x),
        (
            jax.ShapeDtypeStruct(force.shape, f32),
            jax.ShapeDtypeStruct(force.shape, f32),
            jax.ShapeDtypeStruct((3,) + phase.shape, f32),
            jax.ShapeDtypeStruct((8, LANES), f32),
        ),
        [
            pltpu.VMEM((FULL, LANES), f32),
            pltpu.VMEM((FULL, LANES), f32),
            pltpu.VMEM((3, 8, LANES), f32),
            pltpu.VMEM((layers, 18, 8, LANES), f32),
            pltpu.VMEM((comps * nodes, 8, LANES), f32),
            pltpu.VMEM((nodes, 8, LANES), f32),
        ],
    )(force, phase, fixed, strip, near, far)
    sums = total_over(total_over(sums, "gy"), "gx")
    return call(
        combine_kernel,
        (jax.ShapeDtypeStruct(force.shape, f32), jax.ShapeDtypeStruct(phase.shape, f32)),
    )(base, second, energy, sums)


def solution(mesh):
    return jax.shard_map(
        body,
        mesh=mesh,
        in_specs=(
            P(None, None, ("parts", "gx"), "gy"),
            P(None, ("parts", "gx"), "gy"),
            P(None, ("parts", "gx"), "gy"),
        ),
        out_specs=(P(None, None, ("parts", "gx"), "gy"), P(None, ("parts", "gx"), "gy")),
        check_vma=False,
    )
```

```python
import functools

import jax
import jax.numpy as jnp
import numpy as np
from jax import lax
from jax.experimental import pallas as pl
from jax.experimental.pallas import tpu as pltpu
from jax.sharding import PartitionSpec as P

PHASE_STIFFNESS = (0.125, 0.343, 0.614, 1.0)
PHASE_SLOPE = (0.75, 1.47, 2.17, 3.0)
POISSON = 0.3
LAME = POISSON / ((1.0 + POISSON) * (1.0 - 2.0 * POISSON))
SHEAR = 1.0 / (2.0 * (1.0 + POISSON))
KE_DIAGONAL = (LAME + 4.0 * SHEAR) / 9.0

SLOT = 24
LANES = 128
FULL = 168
CORNERS = 152

VMEM = pl.BlockSpec(memory_space=pltpu.VMEM)
PARAMS = pltpu.CompilerParams(vmem_limit_bytes=32 * 1024 * 1024)


def lanes():
    return lax.broadcasted_iota(jnp.int32, (8, LANES), 1)


def sublanes():
    return lax.broadcasted_iota(jnp.int32, (8, LANES), 0)


def table(phase, values):
    out = jnp.full(phase.shape, values[3], jnp.float32)
    for index in (2, 1, 0):
        out = jnp.where(phase == index, jnp.float32(values[index]), out)
    return out


def element_rows(ref, k, layers):
    return ref[pl.ds(k, ref.shape[0] // layers, stride=layers), :]


def lane_roll(x, by):
    if isinstance(by, int):
        by = by % LANES
        return x if by == 0 else pltpu.roll(x, by, 1)
    return pltpu.roll(x, lax.rem(by + LANES, LANES), 1)


def is_even(axis):
    return lax.rem(lax.axis_index(axis), 2) == 0


def pack_kernel(paired_x, paired_y, force, phase, fixed, col1, col2, row1, row2, pad):
    comps, nodes, rows, width = force.shape
    layers = nodes - 1
    lane = lanes()
    even_x = is_even("gx") if paired_x else True
    even_y = is_even("gy") if paired_y else True
    zero = jnp.zeros((8, LANES), jnp.float32)
    low = [zero, zero]
    high = [zero, zero]
    pad[...] = jnp.zeros(pad.shape, jnp.float32)

    def place(planes, tile, column, plane, slot, k):
        target = slot * SLOT + k
        planes[plane] = jnp.where(lane == target, lane_roll(tile, target - column), planes[plane])

    def put(at_low, at_high, value_low, value_high):
        if paired_x:
            if value_high is None:
                value_high = jnp.zeros((1, LANES), jnp.float32)
            row1[at_low : at_low + 1, :] = jnp.where(even_x, value_high, value_low)
            row2[at_low : at_low + 1, :] = jnp.where(even_x, value_low, value_high)
        else:
            row1[at_low : at_low + 1, :] = value_low
            row2[at_low : at_low + 1, :] = jnp.zeros((1, LANES), jnp.float32) if value_high is None else value_high

    for k in range(nodes):
        free = (1 - fixed[k]).astype(jnp.float32)
        for c in range(comps):
            q = c * nodes + k
            r0 = free * force[c, k]
            pad[q, 0:rows, :] = r0
            tile = pad[q]
            place(low, tile, 0, 0, c, k)
            place(low, tile, 1, 1, c, k)
            place(high, tile, width - 1, 0, c, k)
            put(q, q, r0[0:1], r0[rows - 1 : rows])
            put(comps * nodes + 2 * layers + q, None, r0[1:2], None)
        pad[comps * nodes, 0:rows, :] = free
        place(low, pad[comps * nodes], 0, 0, 3, k)
        put(2 * comps * nodes + 2 * layers + k, None, free[0:1], None)
        if k < layers:
            scale = table(element_rows(phase, k, layers), PHASE_STIFFNESS)
            pad[comps * nodes + 1, 0:rows, :] = scale
            tile = pad[comps * nodes + 1]
            place(low, tile, 0, 1, 3, k)
            place(low, tile, 1, 1, 4, k)
            place(high, tile, width - 2, 0, 3, k)
            place(high, tile, width - 1, 0, 4, k)
            put(comps * nodes + k, None, scale[0:1], scale[rows - 2 : rows - 1])
            put(comps * nodes + layers + k, None, scale[1:2], scale[rows - 1 : rows])
    used = 2 * comps * nodes + 2 * layers + nodes
    row1[used:, :] = jnp.zeros((FULL - used, LANES), jnp.float32)
    row2[used:, :] = jnp.zeros((FULL - used, LANES), jnp.float32)
    for plane in range(2):
        if paired_y:
            col1[plane] = jnp.where(even_y, high[plane], low[plane])
            col2[plane] = jnp.where(even_y, low[plane], high[plane])
        else:
            col1[plane] = low[plane]
            col2[plane] = high[plane]


def strip_kernel(paired_x, paired_y, own1, own2, got1, got2, row1, row2, strip, out1, out2):
    lane = lanes()
    even_x = is_even("gx") if paired_x else True
    even_y = is_even("gy") if paired_y else True
    if paired_y:
        own_low = [jnp.where(even_y, own2[p], own1[p]) for p in range(2)]
        own_high = [jnp.where(even_y, own1[p], own2[p]) for p in range(2)]
        from_low = [jnp.where(even_y, got2[p], got1[p]) for p in range(2)]
        from_high = [jnp.where(even_y, got1[p], got2[p]) for p in range(2)]
    else:
        own_low, own_high = [own1[p] for p in range(2)], [own2[p] for p in range(2)]
        from_low, from_high = [got2[p] for p in range(2)], [got1[p] for p in range(2)]

    def build(*items):
        out = jnp.zeros((8, LANES), jnp.float32)
        for planes, plane, source, slot in items:
            inside = (lane >= slot * SLOT) & (lane < slot * SLOT + SLOT)
            out = jnp.where(inside, lane_roll(planes[plane], (slot - source) * SLOT), out)
        return out

    planes = [
        build(
            (from_low, 0, c, 0),
            (own_low, 0, c, 1),
            (own_high, 0, c, 2),
            (from_high, 0, c, 3),
            (from_high, 1, c, 4),
        )
        for c in range(3)
    ]
    planes.append(
        build((from_low, 0, 3, 0), (from_low, 0, 4, 1), (own_high, 0, 3, 2), (own_high, 0, 4, 3), (from_high, 1, 3, 4))
    )
    planes.append(
        build((from_low, 0, 4, 0), (own_low, 1, 3, 1), (own_high, 0, 4, 2), (from_high, 1, 3, 3), (from_high, 1, 4, 4))
    )
    planes.append(build((from_high, 0, 3, 3)))
    rows = 6
    out1[...] = row1[...]
    out2[...] = row2[...]
    for p, plane in enumerate(planes):
        strip[p] = plane
        for which in range(2):
            at = CORNERS + 2 * p + which
            low_row = plane[which : which + 1]
            high_row = plane[rows - 2 + which : rows - 1 + which]
            if paired_x:
                out1[at : at + 1, :] = jnp.where(even_x, high_row, low_row)
                out2[at : at + 1, :] = jnp.where(even_x, low_row, high_row)
            else:
                out1[at : at + 1, :] = low_row
                out2[at : at + 1, :] = high_row


PLANE = ("", "1", "2", "12")


def split_layers(lo, hi):
    sums = [{m: lo[c][m] + hi[c][m] for m in ("1", "2", "12")} for c in range(3)]
    diffs = [{m: hi[c][m] - lo[c][m] for m in PLANE} for c in range(3)]
    u, v, w = range(3)
    return (
        diffs[u][""], sums[v]["1"], sums[w]["2"],
        sums[u]["1"] + diffs[v][""], sums[u]["2"] + diffs[w][""], sums[v]["2"] + sums[w]["1"],
        diffs[u]["1"], sums[w]["12"], diffs[u]["2"], sums[v]["12"], diffs[v]["1"], diffs[w]["2"],
        sums[u]["12"], diffs[v]["2"], diffs[w]["1"],
        diffs[u]["12"], diffs[v]["12"], diffs[w]["12"],
    )


def stress(m):
    one, two, three = 1.0 / 16.0, 1.0 / 48.0, 1.0 / 144.0
    trace = (LAME * one) * (m[0] + m[1] + m[2])
    out = [trace + (2.0 * SHEAR * one) * m[i] for i in range(3)]
    out += [(SHEAR * one) * m[i] for i in (3, 4, 5)]
    own, other = (LAME + 3.0 * SHEAR) * two, LAME * two
    for i in (6, 8, 10):
        out += [own * m[i] + other * m[i + 1], own * m[i + 1] + other * m[i]]
    total = m[12] + m[13] + m[14]
    out += [(SHEAR * two) * (m[i] + total) for i in (12, 13, 14)]
    out += [((LAME + 4.0 * SHEAR) * three) * m[i] for i in (15, 16, 17)]
    return out


def inner(g, m):
    parts = [g[i] * m[i] for i in range(18)]
    while len(parts) > 1:
        parts = [parts[i] + parts[i + 1] if i + 1 < len(parts) else parts[i] for i in range(0, len(parts), 2)]
    return parts[0]


def join_layers(g):
    sums = [
        {"1": g[3], "2": g[4], "12": g[12]},
        {"1": g[1], "2": g[5], "12": g[9]},
        {"1": g[5], "2": g[2], "12": g[7]},
    ]
    diffs = [
        {"": g[0], "1": g[6], "2": g[8], "12": g[15]},
        {"": g[3], "1": g[10], "2": g[13], "12": g[16]},
        {"": g[4], "1": g[14], "2": g[11], "12": g[17]},
    ]
    lower = [{m: (sums[c][m] - diffs[c][m] if m else -diffs[c][m]) for m in PLANE} for c in range(3)]
    upper = [{m: (sums[c][m] + diffs[c][m] if m else diffs[c][m]) for m in PLANE} for c in range(3)]
    return lower, upper


def in_plane(x, right, up):
    y = right(x)
    near, far = x + y, y - x
    near_up, far_up = up(near), up(far)
    return {"": near + near_up, "1": near_up - near, "2": far + far_up, "12": far_up - far}


def out_of_plane(f, right, up):
    plain = (f[""] - f["2"]) + right(f[""] + f["2"])
    steep = (f["1"] - f["12"]) + right(f["1"] + f["12"])
    return (plain - steep) + up(plain + steep)


def operator_kernel(
    paired_x, force, phase, fixed, strip, got1, got2,
    base, second, energy, sums,
    lo, hi, held, modes, residual, inverse,
):
    comps, nodes, rows, width = force.shape
    layers = nodes - 1
    lane, row = lanes(), sublanes()
    last_row, below = row == 6, row == 7
    cn = comps * nodes
    if paired_x:
        even_x = is_even("gx")
        lo[...] = jnp.where(even_x, got2[...], got1[...])
        hi[...] = jnp.where(even_x, got1[...], got2[...])
    else:
        lo[...] = got2[...]
        hi[...] = got1[...]

    def spread(ref, at):
        return jnp.broadcast_to(ref[pl.ds(at, 1), :], (8, LANES))

    def roll_up(x):
        return pltpu.roll(x, 7, 0)

    def roll_down(x):
        return pltpu.roll(x, 1, 0)

    def corner(ref, p, which):
        return spread(ref, CORNERS + 2 * p + which)

    tiles = [
        jnp.where(row < 6, strip[p], jnp.where(last_row, corner(hi, p, 0), corner(lo, p, 1))) for p in range(6)
    ]
    sevens = [corner(hi, p, 1) for p in range(5)]
    left, right = tiles[3], tiles[4]
    around = left + right
    around_7 = sevens[3] + sevens[4]
    around_m2 = corner(lo, 3, 0) + corner(lo, 4, 0)

    def node_rows(x, x_m2):
        return x + jnp.where(below, x_m2, roll_down(x))

    def node_row_7(x, x_7):
        return jnp.broadcast_to(x[6:7], (8, LANES)) + x_7

    def strip_diagonal(x):
        return KE_DIAGONAL * (x + lane_roll(x, 1))

    strip_diag = strip_diagonal(node_rows(around, around_m2))
    strip_diag_7 = strip_diagonal(node_row_7(around, around_7))
    strip_inv = jnp.where(strip_diag > 0.0, 1.0 / strip_diag, 0.0)
    strip_inv_7 = jnp.where(strip_diag_7 > 0.0, 1.0 / strip_diag_7, 0.0)
    strip_base = [tiles[c] * strip_inv for c in range(3)]
    strip_base_7 = [sevens[c] * strip_inv_7 for c in range(3)]
    edge_rows = node_rows(right, corner(lo, 4, 0))
    edge_rows_7 = node_row_7(right, sevens[4])

    slot = lane // SLOT
    live = (slot == 0) | (slot == 2) | (slot == 3)
    strip_scale = jnp.where(live, right, 0.0)

    def strip_modes(c):
        x, x_7 = strip_base[c], strip_base_7[c]
        near, near_7 = x + lane_roll(x, -SLOT), x_7 + lane_roll(x_7, -SLOT)
        far, far_7 = lane_roll(x, -SLOT) - x, lane_roll(x_7, -SLOT) - x_7
        near_up = jnp.where(last_row, near_7, roll_up(near))
        far_up = jnp.where(last_row, far_7, roll_up(far))
        return {"": near + near_up, "1": near_up - near, "2": far + far_up, "12": far_up - far}

    lower = [strip_modes(c) for c in range(3)]
    upper = [{m: lane_roll(lower[c][m], -1) for m in PLANE} for c in range(3)]
    g = [strip_scale * x for x in stress(split_layers(lower, upper))]
    f_low, f_up = join_layers(g)
    f_strip = []
    for c in range(3):
        f = {m: f_low[c][m] + lane_roll(f_up[c][m], 1) for m in PLANE}
        f_strip.append(out_of_plane(f, lambda x: lane_roll(x, SLOT), roll_down))
    strip_second = [jnp.where(tiles[5] > 0.0, (f_strip[c] - tiles[c]) * strip_inv, 0.0) for c in range(3)]

    def scale_of(k):
        held[0, 0:rows, :] = table(element_rows(phase, k, layers), PHASE_STIFFNESS)
        held[0, 6:7, :] = hi[pl.ds(cn + k, 1), :]
        held[0, 7:8, :] = lo[pl.ds(cn + layers + k, 1), :]
        return held[0], spread(hi, cn + layers + k), spread(lo, cn + k)

    def box(k):
        x, x_7, x_m2 = scale_of(k)
        r, r_7 = node_rows(x, x_m2), node_row_7(x, x_7)
        r = r + jnp.where(lane == 0, lane_roll(edge_rows, -k), lane_roll(r, 1))
        r_7 = r_7 + jnp.where(lane == 0, lane_roll(edge_rows_7, -k), lane_roll(r_7, 1))
        return x, r, r_7

    def first_layer(k, around_node, around_node_7):
        inv = 1.0 / (KE_DIAGONAL * around_node)
        inv_7 = 1.0 / (KE_DIAGONAL * around_node_7)
        inverse[k] = inv
        out = []
        free = (1 - fixed[k]).astype(jnp.float32)
        for c in range(3):
            q = c * nodes + k
            residual[q, 0:rows, :] = free * force[c, k]
            residual[q, 6:7, :] = hi[pl.ds(q, 1), :]
            residual[q, 7:8, :] = lo[pl.ds(q, 1), :]
            x = residual[q] * inv
            x_7 = spread(hi, cn + 2 * layers + q) * inv_7
            base[c, k] = x[0:rows]
            shift = LANES - 1 - (3 * SLOT + k)
            at_end = lane == LANES - 1
            y = jnp.where(at_end, lane_roll(strip_base[c], shift), lane_roll(x, -1))
            y_7 = jnp.where(at_end, lane_roll(strip_base_7[c], shift), lane_roll(x_7, -1))
            near, far, near_7, far_7 = x + y, y - x, x_7 + y_7, y_7 - x_7
            near_up = jnp.where(last_row, near_7, roll_up(near))
            far_up = jnp.where(last_row, far_7, roll_up(far))
            out.append({"": near + near_up, "1": near_up - near, "2": far + far_up, "12": far_up - far})
        return out

    def finish_layer(k, f, totals):
        inv = inverse[k]
        held[1, 0:rows, :] = 1.0 - fixed[k].astype(jnp.float32)
        held[1, 6:7, :] = hi[pl.ds(2 * cn + 2 * layers + k, 1), :]
        free = held[1] > 0.0
        a, b, d = totals
        for c in range(3):
            q = c * nodes + k
            r0 = residual[q]
            image = out_of_plane(f[c], lambda x: jnp.where(lane == 0, 0.0, lane_roll(x, 1)), roll_down)
            image = image + jnp.where(lane == 0, lane_roll(f_strip[c], -(SLOT + k)), 0.0)
            d0 = jnp.where(free, r0 * inv, r0)
            s = jnp.where(free, image, d0) - r0
            v = jnp.where(free, s * inv, s)
            second[c, k] = v[0:rows]
            residual[q] = v
            a, b, d = a + r0 * d0, b + d0 * s, d + s * v
        return a, b, d

    def store_energy(which, k, value):
        slope = table(element_rows(phase, k, layers), PHASE_SLOPE)
        energy[which, pl.ds(k, rows, stride=layers), :] = -slope * value[0:rows]

    def flat(x):
        return tuple(x[c][m] for c in range(3) for m in PLANE)

    def unflat(x):
        return [{m: x[4 * c + i] for i, m in enumerate(PLANE)} for c in range(3)]

    zero = jnp.zeros((8, LANES), jnp.float32)
    held[1] = zero
    scale_0, box_0, box_0_7 = box(0)
    start = first_layer(0, box_0, box_0_7)

    def element(k, low_modes, high_modes, scale, pending, totals):
        m = split_layers(low_modes, high_modes)
        g = stress(m)
        store_energy(0, k, inner(g, m))
        for i in range(18):
            modes[k, i] = m[i]
        f_lower, f_upper = join_layers([scale * x for x in g])
        done = [{m: pending[c][m] + f_lower[c][m] for m in PLANE} for c in range(3)]
        return f_upper, finish_layer(k, done, totals)

    def forward(k, carry):
        low_modes, pending, totals, scale, b, b_7 = carry
        next_scale, next_b, next_b_7 = box(k + 1)
        high = first_layer(k + 1, b + next_b, b_7 + next_b_7)
        f_upper, totals = element(k, unflat(low_modes), high, scale, unflat(pending), totals)
        return flat(high), flat(f_upper), totals, next_scale, next_b, next_b_7

    carry = (flat(start), (zero,) * 12, (zero,) * 3, scale_0, box_0, box_0_7)
    low_modes, pending, totals, scale, b, b_7 = lax.fori_loop(0, layers - 1, forward, carry, unroll=True)
    high = first_layer(layers, b, b_7)
    f_upper, totals = element(layers - 1, unflat(low_modes), high, scale, unflat(pending), totals)
    totals = finish_layer(layers, f_upper, totals)

    def second_layer(k):
        out = []
        for c in range(3):
            fill = lane_roll(strip_second[c], LANES - 1 - (3 * SLOT + k))
            x = residual[c * nodes + k]
            out.append(in_plane(x, lambda t: jnp.where(lane == LANES - 1, fill, lane_roll(t, -1)), roll_up))
        return out

    def again(k, carry):
        low_modes, total = carry
        high = second_layer(k + 1)
        m = split_layers(unflat(low_modes), high)
        g = stress(m)
        own = inner(g, m)
        store_energy(2, k, own)
        store_energy(1, k, inner(g, [modes[k, i] for i in range(18)]))
        scale = table(element_rows(phase, k, layers), PHASE_STIFFNESS)
        held[2, 0:rows, :] = scale * own[0:rows]
        return flat(high), total + held[2]

    held[2] = zero
    _, total = lax.fori_loop(0, layers, again, (flat(second_layer(0)), zero), unroll=True)
    for i, x in enumerate(totals + (total,)):
        x = jnp.where(row < rows, x, 0.0)
        x = jnp.sum(jnp.sum(x, axis=0, keepdims=True), axis=1, keepdims=True)
        sums[i : i + 1, :] = jnp.broadcast_to(x, (1, LANES))
    sums[4:, :] = jnp.zeros((4, LANES), jnp.float32)


def combine_kernel(base, second, energy, sums, displacement, sensitivity):
    a, b, d, e = (sums[i : i + 1, :] for i in range(4))
    ratio = b / a
    curve = a + b
    alpha = a / curve
    rest = d - b * ratio
    bend = e - 2.0 * ratio * (b + d) + ratio * ratio * curve
    alpha_next = rest / (bend - rest * rest / curve)
    beta = alpha * alpha * rest / a
    first = alpha + alpha_next * beta + alpha * alpha_next * ratio
    other = -alpha * alpha_next
    displacement[...] = first * base[...] + other * second[...]
    sensitivity[...] = (first * first) * energy[0] + (2.0 * first * other) * energy[1] + (other * other) * energy[2]


def exchange(one, two, axis):
    count = lax.axis_size(axis)
    if count % 2 == 0:
        far = lax.ppermute(two, axis, [(i, (i - 1) % count if i % 2 == 0 else (i + 1) % count) for i in range(count)])
        near = lax.ppermute(one, axis, [(i, i ^ 1) for i in range(count)])
        return near, far
    high = lax.ppermute(one, axis, [((i + 1) % count, i) for i in range(count)])
    low = lax.ppermute(two, axis, [(i, (i + 1) % count) for i in range(count)])
    return high, low


def total_over(x, axis):
    count = lax.axis_size(axis)
    if count & (count - 1):
        return lax.psum(x, axis)
    step = 1
    while step < count:
        width = 4 if count // step >= 4 else 2
        group = [
            lax.ppermute(x, axis, [(i, i ^ (step * by)) for i in range(count)]) for by in range(1, width)
        ]
        x = functools.reduce(jnp.add, group, x)
        step *= width
    return x


def body(force, phase, fixed):
    comps, nodes, rows, width = force.shape
    layers = nodes - 1
    phase = phase.transpose(1, 0, 2).reshape(rows * layers, width)
    f32 = jnp.float32
    paired_x = lax.axis_size("gx") % 2 == 0
    paired_y = lax.axis_size("gy") % 2 == 0
    column = jax.ShapeDtypeStruct((2, 8, LANES), f32)
    message = jax.ShapeDtypeStruct((FULL, LANES), f32)

    def call(kernel, out_shape, scratch=()):
        return pl.pallas_call(
            kernel,
            out_shape=out_shape,
            scratch_shapes=scratch,
            compiler_params=PARAMS,
        )

    col1, col2, row1, row2 = call(
        functools.partial(pack_kernel, paired_x, paired_y),
        (column, column, message, message),
        [pltpu.VMEM((comps * nodes + 2, 8, LANES), f32)],
    )(force, phase, fixed)
    near, far = exchange(col1, col2, "gy")
    strip, row1, row2 = call(
        functools.partial(strip_kernel, paired_x, paired_y),
        (jax.ShapeDtypeStruct((6, 8, LANES), f32), message, message),
    )(col1, col2, near, far, row1, row2)
    near, far = exchange(row1, row2, "gx")
    base, second, energy, sums = call(
        functools.partial(operator_kernel, paired_x),
        (
            jax.ShapeDtypeStruct(force.shape, f32),
            jax.ShapeDtypeStruct(force.shape, f32),
            jax.ShapeDtypeStruct((3,) + phase.shape, f32),
            jax.ShapeDtypeStruct((8, LANES), f32),
        ),
        [
            pltpu.VMEM((FULL, LANES), f32),
            pltpu.VMEM((FULL, LANES), f32),
            pltpu.VMEM((3, 8, LANES), f32),
            pltpu.VMEM((layers, 18, 8, LANES), f32),
            pltpu.VMEM((comps * nodes, 8, LANES), f32),
            pltpu.VMEM((nodes, 8, LANES), f32),
        ],
    )(force, phase, fixed, strip, near, far)
    sums = total_over(total_over(sums, "gy"), "gx")
    displacement, sensitivity = call(
        combine_kernel,
        (jax.ShapeDtypeStruct(force.shape, f32), jax.ShapeDtypeStruct(phase.shape, f32)),
    )(base, second, energy, sums)
    return displacement, sensitivity.reshape(rows, layers, width).transpose(1, 0, 2)


def solution(mesh):
    return jax.shard_map(
        body,
        mesh=mesh,
        in_specs=(
            P(None, None, ("parts", "gx"), "gy"),
            P(None, ("parts", "gx"), "gy"),
            P(None, ("parts", "gx"), "gy"),
        ),
        out_specs=(P(None, None, ("parts", "gx"), "gy"), P(None, ("parts", "gx"), "gy")),
        check_vma=False,
    )
```

```python
import functools

import jax
import jax.numpy as jnp
import numpy as np
from jax import lax
from jax.experimental import pallas as pl
from jax.experimental.pallas import tpu as pltpu
from jax.sharding import PartitionSpec as P

PHASE_STIFFNESS = (0.125, 0.343, 0.614, 1.0)
PHASE_SLOPE = (0.75, 1.47, 2.17, 3.0)
POISSON = 0.3
LAME = POISSON / ((1.0 + POISSON) * (1.0 - 2.0 * POISSON))
SHEAR = 1.0 / (2.0 * (1.0 + POISSON))
KE_DIAGONAL = (LAME + 4.0 * SHEAR) / 9.0

SLOT = 24
LANES = 128
FULL = 168
CORNERS = 152

VMEM = pl.BlockSpec(memory_space=pltpu.VMEM)
PARAMS = pltpu.CompilerParams(vmem_limit_bytes=32 * 1024 * 1024)


def lanes():
    return lax.broadcasted_iota(jnp.int32, (8, LANES), 1)


def sublanes():
    return lax.broadcasted_iota(jnp.int32, (8, LANES), 0)


def table(phase, values):
    out = jnp.full(phase.shape, values[3], jnp.float32)
    for index in (2, 1, 0):
        out = jnp.where(phase == index, jnp.float32(values[index]), out)
    return out


def element_rows(ref, k, layers):
    return ref[pl.ds(k, ref.shape[0] // layers, stride=layers), :]


def lane_roll(x, by):
    if isinstance(by, int):
        by = by % LANES
        return x if by == 0 else pltpu.roll(x, by, 1)
    return pltpu.roll(x, lax.rem(by + LANES, LANES), 1)


def is_even(axis):
    return lax.rem(lax.axis_index(axis), 2) == 0


def pack_kernel(paired_x, paired_y, rhs_0, rhs_1, rhs_2, phase, fixed, col1, col2, row1, row2, pad):
    rhs, comps = (rhs_0, rhs_1, rhs_2), 3
    nodes, rows, width = rhs_0.shape
    layers = nodes - 1
    lane = lanes()
    even_x = is_even("gx") if paired_x else True
    even_y = is_even("gy") if paired_y else True
    zero = jnp.zeros((8, LANES), jnp.float32)
    low = [zero, zero]
    high = [zero, zero]
    pad[...] = jnp.zeros(pad.shape, jnp.float32)

    def place(planes, tile, column, plane, slot, k):
        target = slot * SLOT + k
        planes[plane] = jnp.where(lane == target, lane_roll(tile, target - column), planes[plane])

    def put(at_low, at_high, value_low, value_high):
        if paired_x:
            if value_high is None:
                value_high = jnp.zeros((1, LANES), jnp.float32)
            row1[at_low : at_low + 1, :] = jnp.where(even_x, value_high, value_low)
            row2[at_low : at_low + 1, :] = jnp.where(even_x, value_low, value_high)
        else:
            row1[at_low : at_low + 1, :] = value_low
            row2[at_low : at_low + 1, :] = jnp.zeros((1, LANES), jnp.float32) if value_high is None else value_high

    for k in range(nodes):
        free = (1 - fixed[k]).astype(jnp.float32)
        for c in range(comps):
            q = c * nodes + k
            r0 = rhs[c][k]
            pad[q, 0:rows, :] = r0
            tile = pad[q]
            place(low, tile, 0, 0, c, k)
            place(low, tile, 1, 1, c, k)
            place(high, tile, width - 1, 0, c, k)
            put(q, q, r0[0:1], r0[rows - 1 : rows])
            put(comps * nodes + 2 * layers + q, None, r0[1:2], None)
        pad[comps * nodes, 0:rows, :] = free
        place(low, pad[comps * nodes], 0, 0, 3, k)
        put(2 * comps * nodes + 2 * layers + k, None, free[0:1], None)
        if k < layers:
            scale = table(element_rows(phase, k, layers), PHASE_STIFFNESS)
            pad[comps * nodes + 1, 0:rows, :] = scale
            tile = pad[comps * nodes + 1]
            place(low, tile, 0, 1, 3, k)
            place(low, tile, 1, 1, 4, k)
            place(high, tile, width - 2, 0, 3, k)
            place(high, tile, width - 1, 0, 4, k)
            put(comps * nodes + k, None, scale[0:1], scale[rows - 2 : rows - 1])
            put(comps * nodes + layers + k, None, scale[1:2], scale[rows - 1 : rows])
    used = 2 * comps * nodes + 2 * layers + nodes
    row1[used:, :] = jnp.zeros((FULL - used, LANES), jnp.float32)
    row2[used:, :] = jnp.zeros((FULL - used, LANES), jnp.float32)
    for plane in range(2):
        if paired_y:
            col1[plane] = jnp.where(even_y, high[plane], low[plane])
            col2[plane] = jnp.where(even_y, low[plane], high[plane])
        else:
            col1[plane] = low[plane]
            col2[plane] = high[plane]


def strip_kernel(paired_x, paired_y, own1, own2, got1, got2, row1, row2, strip, out1, out2):
    lane = lanes()
    even_x = is_even("gx") if paired_x else True
    even_y = is_even("gy") if paired_y else True
    if paired_y:
        own_low = [jnp.where(even_y, own2[p], own1[p]) for p in range(2)]
        own_high = [jnp.where(even_y, own1[p], own2[p]) for p in range(2)]
        from_low = [jnp.where(even_y, got2[p], got1[p]) for p in range(2)]
        from_high = [jnp.where(even_y, got1[p], got2[p]) for p in range(2)]
    else:
        own_low, own_high = [own1[p] for p in range(2)], [own2[p] for p in range(2)]
        from_low, from_high = [got2[p] for p in range(2)], [got1[p] for p in range(2)]

    def build(*items):
        out = jnp.zeros((8, LANES), jnp.float32)
        for planes, plane, source, slot in items:
            inside = (lane >= slot * SLOT) & (lane < slot * SLOT + SLOT)
            out = jnp.where(inside, lane_roll(planes[plane], (slot - source) * SLOT), out)
        return out

    planes = [
        build(
            (from_low, 0, c, 0),
            (own_low, 0, c, 1),
            (own_high, 0, c, 2),
            (from_high, 0, c, 3),
            (from_high, 1, c, 4),
        )
        for c in range(3)
    ]
    planes.append(
        build((from_low, 0, 3, 0), (from_low, 0, 4, 1), (own_high, 0, 3, 2), (own_high, 0, 4, 3), (from_high, 1, 3, 4))
    )
    planes.append(
        build((from_low, 0, 4, 0), (own_low, 1, 3, 1), (own_high, 0, 4, 2), (from_high, 1, 3, 3), (from_high, 1, 4, 4))
    )
    planes.append(build((from_high, 0, 3, 3)))
    rows = 6
    out1[...] = row1[...]
    out2[...] = row2[...]
    for p, plane in enumerate(planes):
        strip[p] = plane
        for which in range(2):
            at = CORNERS + 2 * p + which
            low_row = plane[which : which + 1]
            high_row = plane[rows - 2 + which : rows - 1 + which]
            if paired_x:
                out1[at : at + 1, :] = jnp.where(even_x, high_row, low_row)
                out2[at : at + 1, :] = jnp.where(even_x, low_row, high_row)
            else:
                out1[at : at + 1, :] = low_row
                out2[at : at + 1, :] = high_row


PLANE = ("", "1", "2", "12")


def split_layers(lo, hi):
    sums = [{m: lo[c][m] + hi[c][m] for m in ("1", "2", "12")} for c in range(3)]
    diffs = [{m: hi[c][m] - lo[c][m] for m in PLANE} for c in range(3)]
    u, v, w = range(3)
    return (
        diffs[u][""], sums[v]["1"], sums[w]["2"],
        sums[u]["1"] + diffs[v][""], sums[u]["2"] + diffs[w][""], sums[v]["2"] + sums[w]["1"],
        diffs[u]["1"], sums[w]["12"], diffs[u]["2"], sums[v]["12"], diffs[v]["1"], diffs[w]["2"],
        sums[u]["12"], diffs[v]["2"], diffs[w]["1"],
        diffs[u]["12"], diffs[v]["12"], diffs[w]["12"],
    )


def stress(m):
    one, two, three = 1.0 / 16.0, 1.0 / 48.0, 1.0 / 144.0
    trace = (LAME * one) * (m[0] + m[1] + m[2])
    out = [trace + (2.0 * SHEAR * one) * m[i] for i in range(3)]
    out += [(SHEAR * one) * m[i] for i in (3, 4, 5)]
    own, other = (LAME + 3.0 * SHEAR) * two, LAME * two
    for i in (6, 8, 10):
        out += [own * m[i] + other * m[i + 1], own * m[i + 1] + other * m[i]]
    total = m[12] + m[13] + m[14]
    out += [(SHEAR * two) * (m[i] + total) for i in (12, 13, 14)]
    out += [((LAME + 4.0 * SHEAR) * three) * m[i] for i in (15, 16, 17)]
    return out


def inner(g, m):
    parts = [g[i] * m[i] for i in range(18)]
    while len(parts) > 1:
        parts = [parts[i] + parts[i + 1] if i + 1 < len(parts) else parts[i] for i in range(0, len(parts), 2)]
    return parts[0]


def join_layers(g):
    sums = [
        {"1": g[3], "2": g[4], "12": g[12]},
        {"1": g[1], "2": g[5], "12": g[9]},
        {"1": g[5], "2": g[2], "12": g[7]},
    ]
    diffs = [
        {"": g[0], "1": g[6], "2": g[8], "12": g[15]},
        {"": g[3], "1": g[10], "2": g[13], "12": g[16]},
        {"": g[4], "1": g[14], "2": g[11], "12": g[17]},
    ]
    lower = [{m: (sums[c][m] - diffs[c][m] if m else -diffs[c][m]) for m in PLANE} for c in range(3)]
    upper = [{m: (sums[c][m] + diffs[c][m] if m else diffs[c][m]) for m in PLANE} for c in range(3)]
    return lower, upper


def in_plane(x, right, up):
    y = right(x)
    near, far = x + y, y - x
    near_up, far_up = up(near), up(far)
    return {"": near + near_up, "1": near_up - near, "2": far + far_up, "12": far_up - far}


def out_of_plane(f, right, up):
    plain = (f[""] - f["2"]) + right(f[""] + f["2"])
    steep = (f["1"] - f["12"]) + right(f["1"] + f["12"])
    return (plain - steep) + up(plain + steep)


def operator_kernel(
    paired_x, rhs_0, rhs_1, rhs_2, phase, fixed, strip, got1, got2,
    base, second, energy, sums,
    lo, hi, held, modes, residual, inverse,
):
    rhs, comps = (rhs_0, rhs_1, rhs_2), 3
    nodes, rows, width = rhs_0.shape
    layers = nodes - 1
    lane, row = lanes(), sublanes()
    last_row, below = row == 6, row == 7
    cn = comps * nodes
    if paired_x:
        even_x = is_even("gx")
        lo[...] = jnp.where(even_x, got2[...], got1[...])
        hi[...] = jnp.where(even_x, got1[...], got2[...])
    else:
        lo[...] = got2[...]
        hi[...] = got1[...]

    def spread(ref, at):
        return jnp.broadcast_to(ref[pl.ds(at, 1), :], (8, LANES))

    def roll_up(x):
        return pltpu.roll(x, 7, 0)

    def roll_down(x):
        return pltpu.roll(x, 1, 0)

    def corner(ref, p, which):
        return spread(ref, CORNERS + 2 * p + which)

    tiles = [
        jnp.where(row < 6, strip[p], jnp.where(last_row, corner(hi, p, 0), corner(lo, p, 1))) for p in range(6)
    ]
    sevens = [corner(hi, p, 1) for p in range(5)]
    left, right = tiles[3], tiles[4]
    around = left + right
    around_7 = sevens[3] + sevens[4]
    around_m2 = corner(lo, 3, 0) + corner(lo, 4, 0)

    def node_rows(x, x_m2):
        return x + jnp.where(below, x_m2, roll_down(x))

    def node_row_7(x, x_7):
        return jnp.broadcast_to(x[6:7], (8, LANES)) + x_7

    def strip_diagonal(x):
        return KE_DIAGONAL * (x + lane_roll(x, 1))

    strip_diag = strip_diagonal(node_rows(around, around_m2))
    strip_diag_7 = strip_diagonal(node_row_7(around, around_7))
    strip_inv = jnp.where(strip_diag > 0.0, 1.0 / strip_diag, 0.0)
    strip_inv_7 = jnp.where(strip_diag_7 > 0.0, 1.0 / strip_diag_7, 0.0)
    strip_base = [tiles[c] * strip_inv for c in range(3)]
    strip_base_7 = [sevens[c] * strip_inv_7 for c in range(3)]
    edge_rows = node_rows(right, corner(lo, 4, 0))
    edge_rows_7 = node_row_7(right, sevens[4])

    slot = lane // SLOT
    live = (slot == 0) | (slot == 2) | (slot == 3)
    strip_scale = jnp.where(live, right, 0.0)

    def strip_modes(c):
        x, x_7 = strip_base[c], strip_base_7[c]
        near, near_7 = x + lane_roll(x, -SLOT), x_7 + lane_roll(x_7, -SLOT)
        far, far_7 = lane_roll(x, -SLOT) - x, lane_roll(x_7, -SLOT) - x_7
        near_up = jnp.where(last_row, near_7, roll_up(near))
        far_up = jnp.where(last_row, far_7, roll_up(far))
        return {"": near + near_up, "1": near_up - near, "2": far + far_up, "12": far_up - far}

    lower = [strip_modes(c) for c in range(3)]
    upper = [{m: lane_roll(lower[c][m], -1) for m in PLANE} for c in range(3)]
    g = [strip_scale * x for x in stress(split_layers(lower, upper))]
    f_low, f_up = join_layers(g)
    f_strip = []
    for c in range(3):
        f = {m: f_low[c][m] + lane_roll(f_up[c][m], 1) for m in PLANE}
        f_strip.append(out_of_plane(f, lambda x: lane_roll(x, SLOT), roll_down))
    strip_second = [jnp.where(tiles[5] > 0.0, (f_strip[c] - tiles[c]) * strip_inv, 0.0) for c in range(3)]

    def scale_of(k):
        held[0, 0:rows, :] = table(element_rows(phase, k, layers), PHASE_STIFFNESS)
        held[0, 6:7, :] = hi[pl.ds(cn + k, 1), :]
        held[0, 7:8, :] = lo[pl.ds(cn + layers + k, 1), :]
        return held[0], spread(hi, cn + layers + k), spread(lo, cn + k)

    def box(k):
        x, x_7, x_m2 = scale_of(k)
        r, r_7 = node_rows(x, x_m2), node_row_7(x, x_7)
        r = r + jnp.where(lane == 0, lane_roll(edge_rows, -k), lane_roll(r, 1))
        r_7 = r_7 + jnp.where(lane == 0, lane_roll(edge_rows_7, -k), lane_roll(r_7, 1))
        return x, r, r_7

    def first_layer(k, around_node, around_node_7):
        inv = 1.0 / (KE_DIAGONAL * around_node)
        inv_7 = 1.0 / (KE_DIAGONAL * around_node_7)
        inverse[k] = inv
        out = []
        for c in range(3):
            q = c * nodes + k
            residual[q, 0:rows, :] = rhs[c][k]
            residual[q, 6:7, :] = hi[pl.ds(q, 1), :]
            residual[q, 7:8, :] = lo[pl.ds(q, 1), :]
            x = residual[q] * inv
            x_7 = spread(hi, cn + 2 * layers + q) * inv_7
            base[c, k] = x[0:rows]
            shift = LANES - 1 - (3 * SLOT + k)
            at_end = lane == LANES - 1
            y = jnp.where(at_end, lane_roll(strip_base[c], shift), lane_roll(x, -1))
            y_7 = jnp.where(at_end, lane_roll(strip_base_7[c], shift), lane_roll(x_7, -1))
            near, far, near_7, far_7 = x + y, y - x, x_7 + y_7, y_7 - x_7
            near_up = jnp.where(last_row, near_7, roll_up(near))
            far_up = jnp.where(last_row, far_7, roll_up(far))
            out.append({"": near + near_up, "1": near_up - near, "2": far + far_up, "12": far_up - far})
        return out

    def finish_layer(k, f, totals):
        inv = inverse[k]
        held[1, 0:rows, :] = 1.0 - fixed[k].astype(jnp.float32)
        held[1, 6:7, :] = hi[pl.ds(2 * cn + 2 * layers + k, 1), :]
        free = held[1] > 0.0
        a, b, d = totals
        for c in range(3):
            q = c * nodes + k
            r0 = residual[q]
            image = out_of_plane(f[c], lambda x: jnp.where(lane == 0, 0.0, lane_roll(x, 1)), roll_down)
            image = image + jnp.where(lane == 0, lane_roll(f_strip[c], -(SLOT + k)), 0.0)
            d0 = jnp.where(free, r0 * inv, r0)
            s = jnp.where(free, image, d0) - r0
            v = jnp.where(free, s * inv, s)
            second[c, k] = v[0:rows]
            residual[q] = v
            a, b, d = a + r0 * d0, b + d0 * s, d + s * v
        return a, b, d

    def store_energy(which, k, value):
        slope = table(element_rows(phase, k, layers), PHASE_SLOPE)
        energy[which, pl.ds(k, rows, stride=layers), :] = -slope * value[0:rows]

    def flat(x):
        return tuple(x[c][m] for c in range(3) for m in PLANE)

    def unflat(x):
        return [{m: x[4 * c + i] for i, m in enumerate(PLANE)} for c in range(3)]

    zero = jnp.zeros((8, LANES), jnp.float32)
    held[1] = zero
    scale_0, box_0, box_0_7 = box(0)
    start = first_layer(0, box_0, box_0_7)

    def element(k, low_modes, high_modes, scale, pending, totals):
        m = split_layers(low_modes, high_modes)
        g = stress(m)
        store_energy(0, k, inner(g, m))
        for i in range(18):
            modes[k, i] = m[i]
        f_lower, f_upper = join_layers([scale * x for x in g])
        done = [{m: pending[c][m] + f_lower[c][m] for m in PLANE} for c in range(3)]
        return f_upper, finish_layer(k, done, totals)

    def forward(k, carry):
        low_modes, pending, totals, scale, b, b_7 = carry
        next_scale, next_b, next_b_7 = box(k + 1)
        high = first_layer(k + 1, b + next_b, b_7 + next_b_7)
        f_upper, totals = element(k, unflat(low_modes), high, scale, unflat(pending), totals)
        return flat(high), flat(f_upper), totals, next_scale, next_b, next_b_7

    carry = (flat(start), (zero,) * 12, (zero,) * 3, scale_0, box_0, box_0_7)
    low_modes, pending, totals, scale, b, b_7 = lax.fori_loop(0, layers - 1, forward, carry, unroll=True)
    high = first_layer(layers, b, b_7)
    f_upper, totals = element(layers - 1, unflat(low_modes), high, scale, unflat(pending), totals)
    totals = finish_layer(layers, f_upper, totals)

    def second_layer(k):
        out = []
        for c in range(3):
            fill = lane_roll(strip_second[c], LANES - 1 - (3 * SLOT + k))
            x = residual[c * nodes + k]
            out.append(in_plane(x, lambda t: jnp.where(lane == LANES - 1, fill, lane_roll(t, -1)), roll_up))
        return out

    def again(k, carry):
        low_modes, total = carry
        high = second_layer(k + 1)
        m = split_layers(unflat(low_modes), high)
        g = stress(m)
        own = inner(g, m)
        store_energy(2, k, own)
        store_energy(1, k, inner(g, [modes[k, i] for i in range(18)]))
        scale = table(element_rows(phase, k, layers), PHASE_STIFFNESS)
        held[2, 0:rows, :] = scale * own[0:rows]
        return flat(high), total + held[2]

    held[2] = zero
    _, total = lax.fori_loop(0, layers, again, (flat(second_layer(0)), zero), unroll=True)
    for i, x in enumerate(totals + (total,)):
        x = jnp.where(row < rows, x, 0.0)
        x = jnp.sum(jnp.sum(x, axis=0, keepdims=True), axis=1, keepdims=True)
        sums[i : i + 1, :] = jnp.broadcast_to(x, (1, LANES))
    sums[4:, :] = jnp.zeros((4, LANES), jnp.float32)


def combine_kernel(base, second, energy, sums, displacement, sensitivity):
    a, b, d, e = (sums[i : i + 1, :] for i in range(4))
    ratio = b / a
    curve = a + b
    alpha = a / curve
    rest = d - b * ratio
    bend = e - 2.0 * ratio * (b + d) + ratio * ratio * curve
    alpha_next = rest / (bend - rest * rest / curve)
    beta = alpha * alpha * rest / a
    first = alpha + alpha_next * beta + alpha * alpha_next * ratio
    other = -alpha * alpha_next
    displacement[...] = first * base[...] + other * second[...]
    sensitivity[...] = (first * first) * energy[0] + (2.0 * first * other) * energy[1] + (other * other) * energy[2]


def exchange(one, two, axis):
    count = lax.axis_size(axis)
    if count % 2 == 0:
        far = lax.ppermute(two, axis, [(i, (i - 1) % count if i % 2 == 0 else (i + 1) % count) for i in range(count)])
        near = lax.ppermute(one, axis, [(i, i ^ 1) for i in range(count)])
        return near, far
    high = lax.ppermute(one, axis, [((i + 1) % count, i) for i in range(count)])
    low = lax.ppermute(two, axis, [(i, (i + 1) % count) for i in range(count)])
    return high, low


def total_over(x, axis):
    count = lax.axis_size(axis)
    if count & (count - 1):
        return lax.psum(x, axis)
    step = 1
    while step < count:
        width = 4 if count // step >= 4 else 2
        group = [
            lax.ppermute(x, axis, [(i, i ^ (step * by)) for i in range(count)]) for by in range(1, width)
        ]
        x = functools.reduce(jnp.add, group, x)
        step *= width
    return x


def body(force, phase, fixed):
    comps, nodes, rows, width = force.shape
    layers = nodes - 1
    phase = phase.transpose(1, 0, 2).reshape(rows * layers, width)
    rhs = [(1 - fixed).astype(jnp.float32) * force[c] for c in range(comps)]
    f32 = jnp.float32
    paired_x = lax.axis_size("gx") % 2 == 0
    paired_y = lax.axis_size("gy") % 2 == 0
    column = jax.ShapeDtypeStruct((2, 8, LANES), f32)
    message = jax.ShapeDtypeStruct((FULL, LANES), f32)

    def call(kernel, out_shape, scratch=()):
        return pl.pallas_call(
            kernel,
            out_shape=out_shape,
            scratch_shapes=scratch,
            compiler_params=PARAMS,
        )

    col1, col2, row1, row2 = call(
        functools.partial(pack_kernel, paired_x, paired_y),
        (column, column, message, message),
        [pltpu.VMEM((comps * nodes + 2, 8, LANES), f32)],
    )(*rhs, phase, fixed)
    near, far = exchange(col1, col2, "gy")
    strip, row1, row2 = call(
        functools.partial(strip_kernel, paired_x, paired_y),
        (jax.ShapeDtypeStruct((6, 8, LANES), f32), message, message),
    )(col1, col2, near, far, row1, row2)
    near, far = exchange(row1, row2, "gx")
    base, second, energy, sums = call(
        functools.partial(operator_kernel, paired_x),
        (
            jax.ShapeDtypeStruct(force.shape, f32),
            jax.ShapeDtypeStruct(force.shape, f32),
            jax.ShapeDtypeStruct((3,) + phase.shape, f32),
            jax.ShapeDtypeStruct((8, LANES), f32),
        ),
        [
            pltpu.VMEM((FULL, LANES), f32),
            pltpu.VMEM((FULL, LANES), f32),
            pltpu.VMEM((3, 8, LANES), f32),
            pltpu.VMEM((layers, 18, 8, LANES), f32),
            pltpu.VMEM((comps * nodes, 8, LANES), f32),
            pltpu.VMEM((nodes, 8, LANES), f32),
        ],
    )(*rhs, phase, fixed, strip, near, far)
    sums = total_over(total_over(sums, "gy"), "gx")
    displacement, sensitivity = call(
        combine_kernel,
        (jax.ShapeDtypeStruct(force.shape, f32), jax.ShapeDtypeStruct(phase.shape, f32)),
    )(base, second, energy, sums)
    return displacement, sensitivity.reshape(rows, layers, width).transpose(1, 0, 2)


def solution(mesh):
    return jax.shard_map(
        body,
        mesh=mesh,
        in_specs=(
            P(None, None, ("parts", "gx"), "gy"),
            P(None, ("parts", "gx"), "gy"),
            P(None, ("parts", "gx"), "gy"),
        ),
        out_specs=(P(None, None, ("parts", "gx"), "gy"), P(None, ("parts", "gx"), "gy")),
        check_vma=False,
    )
```

```python
import functools

import jax
import jax.numpy as jnp
import numpy as np
from jax import lax
from jax.experimental import pallas as pl
from jax.experimental.pallas import tpu as pltpu
from jax.sharding import PartitionSpec as P

PHASE_STIFFNESS = (0.125, 0.343, 0.614, 1.0)
PHASE_SLOPE = (0.75, 1.47, 2.17, 3.0)
POISSON = 0.3
LAME = POISSON / ((1.0 + POISSON) * (1.0 - 2.0 * POISSON))
SHEAR = 1.0 / (2.0 * (1.0 + POISSON))
KE_DIAGONAL = (LAME + 4.0 * SHEAR) / 9.0

SLOTS = 7
LANES = 128
FULL = 168
CORNERS = 152

VMEM = pl.BlockSpec(memory_space=pltpu.VMEM)
PARAMS = pltpu.CompilerParams(vmem_limit_bytes=32 * 1024 * 1024)


def lanes():
    return lax.broadcasted_iota(jnp.int32, (8, LANES), 1)


def sublanes():
    return lax.broadcasted_iota(jnp.int32, (8, LANES), 0)


def table(phase, values):
    out = jnp.full(phase.shape, values[3], jnp.float32)
    for index in (2, 1, 0):
        out = jnp.where(phase == index, jnp.float32(values[index]), out)
    return out


def element_rows(ref, k, layers):
    return ref[pl.ds(k, ref.shape[0] // layers, stride=layers), :]


def lane_roll(x, by):
    if isinstance(by, int):
        by = by % LANES
        return x if by == 0 else pltpu.roll(x, by, 1)
    return pltpu.roll(x, lax.rem(by + LANES, LANES), 1)


def is_even(axis):
    return lax.rem(lax.axis_index(axis), 2) == 0


def gather(nodes, *items):
    lane = lanes()
    slot = jnp.where(lane < nodes * SLOTS, lax.rem(lane, SLOTS), SLOTS)
    out = jnp.zeros((8, LANES), jnp.float32)
    for plane, by, first, count in items:
        out = jnp.where((slot >= first) & (slot < first + count), lane_roll(plane, by), out)
    return out


def column_kernel(paired, rhs_0, rhs_1, rhs_2, phase, fixed, own, col1, col2, pad):
    rhs = (rhs_0, rhs_1, rhs_2)
    nodes, rows, width = rhs_0.shape
    layers = nodes - 1
    lane = lanes()
    even = is_even("gy") if paired else True
    pad[...] = jnp.zeros(pad.shape, jnp.float32)
    planes = [jnp.zeros((8, LANES), jnp.float32)] * 5
    for k in range(nodes):
        here = (lane >= k * SLOTS) & (lane < k * SLOTS + 5)
        values = [rhs[c][k] for c in range(3)]
        values.append(table(element_rows(phase, k, layers), PHASE_STIFFNESS) if k < layers else None)
        values.append((1 - fixed[k]).astype(jnp.float32))
        for p, value in enumerate(values):
            if value is not None:
                pad[5 * k + p, 0:rows, :] = value
                planes[p] = jnp.where(here, lane_roll(pad[5 * k + p], k * SLOTS + 3), planes[p])
    for p in range(5):
        own[p] = planes[p]
    high = [
        gather(nodes, (planes[0], -2, 0, 1), (planes[1], -1, 1, 1), (planes[2], 0, 2, 1), (planes[3], 2, 3, 2)),
        jnp.zeros((8, LANES), jnp.float32),
    ]
    low = [
        gather(nodes, (planes[0], -3, 0, 2), (planes[1], -1, 2, 2), (planes[2], 1, 4, 2), (planes[4], 3, 6, 1)),
        planes[3],
    ]
    for p in range(2):
        if paired:
            col1[p] = jnp.where(even, high[p], low[p])
            col2[p] = jnp.where(even, low[p], high[p])
        else:
            col1[p] = low[p]
            col2[p] = high[p]


def row_kernel(paired, rhs_0, rhs_1, rhs_2, phase, fixed, row1, row2):
    rhs = (rhs_0, rhs_1, rhs_2)
    nodes, rows, width = rhs_0.shape
    layers, cn = nodes - 1, 3 * nodes
    even = is_even("gx") if paired else True
    nothing = jnp.zeros((1, LANES), jnp.float32)

    def put(at, low, high):
        if paired:
            row1[at : at + 1, :] = jnp.where(even, high, low)
            row2[at : at + 1, :] = jnp.where(even, low, high)
        else:
            row1[at : at + 1, :] = low
            row2[at : at + 1, :] = high

    for k in range(nodes):
        for c in range(3):
            q = c * nodes + k
            put(q, rhs[c][k, 0:1], rhs[c][k, rows - 1 : rows])
            put(cn + 2 * layers + q, rhs[c][k, 1:2], nothing)
        put(2 * cn + 2 * layers + k, (1 - fixed[k, 0:1]).astype(jnp.float32), nothing)
    scale = [table(phase[i * layers : (i + 1) * layers], PHASE_STIFFNESS) for i in (0, 1, rows - 2, rows - 1)]
    for i in range(2):
        at = cn + i * layers
        if paired:
            row1[at : at + layers, :] = jnp.where(even, scale[2 + i], scale[i])
            row2[at : at + layers, :] = jnp.where(even, scale[i], scale[2 + i])
        else:
            row1[at : at + layers, :] = scale[i]
            row2[at : at + layers, :] = scale[2 + i]
    used = 2 * cn + 2 * layers + nodes
    row1[used:, :] = jnp.zeros((FULL - used, LANES), jnp.float32)
    row2[used:, :] = jnp.zeros((FULL - used, LANES), jnp.float32)


def strip_kernel(nodes, paired_x, paired_y, own, got1, got2, row1, row2, strip, out1, out2):
    even_x = is_even("gx") if paired_x else True
    even_y = is_even("gy") if paired_y else True
    if paired_y:
        from_low = jnp.where(even_y, got2[0], got1[0])
        from_high = [jnp.where(even_y, got1[p], got2[p]) for p in range(2)]
    else:
        from_low, from_high = got2[0], [got1[p] for p in range(2)]
    planes = [
        gather(nodes, (from_low, -c, 0, 1), (own[c], -2, 1, 2), (own[c], 2, 3, 2), (from_high[0], 5 - 2 * c, 5, 2))
        for c in range(3)
    ]
    scale = own[3]
    planes.append(gather(nodes, (from_low, -3, 0, 2), (scale, -1, 2, 1), (scale, 3, 3, 3), (from_high[1], 3, 6, 1)))
    planes.append(gather(nodes, (from_low, -4, 0, 1), (scale, -2, 1, 2), (scale, 2, 3, 2), (from_high[1], 2, 5, 2)))
    planes.append(gather(nodes, (own[4], -2, 1, 1), (own[4], 2, 4, 1), (from_high[0], -1, 5, 1)))
    rows = 6
    out1[...] = row1[...]
    out2[...] = row2[...]
    for p, plane in enumerate(planes):
        strip[p] = plane
        for which in range(2):
            at = CORNERS + 2 * p + which
            low_row = plane[which : which + 1]
            high_row = plane[rows - 2 + which : rows - 1 + which]
            if paired_x:
                out1[at : at + 1, :] = jnp.where(even_x, high_row, low_row)
                out2[at : at + 1, :] = jnp.where(even_x, low_row, high_row)
            else:
                out1[at : at + 1, :] = low_row
                out2[at : at + 1, :] = high_row


PLANE = ("", "1", "2", "12")


def split_layers(lo, hi):
    sums = [{m: lo[c][m] + hi[c][m] for m in ("1", "2", "12")} for c in range(3)]
    diffs = [{m: hi[c][m] - lo[c][m] for m in PLANE} for c in range(3)]
    u, v, w = range(3)
    return (
        diffs[u][""], sums[v]["1"], sums[w]["2"],
        sums[u]["1"] + diffs[v][""], sums[u]["2"] + diffs[w][""], sums[v]["2"] + sums[w]["1"],
        diffs[u]["1"], sums[w]["12"], diffs[u]["2"], sums[v]["12"], diffs[v]["1"], diffs[w]["2"],
        sums[u]["12"], diffs[v]["2"], diffs[w]["1"],
        diffs[u]["12"], diffs[v]["12"], diffs[w]["12"],
    )


def stress(m):
    one, two, three = 1.0 / 16.0, 1.0 / 48.0, 1.0 / 144.0
    trace = (LAME * one) * (m[0] + m[1] + m[2])
    out = [trace + (2.0 * SHEAR * one) * m[i] for i in range(3)]
    out += [(SHEAR * one) * m[i] for i in (3, 4, 5)]
    own, other = (LAME + 3.0 * SHEAR) * two, LAME * two
    for i in (6, 8, 10):
        out += [own * m[i] + other * m[i + 1], own * m[i + 1] + other * m[i]]
    total = m[12] + m[13] + m[14]
    out += [(SHEAR * two) * (m[i] + total) for i in (12, 13, 14)]
    out += [((LAME + 4.0 * SHEAR) * three) * m[i] for i in (15, 16, 17)]
    return out


def inner(g, m):
    parts = [g[i] * m[i] for i in range(18)]
    while len(parts) > 1:
        parts = [parts[i] + parts[i + 1] if i + 1 < len(parts) else parts[i] for i in range(0, len(parts), 2)]
    return parts[0]


def join_layers(g):
    sums = [
        {"1": g[3], "2": g[4], "12": g[12]},
        {"1": g[1], "2": g[5], "12": g[9]},
        {"1": g[5], "2": g[2], "12": g[7]},
    ]
    diffs = [
        {"": g[0], "1": g[6], "2": g[8], "12": g[15]},
        {"": g[3], "1": g[10], "2": g[13], "12": g[16]},
        {"": g[4], "1": g[14], "2": g[11], "12": g[17]},
    ]
    lower = [{m: (sums[c][m] - diffs[c][m] if m else -diffs[c][m]) for m in PLANE} for c in range(3)]
    upper = [{m: (sums[c][m] + diffs[c][m] if m else diffs[c][m]) for m in PLANE} for c in range(3)]
    return lower, upper


def in_plane(x, right, up):
    y = right(x)
    near, far = x + y, y - x
    near_up, far_up = up(near), up(far)
    return {"": near + near_up, "1": near_up - near, "2": far + far_up, "12": far_up - far}


def out_of_plane(f, right, up):
    plain = (f[""] - f["2"]) + right(f[""] + f["2"])
    steep = (f["1"] - f["12"]) + right(f["1"] + f["12"])
    return (plain - steep) + up(plain + steep)


def operator_kernel(
    paired_x, rhs_0, rhs_1, rhs_2, phase, fixed, strip, got1, got2,
    base, second, edges, sums,
    lo, hi, held, residual, inverse, dense, far_base,
):
    rhs, comps = (rhs_0, rhs_1, rhs_2), 3
    nodes, rows, width = rhs_0.shape
    layers = nodes - 1
    lane, row = lanes(), sublanes()
    last_row, below = row == 6, row == 7
    cn = comps * nodes
    if paired_x:
        even_x = is_even("gx")
        lo[...] = jnp.where(even_x, got2[...], got1[...])
        hi[...] = jnp.where(even_x, got1[...], got2[...])
    else:
        lo[...] = got2[...]
        hi[...] = got1[...]

    def spread(ref, at):
        return jnp.broadcast_to(ref[pl.ds(at, 1), :], (8, LANES))

    def roll_up(x):
        return pltpu.roll(x, 7, 0)

    def roll_down(x):
        return pltpu.roll(x, 1, 0)

    def node_rows(x, x_m2):
        return x + jnp.where(below, x_m2, roll_down(x))

    def node_row_7(x, x_7):
        return jnp.broadcast_to(x[6:7], (8, LANES)) + x_7

    def plane_modes(x, y, x_up, y_up):
        near, far, near_up, far_up = x + y, y - x, x_up + y_up, y_up - x_up
        return {"": near + near_up, "1": near_up - near, "2": far + far_up, "12": far_up - far}

    def node_forces(f, by):
        sides = []
        for sign in (-1, 1):
            plain = f[""] + f["2"] if sign > 0 else f[""] - f["2"]
            steep = f["1"] + f["12"] if sign > 0 else f["1"] - f["12"]
            sides.append((plain - steep) + roll_down(plain + steep))
        return sides[0] + lane_roll(sides[1], by)

    def products(totals, d0, image, z, s, v):
        return tuple(t + x for t, x in zip(totals, (d0 * image, image * z, s * v, v * image)))

    def corner(ref, p, which):
        return spread(ref, CORNERS + 2 * p + which)

    tiles = [
        jnp.where(row < 6, strip[p], jnp.where(last_row, corner(hi, p, 0), corner(lo, p, 1))) for p in range(6)
    ]
    sevens = [corner(hi, p, 1) for p in range(5)]
    left, right = tiles[3], tiles[4]
    edge_rows = node_rows(right, corner(lo, 4, 0))
    edge_rows_7 = node_row_7(right, sevens[4])

    tall = lax.broadcasted_iota(jnp.int32, (layers, LANES), 0)
    wide = lax.broadcasted_iota(jnp.int32, (layers, LANES), 1)
    pair = hi[cn : cn + layers, :] + hi[cn + layers : cn + 2 * layers, :]
    edge = jnp.broadcast_to(edge_rows_7[0:1], (layers, LANES))
    edge = jnp.sum(jnp.where(wide == SLOTS * tall, edge, 0.0), axis=1, keepdims=True)
    dense[...] = jnp.zeros(dense.shape, jnp.float32)
    dense[1 : layers + 1, :] = pair + jnp.where(wide == 0, edge, pltpu.roll(pair, 1, 1))
    inv_7 = dense[0:24, :] + dense[1:25, :]
    inv_7 = jnp.where(inv_7 > 0.0, 1.0 / (KE_DIAGONAL * inv_7), 0.0)
    for c in range(3):
        x_7 = hi[cn + 2 * layers + c * nodes : cn + 2 * layers + c * nodes + 24, :] * inv_7
        far_base[c] = x_7
        far_base[3 + c] = pltpu.roll(x_7, LANES - 1, 1)

    def strip_diagonal(x):
        return KE_DIAGONAL * (x + lane_roll(x, SLOTS))

    strip_diag = strip_diagonal(node_rows(left + right, corner(lo, 3, 0) + corner(lo, 4, 0)))
    strip_diag_7 = strip_diagonal(node_row_7(left + right, sevens[3] + sevens[4]))
    strip_inv = jnp.where(strip_diag > 0.0, 1.0 / strip_diag, 0.0)
    strip_inv_7 = jnp.where(strip_diag_7 > 0.0, 1.0 / strip_diag_7, 0.0)
    slot = lax.rem(lane, SLOTS)
    strip_scale = jnp.where((slot == 2) | (slot == 6), 0.0, right)
    strip_base = [tiles[c] * strip_inv for c in range(3)]

    def strip_layers(modes):
        return [{m: lane_roll(modes[c][m], -SLOTS) for m in PLANE} for c in range(3)]

    lower = []
    for c in range(3):
        x, x_7 = strip_base[c], sevens[c] * strip_inv_7
        y, y_7 = lane_roll(x, -1), lane_roll(x_7, -1)
        lower.append(plane_modes(x, y, jnp.where(last_row, x_7, roll_up(x)), jnp.where(last_row, y_7, roll_up(y))))
    f_low, f_up = join_layers([strip_scale * x for x in stress(split_layers(lower, strip_layers(lower)))])
    strip_second, strip_sums = [], (0.0,) * 4
    for c in range(3):
        f = node_forces({m: f_low[c][m] + lane_roll(f_up[c][m], SLOTS) for m in PLANE}, 1)
        image = jnp.where(tiles[5] > 0.0, f, 0.0)
        s = jnp.where(tiles[5] > 0.0, f - tiles[c], 0.0)
        strip_second.append(s * strip_inv)
        strip_sums = products(strip_sums, strip_base[c], image, image * strip_inv, s, strip_second[c])
        edges[c] = strip_base[c]
        edges[3 + c] = strip_second[c]
    ends = [jnp.where(slot == 4, x, lane_roll(x, 4)) for x in strip_second]
    lower = [plane_modes(x, lane_roll(x, -1), roll_up(x), roll_up(lane_roll(x, -1))) for x in strip_second]
    m = split_layers(lower, strip_layers(lower))
    strip_e = strip_scale * inner(stress(m), m)

    def box(k):
        held[0, 0:rows, :] = table(element_rows(phase, k, layers), PHASE_STIFFNESS)
        held[0, 6:7, :] = hi[pl.ds(cn + k, 1), :]
        held[0, 7:8, :] = lo[pl.ds(cn + layers + k, 1), :]
        x = held[0]
        r = node_rows(x, spread(lo, cn + k))
        return x, r + jnp.where(lane == 0, lane_roll(edge_rows, -SLOTS * k), lane_roll(r, 1))

    def first_layer(k, around_node):
        inv = 1.0 / (KE_DIAGONAL * around_node)
        inverse[k] = inv
        out = []
        for c in range(3):
            q = c * nodes + k
            residual[q, 0:rows, :] = rhs[c][k]
            residual[q, 6:7, :] = hi[pl.ds(q, 1), :]
            residual[q, 7:8, :] = lo[pl.ds(q, 1), :]
            x = residual[q] * inv
            base[q] = x
            y = lane_roll(x, -1)
            x_up = jnp.where(last_row, spread(far_base.at[c], k), roll_up(x))
            y_up = jnp.where(last_row, spread(far_base.at[3 + c], k), roll_up(y))
            out.append(plane_modes(x, y, x_up, y_up))
        return out

    def finish_layer(k, f, totals):
        inv = inverse[k]
        held[1, 0:rows, :] = 1.0 - fixed[k].astype(jnp.float32)
        held[1, 6:7, :] = hi[pl.ds(2 * cn + 2 * layers + k, 1), :]
        free = held[1] > 0.0
        inv = jnp.where(free, inv, 1.0)
        a, rest = totals[0], totals[1:]
        for c in range(3):
            q = c * nodes + k
            r0 = residual[q]
            d0 = r0 * inv
            image = jnp.where(free, node_forces(f[c], 1), d0)
            s = image - r0
            v = s * inv
            ends_now = lane_roll(ends[c], LANES - 1 - (SLOTS * k + 4))
            second[q] = jnp.where((lane == 0) | (lane == LANES - 1), ends_now, v)
            a, rest = a + r0 * d0, products(rest, d0, image, image * inv, s, v)
        return (a,) + rest

    def flat(x):
        return tuple(x[c][m] for c in range(3) for m in PLANE)

    def unflat(x):
        return [{m: x[4 * c + i] for i, m in enumerate(PLANE)} for c in range(3)]

    zero = jnp.zeros((8, LANES), jnp.float32)
    held[1] = zero
    held[2] = zero

    def element(k, low_modes, high_modes, scale, pending, totals):
        g = stress(split_layers(low_modes, high_modes))
        f_lower, f_upper = join_layers([scale * x for x in g])
        done = [{m: pending[c][m] + f_lower[c][m] for m in PLANE} for c in range(3)]
        return f_upper, finish_layer(k, done, totals)

    def forward(k, carry):
        low_modes, pending, totals, scale, b = carry
        next_scale, next_b = box(k + 1)
        high = first_layer(k + 1, b + next_b)
        f_upper, totals = element(k, unflat(low_modes), high, scale, unflat(pending), totals)
        return flat(high), flat(f_upper), totals, next_scale, next_b

    scale, b = box(0)
    carry = (flat(first_layer(0, b)), (zero,) * 12, (zero,) * 5, scale, b)
    low_modes, pending, totals, scale, b = lax.fori_loop(0, layers - 1, forward, carry, unroll=True)
    high = first_layer(layers, b)
    f_upper, totals = element(layers - 1, unflat(low_modes), high, scale, unflat(pending), totals)
    totals = finish_layer(layers, f_upper, totals)

    def second_layer(k):
        out = []
        for c in range(3):
            x = second[c * nodes + k]
            y = lane_roll(x, -1)
            out.append(plane_modes(x, y, roll_up(x), roll_up(y)))
        return out

    def again(k, carry):
        low_modes, total = carry
        high = second_layer(k + 1)
        m = split_layers(unflat(low_modes), high)
        held[2, 0:rows, :] = table(element_rows(phase, k, layers), PHASE_STIFFNESS)
        return flat(high), total + held[2] * inner(stress(m), m)

    _, total = lax.fori_loop(0, layers, again, (flat(second_layer(0)), zero), unroll=True)
    mine = row < rows
    inside = mine & (lane > 0) & (lane < LANES - 1)
    at_ends = mine & ((slot == 1) | (slot == 4))
    totals = [jnp.where(mine, totals[0], 0.0)] + [
        jnp.where(inside, x, 0.0) + jnp.where(at_ends, y, 0.0) for x, y in zip(totals[1:], strip_sums)
    ]
    totals.append(
        jnp.where(mine & (lane < LANES - 1), total, 0.0) + jnp.where(mine & (slot == 4), strip_e, 0.0)
    )
    for i, x in enumerate(totals):
        x = jnp.sum(jnp.sum(x, axis=0, keepdims=True), axis=1, keepdims=True)
        sums[i : i + 1, :] = jnp.broadcast_to(x, (1, LANES))
    sums[6:, :] = jnp.zeros((2, LANES), jnp.float32)


def energy_kernel(base, second, edges, phase, energy):
    nodes = base.shape[0] // 3
    layers = nodes - 1
    rows = phase.shape[0] // layers
    lane = lanes()

    def layer(field, first_edge, k):
        out = []
        for c in range(3):
            fill = lane_roll(edges[first_edge + c], LANES - 1 - (SLOTS * k + 5))
            out.append(
                in_plane(
                    field[c * nodes + k],
                    lambda t: jnp.where(lane == LANES - 1, fill, lane_roll(t, -1)),
                    lambda t: pltpu.roll(t, 7, 0),
                )
            )
        return out

    low = layer(base, 0, 0), layer(second, 3, 0)
    for k in range(layers):
        high = layer(base, 0, k + 1), layer(second, 3, k + 1)
        m, n = split_layers(low[0], high[0]), split_layers(low[1], high[1])
        g, h = stress(m), stress(n)
        slope = -table(element_rows(phase, k, layers), PHASE_SLOPE)
        for which, value in enumerate((inner(g, m), inner(h, m), inner(h, n))):
            energy[which, pl.ds(k, rows, stride=layers), :] = slope * value[0:rows]
        low = high


def combine_kernel(base, second, energy, sums, displacement, sensitivity):
    a, curve, plain, shifted, cross, bend = (sums[i : i + 1, :] for i in range(6))
    slope = curve / a
    alpha = a / curve
    less = 1.0 - slope
    rest = jnp.where(slope < 0.5, plain - slope * curve, shifted - less * less * a)
    bend = bend + 2.0 * less * cross + less * less * curve
    alpha_next = rest / (bend - rest * rest / curve)
    beta = alpha * alpha * rest / a
    first = alpha + alpha_next * beta - alpha * alpha_next * less
    other = -alpha * alpha_next
    comps, nodes, rows, width = displacement.shape
    for c in range(comps):
        for k in range(nodes):
            q = c * nodes + k
            displacement[c, k] = (first * base[q] + other * second[q])[0:rows]
    sensitivity[...] = (first * first) * energy[0] + (2.0 * first * other) * energy[1] + (other * other) * energy[2]


def exchange(one, two, axis):
    count = lax.axis_size(axis)
    if count % 2 == 0:
        far = lax.ppermute(two, axis, [(i, (i - 1) % count if i % 2 == 0 else (i + 1) % count) for i in range(count)])
        near = lax.ppermute(one, axis, [(i, i ^ 1) for i in range(count)])
        return near, far
    high = lax.ppermute(one, axis, [((i + 1) % count, i) for i in range(count)])
    low = lax.ppermute(two, axis, [(i, (i + 1) % count) for i in range(count)])
    return high, low


def total_over(x, axis, order):
    count = lax.axis_size(axis)
    if count & (count - 1):
        return lax.psum(x, axis)
    step = 1
    while step < count:
        width = 4 if count // step >= 4 else 2
        group = [
            lax.ppermute(x, axis, [(i, i ^ (step * by)) for i in range(count)]) for by in order if by < width
        ]
        x = functools.reduce(jnp.add, group, x)
        step *= width
    return x


def body(force, phase, fixed):
    comps, nodes, rows, width = force.shape
    layers = nodes - 1
    phase = phase.transpose(1, 0, 2).reshape(rows * layers, width)
    rhs = [(1 - fixed).astype(jnp.float32) * force[c] for c in range(comps)]
    f32 = jnp.float32
    paired_x = lax.axis_size("gx") % 2 == 0
    paired_y = lax.axis_size("gy") % 2 == 0
    column = jax.ShapeDtypeStruct((2, 8, LANES), f32)
    message = jax.ShapeDtypeStruct((FULL, LANES), f32)

    def call(kernel, out_shape, scratch=()):
        return pl.pallas_call(
            kernel,
            out_shape=out_shape,
            scratch_shapes=scratch,
            compiler_params=PARAMS,
        )

    strips = jax.ShapeDtypeStruct((6, 8, LANES), f32)
    own, col1, col2 = call(
        functools.partial(column_kernel, paired_y),
        (jax.ShapeDtypeStruct((5, 8, LANES), f32), column, column),
        [pltpu.VMEM((5 * nodes, 8, LANES), f32)],
    )(*rhs, phase, fixed)
    row1, row2 = call(functools.partial(row_kernel, paired_x), (message, message))(*rhs, phase, fixed)
    near, far = exchange(col1, col2, "gy")
    strip, row1, row2 = call(
        functools.partial(strip_kernel, nodes, paired_x, paired_y),
        (strips, message, message),
    )(own, near, far, row1, row2)
    near, far = exchange(row1, row2, "gx")
    field = jax.ShapeDtypeStruct((comps * nodes, 8, LANES), f32)
    base, second, edges, sums = call(
        functools.partial(operator_kernel, paired_x),
        (
            field,
            field,
            strips,
            jax.ShapeDtypeStruct((8, LANES), f32),
        ),
        [
            pltpu.VMEM((FULL, LANES), f32),
            pltpu.VMEM((FULL, LANES), f32),
            pltpu.VMEM((3, 8, LANES), f32),
            pltpu.VMEM((comps * nodes, 8, LANES), f32),
            pltpu.VMEM((nodes, 8, LANES), f32),
            pltpu.VMEM((32, LANES), f32),
            pltpu.VMEM((6, 24, LANES), f32),
        ],
    )(*rhs, phase, fixed, strip, near, far)
    energy = call(energy_kernel, jax.ShapeDtypeStruct((3,) + phase.shape, f32))(base, second, edges, phase)
    sums = total_over(total_over(sums, "gy", (1, 2, 3)), "gx", (1, 2, 3))
    displacement, sensitivity = call(
        combine_kernel,
        (jax.ShapeDtypeStruct(force.shape, f32), jax.ShapeDtypeStruct(phase.shape, f32)),
    )(base, second, energy, sums)
    return displacement, sensitivity.reshape(rows, layers, width).transpose(1, 0, 2)


def solution(mesh):
    return jax.shard_map(
        body,
        mesh=mesh,
        in_specs=(
            P(None, None, ("parts", "gx"), "gy"),
            P(None, ("parts", "gx"), "gy"),
            P(None, ("parts", "gx"), "gy"),
        ),
        out_specs=(P(None, None, ("parts", "gx"), "gy"), P(None, ("parts", "gx"), "gy")),
        check_vma=False,
    )
```

```python
import functools

import jax
import jax.numpy as jnp
import numpy as np
from jax import lax
from jax.experimental import pallas as pl
from jax.experimental.pallas import tpu as pltpu
from jax.sharding import PartitionSpec as P

PHASE_STIFFNESS = (0.125, 0.343, 0.614, 1.0)
PHASE_SLOPE = (0.75, 1.47, 2.17, 3.0)
POISSON = 0.3
LAME = POISSON / ((1.0 + POISSON) * (1.0 - 2.0 * POISSON))
SHEAR = 1.0 / (2.0 * (1.0 + POISSON))
KE_DIAGONAL = (LAME + 4.0 * SHEAR) / 9.0

SLOTS = 7
LANES = 128
DOWN, DOWN_CORNERS = 168, 152
UP, UP_CORNERS = 168, 83

VMEM = pl.BlockSpec(memory_space=pltpu.VMEM)
PARAMS = pltpu.CompilerParams(vmem_limit_bytes=32 * 1024 * 1024)


def lanes():
    return lax.broadcasted_iota(jnp.int32, (8, LANES), 1)


def sublanes():
    return lax.broadcasted_iota(jnp.int32, (8, LANES), 0)


def table(phase, values):
    out = jnp.full(phase.shape, values[3], jnp.float32)
    for index in (2, 1, 0):
        out = jnp.where(phase == index, jnp.float32(values[index]), out)
    return out


def element_rows(ref, k, layers):
    return ref[pl.ds(k, ref.shape[0] // layers, stride=layers), :]


def lane_roll(x, by):
    if isinstance(by, int):
        by = by % LANES
        return x if by == 0 else pltpu.roll(x, by, 1)
    return pltpu.roll(x, lax.rem(by + LANES, LANES), 1)


def is_even(axis):
    return lax.rem(lax.axis_index(axis), 2) == 0


def gather(nodes, *items):
    lane = lanes()
    slot = jnp.where(lane < nodes * SLOTS, lax.rem(lane, SLOTS), SLOTS)
    out = jnp.zeros((8, LANES), jnp.float32)
    for plane, by, first, count in items:
        out = jnp.where((slot >= first) & (slot < first + count), lane_roll(plane, by), out)
    return out


def column_kernel(paired, rhs_0, rhs_1, rhs_2, phase, fixed, own, col1, col2, pad):
    rhs = (rhs_0, rhs_1, rhs_2)
    nodes, rows, width = rhs_0.shape
    layers = nodes - 1
    lane = lanes()
    even = is_even("gy") if paired else True
    pad[...] = jnp.zeros(pad.shape, jnp.float32)
    planes = [jnp.zeros((8, LANES), jnp.float32)] * 5
    for k in range(nodes):
        here = (lane >= k * SLOTS) & (lane < k * SLOTS + 5)
        values = [rhs[c][k] for c in range(3)]
        values.append(table(element_rows(phase, k, layers), PHASE_STIFFNESS) if k < layers else None)
        values.append((1 - fixed[k]).astype(jnp.float32))
        for p, value in enumerate(values):
            if value is not None:
                pad[5 * k + p, 0:rows, :] = value
                planes[p] = jnp.where(here, lane_roll(pad[5 * k + p], k * SLOTS + 3), planes[p])
    for p in range(5):
        own[p] = planes[p]
    high = [
        gather(nodes, (planes[0], -2, 0, 1), (planes[1], -1, 1, 1), (planes[2], 0, 2, 1), (planes[3], 2, 3, 2)),
        jnp.zeros((8, LANES), jnp.float32),
    ]
    low = [
        gather(nodes, (planes[0], -3, 0, 2), (planes[1], -1, 2, 2), (planes[2], 1, 4, 2), (planes[4], 3, 6, 1)),
        planes[3],
    ]
    for p in range(2):
        if paired:
            col1[p] = jnp.where(even, high[p], low[p])
            col2[p] = jnp.where(even, low[p], high[p])
        else:
            col1[p] = low[p]
            col2[p] = high[p]


def row_kernel(rhs_0, rhs_1, rhs_2, phase, fixed, down, up):
    rhs = (rhs_0, rhs_1, rhs_2)
    nodes, rows, width = rhs_0.shape
    layers, cn = nodes - 1, 3 * nodes
    for k in range(nodes):
        for c in range(3):
            q = c * nodes + k
            down[q : q + 1, :] = rhs[c][k, 0:1]
            down[cn + 2 * layers + q : cn + 2 * layers + q + 1, :] = rhs[c][k, 1:2]
            up[q : q + 1, :] = rhs[c][k, rows - 1 : rows]
        at = 2 * cn + 2 * layers + k
        down[at : at + 1, :] = (1 - fixed[k, 0:1]).astype(jnp.float32)
    for i in range(2):
        at = cn + i * layers
        down[at : at + layers, :] = table(phase[i * layers : (i + 1) * layers], PHASE_STIFFNESS)
        first = (rows - 2 + i) * layers
        up[at : at + layers, :] = table(phase[first : first + layers], PHASE_STIFFNESS)
    down[2 * cn + 2 * layers + nodes :, :] = jnp.zeros((DOWN - 2 * cn - 2 * layers - nodes, LANES), jnp.float32)
    up[cn + 2 * layers :, :] = jnp.zeros((UP - cn - 2 * layers, LANES), jnp.float32)


def strip_kernel(nodes, paired, own, got2, got1, down, up, strip, down_out, up_out):
    even_y = is_even("gy") if paired else True
    if paired:
        from_low = jnp.where(even_y, got2[0], got1[0])
        from_high = [jnp.where(even_y, got1[p], got2[p]) for p in range(2)]
    else:
        from_low, from_high = got2[0], [got1[p] for p in range(2)]
    planes = [
        gather(nodes, (from_low, -c, 0, 1), (own[c], -2, 1, 2), (own[c], 2, 3, 2), (from_high[0], 5 - 2 * c, 5, 2))
        for c in range(3)
    ]
    scale = own[3]
    planes.append(gather(nodes, (from_low, -3, 0, 2), (scale, -1, 2, 1), (scale, 3, 3, 3), (from_high[1], 3, 6, 1)))
    planes.append(gather(nodes, (from_low, -4, 0, 1), (scale, -2, 1, 2), (scale, 2, 3, 2), (from_high[1], 2, 5, 2)))
    planes.append(gather(nodes, (own[4], -2, 1, 1), (own[4], 2, 4, 1), (from_high[0], -1, 5, 1)))
    rows = 6
    down_out[...] = down[...]
    up_out[...] = up[...]
    for p, plane in enumerate(planes):
        strip[p] = plane
        down_out[DOWN_CORNERS + 2 * p : DOWN_CORNERS + 2 * p + 2, :] = plane[0:2]
        up_out[UP_CORNERS + 2 * p : UP_CORNERS + 2 * p + 2, :] = plane[rows - 2 : rows]


PLANE = ("", "1", "2", "12")


def split_layers(lo, hi):
    sums = [{m: lo[c][m] + hi[c][m] for m in ("1", "2", "12")} for c in range(3)]
    diffs = [{m: hi[c][m] - lo[c][m] for m in PLANE} for c in range(3)]
    u, v, w = range(3)
    return (
        diffs[u][""], sums[v]["1"], sums[w]["2"],
        sums[u]["1"] + diffs[v][""], sums[u]["2"] + diffs[w][""], sums[v]["2"] + sums[w]["1"],
        diffs[u]["1"], sums[w]["12"], diffs[u]["2"], sums[v]["12"], diffs[v]["1"], diffs[w]["2"],
        sums[u]["12"], diffs[v]["2"], diffs[w]["1"],
        diffs[u]["12"], diffs[v]["12"], diffs[w]["12"],
    )


def stress(m):
    one, two, three = 1.0 / 16.0, 1.0 / 48.0, 1.0 / 144.0
    trace = (LAME * one) * (m[0] + m[1] + m[2])
    out = [trace + (2.0 * SHEAR * one) * m[i] for i in range(3)]
    out += [(SHEAR * one) * m[i] for i in (3, 4, 5)]
    own, other = (LAME + 3.0 * SHEAR) * two, LAME * two
    for i in (6, 8, 10):
        out += [own * m[i] + other * m[i + 1], own * m[i + 1] + other * m[i]]
    total = m[12] + m[13] + m[14]
    out += [(SHEAR * two) * (m[i] + total) for i in (12, 13, 14)]
    out += [((LAME + 4.0 * SHEAR) * three) * m[i] for i in (15, 16, 17)]
    return out


def inner(g, m):
    parts = [g[i] * m[i] for i in range(18)]
    while len(parts) > 1:
        parts = [parts[i] + parts[i + 1] if i + 1 < len(parts) else parts[i] for i in range(0, len(parts), 2)]
    return parts[0]


def join_layers(g):
    sums = [
        {"1": g[3], "2": g[4], "12": g[12]},
        {"1": g[1], "2": g[5], "12": g[9]},
        {"1": g[5], "2": g[2], "12": g[7]},
    ]
    diffs = [
        {"": g[0], "1": g[6], "2": g[8], "12": g[15]},
        {"": g[3], "1": g[10], "2": g[13], "12": g[16]},
        {"": g[4], "1": g[14], "2": g[11], "12": g[17]},
    ]
    lower = [{m: (sums[c][m] - diffs[c][m] if m else -diffs[c][m]) for m in PLANE} for c in range(3)]
    upper = [{m: (sums[c][m] + diffs[c][m] if m else diffs[c][m]) for m in PLANE} for c in range(3)]
    return lower, upper


def in_plane(x, right, up):
    y = right(x)
    near, far = x + y, y - x
    near_up, far_up = up(near), up(far)
    return {"": near + near_up, "1": near_up - near, "2": far + far_up, "12": far_up - far}


def out_of_plane(f, right, up):
    plain = (f[""] - f["2"]) + right(f[""] + f["2"])
    steep = (f["1"] - f["12"]) + right(f["1"] + f["12"])
    return (plain - steep) + up(plain + steep)


def operator_kernel(
    rhs_0, rhs_1, rhs_2, phase, fixed, strip, lo, hi,
    base, second, edges, sums,
    held, residual, inverse, dense, far_base,
):
    rhs, comps = (rhs_0, rhs_1, rhs_2), 3
    nodes, rows, width = rhs_0.shape
    layers = nodes - 1
    lane, row = lanes(), sublanes()
    last_row, below = row == 6, row == 7
    cn = comps * nodes
    def spread(ref, at):
        return jnp.broadcast_to(ref[pl.ds(at, 1), :], (8, LANES))

    def roll_up(x):
        return pltpu.roll(x, 7, 0)

    def roll_down(x):
        return pltpu.roll(x, 1, 0)

    def node_rows(x, x_m2):
        return x + jnp.where(below, x_m2, roll_down(x))

    def node_row_7(x, x_7):
        return jnp.broadcast_to(x[6:7], (8, LANES)) + x_7

    def plane_modes(x, y, x_up, y_up):
        near, far, near_up, far_up = x + y, y - x, x_up + y_up, y_up - x_up
        return {"": near + near_up, "1": near_up - near, "2": far + far_up, "12": far_up - far}

    def node_forces(f, by):
        sides = []
        for sign in (-1, 1):
            plain = f[""] + f["2"] if sign > 0 else f[""] - f["2"]
            steep = f["1"] + f["12"] if sign > 0 else f["1"] - f["12"]
            sides.append((plain - steep) + roll_down(plain + steep))
        return sides[0] + lane_roll(sides[1], by)

    def products(totals, d0, image, z, s, v):
        return tuple(t + x for t, x in zip(totals, (d0 * image, image * z, s * v, v * image)))

    def corner(ref, p, which):
        return spread(ref, (UP_CORNERS if ref is lo else DOWN_CORNERS) + 2 * p + which)

    tiles = [
        jnp.where(row < 6, strip[p], jnp.where(last_row, corner(hi, p, 0), corner(lo, p, 1))) for p in range(6)
    ]
    sevens = [corner(hi, p, 1) for p in range(5)]
    left, right = tiles[3], tiles[4]
    edge_rows = node_rows(right, corner(lo, 4, 0))
    edge_rows_7 = node_row_7(right, sevens[4])

    tall = lax.broadcasted_iota(jnp.int32, (layers, LANES), 0)
    wide = lax.broadcasted_iota(jnp.int32, (layers, LANES), 1)
    pair = hi[cn : cn + layers, :] + hi[cn + layers : cn + 2 * layers, :]
    edge = jnp.broadcast_to(edge_rows_7[0:1], (layers, LANES))
    edge = jnp.sum(jnp.where(wide == SLOTS * tall, edge, 0.0), axis=1, keepdims=True)
    dense[...] = jnp.zeros(dense.shape, jnp.float32)
    dense[1 : layers + 1, :] = pair + jnp.where(wide == 0, edge, pltpu.roll(pair, 1, 1))
    inv_7 = dense[0:24, :] + dense[1:25, :]
    inv_7 = jnp.where(inv_7 > 0.0, 1.0 / (KE_DIAGONAL * inv_7), 0.0)
    for c in range(3):
        x_7 = hi[cn + 2 * layers + c * nodes : cn + 2 * layers + c * nodes + 24, :] * inv_7
        far_base[c] = x_7
        far_base[3 + c] = pltpu.roll(x_7, LANES - 1, 1)

    def strip_diagonal(x):
        return KE_DIAGONAL * (x + lane_roll(x, SLOTS))

    strip_diag = strip_diagonal(node_rows(left + right, corner(lo, 3, 0) + corner(lo, 4, 0)))
    strip_diag_7 = strip_diagonal(node_row_7(left + right, sevens[3] + sevens[4]))
    strip_inv = jnp.where(strip_diag > 0.0, 1.0 / strip_diag, 0.0)
    strip_inv_7 = jnp.where(strip_diag_7 > 0.0, 1.0 / strip_diag_7, 0.0)
    slot = lax.rem(lane, SLOTS)
    strip_scale = jnp.where((slot == 2) | (slot == 6), 0.0, right)
    strip_base = [tiles[c] * strip_inv for c in range(3)]

    def strip_layers(modes):
        return [{m: lane_roll(modes[c][m], -SLOTS) for m in PLANE} for c in range(3)]

    lower = []
    for c in range(3):
        x, x_7 = strip_base[c], sevens[c] * strip_inv_7
        y, y_7 = lane_roll(x, -1), lane_roll(x_7, -1)
        lower.append(plane_modes(x, y, jnp.where(last_row, x_7, roll_up(x)), jnp.where(last_row, y_7, roll_up(y))))
    f_low, f_up = join_layers([strip_scale * x for x in stress(split_layers(lower, strip_layers(lower)))])
    strip_second, strip_sums = [], (0.0,) * 4
    for c in range(3):
        f = node_forces({m: f_low[c][m] + lane_roll(f_up[c][m], SLOTS) for m in PLANE}, 1)
        image = jnp.where(tiles[5] > 0.0, f, 0.0)
        s = jnp.where(tiles[5] > 0.0, f - tiles[c], 0.0)
        strip_second.append(s * strip_inv)
        strip_sums = products(strip_sums, strip_base[c], image, image * strip_inv, s, strip_second[c])
        edges[c] = strip_base[c]
        edges[3 + c] = strip_second[c]
    ends = [jnp.where(slot == 4, x, lane_roll(x, 4)) for x in strip_second]
    lower = [plane_modes(x, lane_roll(x, -1), roll_up(x), roll_up(lane_roll(x, -1))) for x in strip_second]
    m = split_layers(lower, strip_layers(lower))
    strip_e = strip_scale * inner(stress(m), m)

    def box(k):
        held[0, 0:rows, :] = table(element_rows(phase, k, layers), PHASE_STIFFNESS)
        held[0, 6:7, :] = hi[pl.ds(cn + k, 1), :]
        held[0, 7:8, :] = lo[pl.ds(cn + layers + k, 1), :]
        x = held[0]
        r = node_rows(x, spread(lo, cn + k))
        return x, r + jnp.where(lane == 0, lane_roll(edge_rows, -SLOTS * k), lane_roll(r, 1))

    def first_layer(k, around_node):
        inv = 1.0 / (KE_DIAGONAL * around_node)
        inverse[k] = inv
        out = []
        for c in range(3):
            q = c * nodes + k
            residual[q, 0:rows, :] = rhs[c][k]
            residual[q, 6:7, :] = hi[pl.ds(q, 1), :]
            residual[q, 7:8, :] = lo[pl.ds(q, 1), :]
            x = residual[q] * inv
            base[q] = x
            y = lane_roll(x, -1)
            x_up = jnp.where(last_row, spread(far_base.at[c], k), roll_up(x))
            y_up = jnp.where(last_row, spread(far_base.at[3 + c], k), roll_up(y))
            out.append(plane_modes(x, y, x_up, y_up))
        return out

    def finish_layer(k, f, totals):
        inv = inverse[k]
        held[1, 0:rows, :] = 1.0 - fixed[k].astype(jnp.float32)
        held[1, 6:7, :] = hi[pl.ds(2 * cn + 2 * layers + k, 1), :]
        free = held[1] > 0.0
        inv = jnp.where(free, inv, 1.0)
        a, rest = totals[0], totals[1:]
        for c in range(3):
            q = c * nodes + k
            r0 = residual[q]
            d0 = r0 * inv
            image = jnp.where(free, node_forces(f[c], 1), d0)
            s = image - r0
            v = s * inv
            ends_now = lane_roll(ends[c], LANES - 1 - (SLOTS * k + 4))
            second[q] = jnp.where((lane == 0) | (lane == LANES - 1), ends_now, v)
            a, rest = a + r0 * d0, products(rest, d0, image, image * inv, s, v)
        return (a,) + rest

    def flat(x):
        return tuple(x[c][m] for c in range(3) for m in PLANE)

    def unflat(x):
        return [{m: x[4 * c + i] for i, m in enumerate(PLANE)} for c in range(3)]

    zero = jnp.zeros((8, LANES), jnp.float32)
    held[1] = zero
    held[2] = zero

    def element(k, low_modes, high_modes, scale, pending, totals):
        g = stress(split_layers(low_modes, high_modes))
        f_lower, f_upper = join_layers([scale * x for x in g])
        done = [{m: pending[c][m] + f_lower[c][m] for m in PLANE} for c in range(3)]
        return f_upper, finish_layer(k, done, totals)

    def forward(k, carry):
        low_modes, pending, totals, scale, b = carry
        next_scale, next_b = box(k + 1)
        high = first_layer(k + 1, b + next_b)
        f_upper, totals = element(k, unflat(low_modes), high, scale, unflat(pending), totals)
        return flat(high), flat(f_upper), totals, next_scale, next_b

    scale, b = box(0)
    carry = (flat(first_layer(0, b)), (zero,) * 12, (zero,) * 5, scale, b)
    low_modes, pending, totals, scale, b = lax.fori_loop(0, layers - 1, forward, carry, unroll=True)
    high = first_layer(layers, b)
    f_upper, totals = element(layers - 1, unflat(low_modes), high, scale, unflat(pending), totals)
    totals = finish_layer(layers, f_upper, totals)

    def second_layer(k):
        out = []
        for c in range(3):
            x = second[c * nodes + k]
            y = lane_roll(x, -1)
            out.append(plane_modes(x, y, roll_up(x), roll_up(y)))
        return out

    def again(k, carry):
        low_modes, total = carry
        high = second_layer(k + 1)
        m = split_layers(unflat(low_modes), high)
        held[2, 0:rows, :] = table(element_rows(phase, k, layers), PHASE_STIFFNESS)
        return flat(high), total + held[2] * inner(stress(m), m)

    _, total = lax.fori_loop(0, layers, again, (flat(second_layer(0)), zero), unroll=True)
    mine = row < rows
    inside = mine & (lane > 0) & (lane < LANES - 1)
    at_ends = mine & ((slot == 1) | (slot == 4))
    totals = [jnp.where(mine, totals[0], 0.0)] + [
        jnp.where(inside, x, 0.0) + jnp.where(at_ends, y, 0.0) for x, y in zip(totals[1:], strip_sums)
    ]
    totals.append(
        jnp.where(mine & (lane < LANES - 1), total, 0.0) + jnp.where(mine & (slot == 4), strip_e, 0.0)
    )
    for i, x in enumerate(totals):
        x = jnp.sum(jnp.sum(x, axis=0, keepdims=True), axis=1, keepdims=True)
        sums[i : i + 1, :] = jnp.broadcast_to(x, (1, LANES))
    sums[6:, :] = jnp.zeros((2, LANES), jnp.float32)


def energy_kernel(base, second, edges, phase, energy):
    nodes = base.shape[0] // 3
    layers = nodes - 1
    rows = phase.shape[0] // layers
    lane = lanes()

    def layer(field, first_edge, k):
        out = []
        for c in range(3):
            fill = lane_roll(edges[first_edge + c], LANES - 1 - (SLOTS * k + 5))
            out.append(
                in_plane(
                    field[c * nodes + k],
                    lambda t: jnp.where(lane == LANES - 1, fill, lane_roll(t, -1)),
                    lambda t: pltpu.roll(t, 7, 0),
                )
            )
        return out

    low = layer(base, 0, 0), layer(second, 3, 0)
    for k in range(layers):
        high = layer(base, 0, k + 1), layer(second, 3, k + 1)
        m, n = split_layers(low[0], high[0]), split_layers(low[1], high[1])
        g, h = stress(m), stress(n)
        slope = -table(element_rows(phase, k, layers), PHASE_SLOPE)
        for which, value in enumerate((inner(g, m), inner(h, m), inner(h, n))):
            energy[which, pl.ds(k, rows, stride=layers), :] = slope * value[0:rows]
        low = high


def combine_kernel(base, second, energy, sums, displacement, sensitivity):
    a, curve, plain, shifted, cross, bend = (sums[i : i + 1, :] for i in range(6))
    slope = curve / a
    alpha = a / curve
    less = 1.0 - slope
    rest = jnp.where(slope < 0.5, plain - slope * curve, shifted - less * less * a)
    bend = bend + 2.0 * less * cross + less * less * curve
    alpha_next = rest / (bend - rest * rest / curve)
    beta = alpha * alpha * rest / a
    first = alpha + alpha_next * beta - alpha * alpha_next * less
    other = -alpha * alpha_next
    comps, nodes, rows, width = displacement.shape
    for c in range(comps):
        for k in range(nodes):
            q = c * nodes + k
            displacement[c, k] = (first * base[q] + other * second[q])[0:rows]
    sensitivity[...] = (first * first) * energy[0] + (2.0 * first * other) * energy[1] + (other * other) * energy[2]


def exchange_pairs(one, two, axis):
    count = lax.axis_size(axis)
    far = lax.ppermute(two, axis, [(i, (i - 1) % count if i % 2 == 0 else (i + 1) % count) for i in range(count)])
    near = lax.ppermute(one, axis, [(i, i ^ 1) for i in range(count)])
    return near, far


def exchange(down, up, axis):
    count = lax.axis_size(axis)
    low = lax.ppermute(up, axis, [(i, (i + 1) % count) for i in range(count)])
    high = lax.ppermute(down, axis, [((i + 1) % count, i) for i in range(count)])
    return high, low


def total_over(x, axis):
    count = lax.axis_size(axis)
    if count & (count - 1):
        return lax.psum(x, axis)
    step = 1
    while step < count:
        width = 4 if count // step >= 4 else 2
        if axis == "gx" and count == 4:
            to = [[(i, (i + by) % 4) for i in range(4)] for by in (3, 2, 1)]
        else:
            to = [[(i, i ^ (step * by)) for i in range(count)] for by in range(1, width)]
        x = functools.reduce(jnp.add, [lax.ppermute(x, axis, pairs) for pairs in to], x)
        step *= width
    return x


def body(force, phase, fixed):
    comps, nodes, rows, width = force.shape
    layers = nodes - 1
    phase = phase.transpose(1, 0, 2).reshape(rows * layers, width)
    rhs = [(1 - fixed).astype(jnp.float32) * force[c] for c in range(comps)]
    f32 = jnp.float32
    paired = lax.axis_size("gy") % 2 == 0
    column = jax.ShapeDtypeStruct((2, 8, LANES), f32)
    messages = (jax.ShapeDtypeStruct((DOWN, LANES), f32), jax.ShapeDtypeStruct((UP, LANES), f32))
    strips = jax.ShapeDtypeStruct((6, 8, LANES), f32)

    def call(kernel, out_shape, scratch=()):
        return pl.pallas_call(kernel, out_shape=out_shape, scratch_shapes=scratch, compiler_params=PARAMS)

    own, col1, col2 = call(
        functools.partial(column_kernel, paired),
        (jax.ShapeDtypeStruct((5, 8, LANES), f32), column, column),
        [pltpu.VMEM((5 * nodes, 8, LANES), f32)],
    )(*rhs, phase, fixed)
    down, up = call(row_kernel, messages)(*rhs, phase, fixed)
    near, far = (exchange_pairs if paired else exchange)(col1, col2, "gy")
    strip, down, up = call(
        functools.partial(strip_kernel, nodes, paired),
        (strips,) + messages,
    )(own, far, near, down, up)
    high, low = exchange(down, up, "gx")
    field = jax.ShapeDtypeStruct((comps * nodes, 8, LANES), f32)
    base, second, edges, sums = call(
        operator_kernel,
        (
            field,
            field,
            strips,
            jax.ShapeDtypeStruct((8, LANES), f32),
        ),
        [
            pltpu.VMEM((3, 8, LANES), f32),
            pltpu.VMEM((comps * nodes, 8, LANES), f32),
            pltpu.VMEM((nodes, 8, LANES), f32),
            pltpu.VMEM((32, LANES), f32),
            pltpu.VMEM((6, 24, LANES), f32),
        ],
    )(*rhs, phase, fixed, strip, low, high)
    energy = call(energy_kernel, jax.ShapeDtypeStruct((3,) + phase.shape, f32))(base, second, edges, phase)
    sums = total_over(total_over(sums, "gx"), "gy")
    displacement, sensitivity = call(
        combine_kernel,
        (jax.ShapeDtypeStruct(force.shape, f32), jax.ShapeDtypeStruct(phase.shape, f32)),
    )(base, second, energy, sums)
    return displacement, sensitivity.reshape(rows, layers, width).transpose(1, 0, 2)


def solution(mesh):
    return jax.shard_map(
        body,
        mesh=mesh,
        in_specs=(
            P(None, None, ("parts", "gx"), "gy"),
            P(None, ("parts", "gx"), "gy"),
            P(None, ("parts", "gx"), "gy"),
        ),
        out_specs=(P(None, None, ("parts", "gx"), "gy"), P(None, ("parts", "gx"), "gy")),
        check_vma=False,
    )
```

```python
import functools

import jax
import jax.numpy as jnp
import numpy as np
from jax import lax
from jax.experimental import pallas as pl
from jax.experimental.pallas import tpu as pltpu
from jax.sharding import PartitionSpec as P

PHASE_STIFFNESS = (0.125, 0.343, 0.614, 1.0)
PHASE_SLOPE = (0.75, 1.47, 2.17, 3.0)
POISSON = 0.3
LAME = POISSON / ((1.0 + POISSON) * (1.0 - 2.0 * POISSON))
SHEAR = 1.0 / (2.0 * (1.0 + POISSON))
KE_DIAGONAL = (LAME + 4.0 * SHEAR) / 9.0

SLOTS = 7
LANES = 128
DOWN, DOWN_CORNERS = 144, 135
UP, UP_CORNERS = 144, 83

VMEM = pl.BlockSpec(memory_space=pltpu.VMEM)
PARAMS = pltpu.CompilerParams(vmem_limit_bytes=32 * 1024 * 1024)


def lanes():
    return lax.broadcasted_iota(jnp.int32, (8, LANES), 1)


def sublanes():
    return lax.broadcasted_iota(jnp.int32, (8, LANES), 0)


def table(phase, values):
    out = jnp.full(phase.shape, values[3], jnp.float32)
    for index in (2, 1, 0):
        out = jnp.where(phase == index, jnp.float32(values[index]), out)
    return out


def element_rows(ref, k, layers):
    return ref[pl.ds(k, ref.shape[0] // layers, stride=layers), :]


def lane_roll(x, by):
    if isinstance(by, int):
        by = by % LANES
        return x if by == 0 else pltpu.roll(x, by, 1)
    return pltpu.roll(x, lax.rem(by + LANES, LANES), 1)


def is_even(axis):
    return lax.rem(lax.axis_index(axis), 2) == 0


def gather(nodes, *items):
    lane = lanes()
    slot = jnp.where(lane < nodes * SLOTS, lax.rem(lane, SLOTS), SLOTS)
    out = jnp.zeros((8, LANES), jnp.float32)
    for plane, by, first, count in items:
        out = jnp.where((slot >= first) & (slot < first + count), lane_roll(plane, by), out)
    return out


def column_kernel(paired, rhs_0, rhs_1, rhs_2, phase, fixed, own, col1, col2, pad):
    rhs = (rhs_0, rhs_1, rhs_2)
    nodes, rows, width = rhs_0.shape
    layers = nodes - 1
    lane = lax.broadcasted_iota(jnp.int32, (rows, LANES), 1)
    even = is_even("gy") if paired else True
    pad[...] = jnp.zeros(pad.shape, jnp.float32)
    planes = [jnp.zeros((rows, LANES), jnp.float32)] * 5
    for k in range(nodes):
        here = (lane >= k * SLOTS) & (lane < k * SLOTS + 5)
        values = [rhs[c][k] for c in range(3)]
        values.append(table(element_rows(phase, k, layers), PHASE_STIFFNESS) if k < layers else None)
        values.append((1 - fixed[k]).astype(jnp.float32))
        for p, value in enumerate(values):
            if value is not None:
                planes[p] = jnp.where(here, lane_roll(value, k * SLOTS + 3), planes[p])
    for p in range(5):
        pad[p, 0:rows, :] = planes[p]
        planes[p] = pad[p]
        own[p] = planes[p]
    high = [
        gather(nodes, (planes[0], -2, 0, 1), (planes[1], -1, 1, 1), (planes[2], 0, 2, 1), (planes[3], 2, 3, 2)),
        jnp.zeros((8, LANES), jnp.float32),
    ]
    low = [
        gather(nodes, (planes[0], -3, 0, 2), (planes[1], -1, 2, 2), (planes[2], 1, 4, 2), (planes[4], 3, 6, 1)),
        planes[3],
    ]
    for p in range(2):
        if paired:
            col1[p] = jnp.where(even, high[p], low[p])
            col2[p] = jnp.where(even, low[p], high[p])
        else:
            col1[p] = low[p]
            col2[p] = high[p]


def row_kernel(rhs_0, rhs_1, rhs_2, phase, fixed, down, up, pair):
    rhs = (rhs_0, rhs_1, rhs_2)
    nodes, rows, width = rhs_0.shape
    layers, cn = nodes - 1, 3 * nodes
    for k in range(nodes):
        for c in range(3):
            q = c * nodes + k
            down[q : q + 1, :] = rhs[c][k, 0:1]
            down[cn + layers + nodes + q : cn + layers + nodes + q + 1, :] = rhs[c][k, 1:2]
            up[q : q + 1, :] = rhs[c][k, rows - 1 : rows]
        at = cn + layers + k
        down[at : at + 1, :] = (1 - fixed[k, 0:1]).astype(jnp.float32)
    scale = [table(phase[i * layers : (i + 1) * layers], PHASE_STIFFNESS) for i in (0, 1, rows - 2, rows - 1)]
    down[cn : cn + layers, :] = scale[0]
    up[cn : cn + layers, :] = scale[2]
    up[cn + layers : cn + 2 * layers, :] = scale[3]
    pair[...] = scale[0] + scale[1]
    down[DOWN_CORNERS:, :] = jnp.zeros((DOWN - DOWN_CORNERS, LANES), jnp.float32)
    up[UP_CORNERS:, :] = jnp.zeros((UP - UP_CORNERS, LANES), jnp.float32)


def strip_kernel(nodes, paired, own, got2, got1, down, up, pair, strip, down_out, up_out, dense):
    even_y = is_even("gy") if paired else True
    if paired:
        from_low = jnp.where(even_y, got2[0], got1[0])
        from_high = [jnp.where(even_y, got1[p], got2[p]) for p in range(2)]
    else:
        from_low, from_high = got2[0], [got1[p] for p in range(2)]
    planes = [
        gather(nodes, (from_low, -c, 0, 1), (own[c], -2, 1, 2), (own[c], 2, 3, 2), (from_high[0], 5 - 2 * c, 5, 2))
        for c in range(3)
    ]
    scale = own[3]
    planes.append(gather(nodes, (from_low, -3, 0, 2), (scale, -1, 2, 1), (scale, 3, 3, 3), (from_high[1], 3, 6, 1)))
    planes.append(gather(nodes, (from_low, -4, 0, 1), (scale, -2, 1, 2), (scale, 2, 3, 2), (from_high[1], 2, 5, 2)))
    planes.append(gather(nodes, (own[4], -2, 1, 1), (own[4], 2, 4, 1), (from_high[0], -1, 5, 1)))
    rows = 6
    down_out[...] = down[...]
    up_out[...] = up[...]
    for p, plane in enumerate(planes):
        strip[p] = plane
        up_out[UP_CORNERS + 2 * p : UP_CORNERS + 2 * p + 2, :] = plane[rows - 2 : rows]
    around = planes[3] + planes[4]
    around = around + pltpu.roll(around, 1, 0)
    around = KE_DIAGONAL * (around + lane_roll(around, SLOTS))
    inv = jnp.where(around > 0.0, 1.0 / around, 0.0)
    corners = [plane[0:1] for plane in planes[0:3]]
    corners += [(plane * inv)[1:2] for plane in planes[0:3]]
    corners += [plane[0:1] for plane in planes[3:6]]
    for p, value in enumerate(corners):
        down_out[DOWN_CORNERS + p : DOWN_CORNERS + p + 1, :] = value
    layers, cn = nodes - 1, 3 * nodes
    tall = lax.broadcasted_iota(jnp.int32, (layers, LANES), 0)
    wide = lax.broadcasted_iota(jnp.int32, (layers, LANES), 1)
    edge = jnp.broadcast_to(planes[4][0:1] + planes[4][1:2], (layers, LANES))
    edge = jnp.sum(jnp.where(wide == SLOTS * tall, edge, 0.0), axis=1, keepdims=True)
    dense[...] = jnp.zeros(dense.shape, jnp.float32)
    dense[1 : layers + 1, :] = pair[...] + jnp.where(wide == 0, edge, pltpu.roll(pair[...], 1, 1))
    inv = 1.0 / (KE_DIAGONAL * (dense[0:nodes, :] + dense[1 : nodes + 1, :]))
    for c in range(3):
        at = cn + layers + nodes + c * nodes
        down_out[at : at + nodes, :] = down[at : at + nodes, :] * inv


PLANE = ("", "1", "2", "12")


def split_layers(lo, hi):
    sums = [{m: lo[c][m] + hi[c][m] for m in ("1", "2", "12")} for c in range(3)]
    diffs = [{m: hi[c][m] - lo[c][m] for m in PLANE} for c in range(3)]
    u, v, w = range(3)
    return (
        diffs[u][""], sums[v]["1"], sums[w]["2"],
        sums[u]["1"] + diffs[v][""], sums[u]["2"] + diffs[w][""], sums[v]["2"] + sums[w]["1"],
        diffs[u]["1"], sums[w]["12"], diffs[u]["2"], sums[v]["12"], diffs[v]["1"], diffs[w]["2"],
        sums[u]["12"], diffs[v]["2"], diffs[w]["1"],
        diffs[u]["12"], diffs[v]["12"], diffs[w]["12"],
    )


def stress(m):
    one, two, three = 1.0 / 16.0, 1.0 / 48.0, 1.0 / 144.0
    trace = (LAME * one) * (m[0] + m[1] + m[2])
    out = [trace + (2.0 * SHEAR * one) * m[i] for i in range(3)]
    out += [(SHEAR * one) * m[i] for i in (3, 4, 5)]
    own, other = (LAME + 3.0 * SHEAR) * two, LAME * two
    for i in (6, 8, 10):
        out += [own * m[i] + other * m[i + 1], own * m[i + 1] + other * m[i]]
    total = m[12] + m[13] + m[14]
    out += [(SHEAR * two) * (m[i] + total) for i in (12, 13, 14)]
    out += [((LAME + 4.0 * SHEAR) * three) * m[i] for i in (15, 16, 17)]
    return out


def inner(g, m):
    parts = [g[i] * m[i] for i in range(18)]
    while len(parts) > 1:
        parts = [parts[i] + parts[i + 1] if i + 1 < len(parts) else parts[i] for i in range(0, len(parts), 2)]
    return parts[0]


def join_layers(g):
    sums = [
        {"1": g[3], "2": g[4], "12": g[12]},
        {"1": g[1], "2": g[5], "12": g[9]},
        {"1": g[5], "2": g[2], "12": g[7]},
    ]
    diffs = [
        {"": g[0], "1": g[6], "2": g[8], "12": g[15]},
        {"": g[3], "1": g[10], "2": g[13], "12": g[16]},
        {"": g[4], "1": g[14], "2": g[11], "12": g[17]},
    ]
    lower = [{m: (sums[c][m] - diffs[c][m] if m else -diffs[c][m]) for m in PLANE} for c in range(3)]
    upper = [{m: (sums[c][m] + diffs[c][m] if m else diffs[c][m]) for m in PLANE} for c in range(3)]
    return lower, upper


def in_plane(x, right, up):
    y = right(x)
    near, far = x + y, y - x
    near_up, far_up = up(near), up(far)
    return {"": near + near_up, "1": near_up - near, "2": far + far_up, "12": far_up - far}


def out_of_plane(f, right, up):
    plain = (f[""] - f["2"]) + right(f[""] + f["2"])
    steep = (f["1"] - f["12"]) + right(f["1"] + f["12"])
    return (plain - steep) + up(plain + steep)


def operator_kernel(
    rhs_0, rhs_1, rhs_2, phase, fixed, strip, lo, hi,
    base, second, edges, sums,
    held, residual, inverse, turned,
):
    rhs, comps = (rhs_0, rhs_1, rhs_2), 3
    nodes, rows, width = rhs_0.shape
    layers = nodes - 1
    lane, row = lanes(), sublanes()
    last_row, below = row == 6, row == 7
    cn = comps * nodes
    def spread(ref, at):
        return jnp.broadcast_to(ref[pl.ds(at, 1), :], (8, LANES))

    def roll_up(x):
        return pltpu.roll(x, 7, 0)

    def roll_down(x):
        return pltpu.roll(x, 1, 0)

    def node_rows(x, x_m2):
        return x + jnp.where(below, x_m2, roll_down(x))

    def plane_modes(x, y, x_up, y_up):
        near, far, near_up, far_up = x + y, y - x, x_up + y_up, y_up - x_up
        return {"": near + near_up, "1": near_up - near, "2": far + far_up, "12": far_up - far}

    def node_forces(f, by):
        sides = []
        for sign in (-1, 1):
            plain = f[""] + f["2"] if sign > 0 else f[""] - f["2"]
            steep = f["1"] + f["12"] if sign > 0 else f["1"] - f["12"]
            sides.append((plain - steep) + roll_down(plain + steep))
        return sides[0] + lane_roll(sides[1], by)

    def products(totals, d0, image, z, s, v):
        return tuple(t + x for t, x in zip(totals, (d0 * image, image * z, s * v, v * image)))

    def above(p):
        return spread(hi, DOWN_CORNERS + p)

    def under(p, which):
        return spread(lo, UP_CORNERS + 2 * p + which)

    tiles = [
        jnp.where(row < 6, strip[p], jnp.where(last_row, above(p if p < 3 else p + 3), under(p, 1))) for p in range(6)
    ]
    left, right = tiles[3], tiles[4]
    edge_rows = node_rows(right, under(4, 0))
    row_7 = cn + layers + nodes
    first_7 = row_7 // 8 * 8
    turned[...] = pltpu.roll(hi[first_7:DOWN, :], LANES - 1, 1)

    def strip_diagonal(x):
        return KE_DIAGONAL * (x + lane_roll(x, SLOTS))

    strip_diag = strip_diagonal(node_rows(left + right, under(3, 0) + under(4, 0)))
    strip_inv = jnp.where(strip_diag > 0.0, 1.0 / strip_diag, 0.0)
    slot = lax.rem(lane, SLOTS)
    strip_scale = jnp.where((slot == 2) | (slot == 6), 0.0, right)
    strip_base = [tiles[c] * strip_inv for c in range(3)]

    def strip_layers(modes):
        return [{m: lane_roll(modes[c][m], -SLOTS) for m in PLANE} for c in range(3)]

    lower = []
    for c in range(3):
        x, x_7 = strip_base[c], above(3 + c)
        y, y_7 = lane_roll(x, -1), lane_roll(x_7, -1)
        lower.append(plane_modes(x, y, jnp.where(last_row, x_7, roll_up(x)), jnp.where(last_row, y_7, roll_up(y))))
    f_low, f_up = join_layers([strip_scale * x for x in stress(split_layers(lower, strip_layers(lower)))])
    strip_second, strip_sums = [], (0.0,) * 4
    for c in range(3):
        f = node_forces({m: f_low[c][m] + lane_roll(f_up[c][m], SLOTS) for m in PLANE}, 1)
        image = jnp.where(tiles[5] > 0.0, f, 0.0)
        s = jnp.where(tiles[5] > 0.0, f - tiles[c], 0.0)
        strip_second.append(s * strip_inv)
        strip_sums = products(strip_sums, strip_base[c], image, image * strip_inv, s, strip_second[c])
        edges[c] = strip_base[c]
        edges[3 + c] = strip_second[c]
    ends = [jnp.where(slot == 4, x, lane_roll(x, 4)) for x in strip_second]
    lower = [plane_modes(x, lane_roll(x, -1), roll_up(x), roll_up(lane_roll(x, -1))) for x in strip_second]
    m = split_layers(lower, strip_layers(lower))
    strip_e = strip_scale * inner(stress(m), m)

    def box(k):
        held[0, 0:rows, :] = table(element_rows(phase, k, layers), PHASE_STIFFNESS)
        held[0, 6:7, :] = hi[pl.ds(cn + k, 1), :]
        held[0, 7:8, :] = lo[pl.ds(cn + layers + k, 1), :]
        x = held[0]
        r = node_rows(x, spread(lo, cn + k))
        return x, r + jnp.where(lane == 0, lane_roll(edge_rows, -SLOTS * k), lane_roll(r, 1))

    def first_layer(k, around_node):
        inv = 1.0 / (KE_DIAGONAL * around_node)
        inverse[k] = inv
        out = []
        for c in range(3):
            q = c * nodes + k
            residual[q, 0:rows, :] = rhs[c][k]
            residual[q, 6:7, :] = hi[pl.ds(q, 1), :]
            residual[q, 7:8, :] = lo[pl.ds(q, 1), :]
            x = residual[q] * inv
            base[q] = x
            y = lane_roll(x, -1)
            x_up = jnp.where(last_row, spread(hi, row_7 + q), roll_up(x))
            y_up = jnp.where(last_row, spread(turned, row_7 - first_7 + q), roll_up(y))
            out.append(plane_modes(x, y, x_up, y_up))
        return out

    def finish_layer(k, f, totals):
        inv = inverse[k]
        held[1, 0:rows, :] = 1.0 - fixed[k].astype(jnp.float32)
        held[1, 6:7, :] = hi[pl.ds(cn + layers + k, 1), :]
        free = held[1] > 0.0
        inv = jnp.where(free, inv, 1.0)
        a, rest = totals[0], totals[1:]
        for c in range(3):
            q = c * nodes + k
            r0 = residual[q]
            d0 = r0 * inv
            image = jnp.where(free, node_forces(f[c], 1), d0)
            s = image - r0
            v = s * inv
            ends_now = lane_roll(ends[c], LANES - 1 - (SLOTS * k + 4))
            second[q] = jnp.where((lane == 0) | (lane == LANES - 1), ends_now, v)
            a, rest = a + r0 * d0, products(rest, d0, image, image * inv, s, v)
        return (a,) + rest

    def flat(x):
        return tuple(x[c][m] for c in range(3) for m in PLANE)

    def unflat(x):
        return [{m: x[4 * c + i] for i, m in enumerate(PLANE)} for c in range(3)]

    zero = jnp.zeros((8, LANES), jnp.float32)
    held[1] = zero
    held[2] = zero

    def element(k, low_modes, high_modes, scale, pending, totals):
        g = stress(split_layers(low_modes, high_modes))
        f_lower, f_upper = join_layers([scale * x for x in g])
        done = [{m: pending[c][m] + f_lower[c][m] for m in PLANE} for c in range(3)]
        return f_upper, finish_layer(k, done, totals)

    def forward(k, carry):
        low_modes, pending, totals, scale, b = carry
        next_scale, next_b = box(k + 1)
        high = first_layer(k + 1, b + next_b)
        f_upper, totals = element(k, unflat(low_modes), high, scale, unflat(pending), totals)
        return flat(high), flat(f_upper), totals, next_scale, next_b

    scale, b = box(0)
    carry = (flat(first_layer(0, b)), (zero,) * 12, (zero,) * 5, scale, b)
    low_modes, pending, totals, scale, b = lax.fori_loop(0, layers - 1, forward, carry, unroll=True)
    high = first_layer(layers, b)
    f_upper, totals = element(layers - 1, unflat(low_modes), high, scale, unflat(pending), totals)
    totals = finish_layer(layers, f_upper, totals)

    def second_layer(k):
        out = []
        for c in range(3):
            x = second[c * nodes + k]
            y = lane_roll(x, -1)
            out.append(plane_modes(x, y, roll_up(x), roll_up(y)))
        return out

    def again(k, carry):
        low_modes, total = carry
        high = second_layer(k + 1)
        m = split_layers(unflat(low_modes), high)
        held[2, 0:rows, :] = table(element_rows(phase, k, layers), PHASE_STIFFNESS)
        return flat(high), total + held[2] * inner(stress(m), m)

    _, total = lax.fori_loop(0, layers, again, (flat(second_layer(0)), zero), unroll=True)
    mine = row < rows
    inside = mine & (lane > 0) & (lane < LANES - 1)
    at_ends = mine & ((slot == 1) | (slot == 4))
    totals = [jnp.where(mine, totals[0], 0.0)] + [
        jnp.where(inside, x, 0.0) + jnp.where(at_ends, y, 0.0) for x, y in zip(totals[1:], strip_sums)
    ]
    totals.append(
        jnp.where(mine & (lane < LANES - 1), total, 0.0) + jnp.where(mine & (slot == 4), strip_e, 0.0)
    )
    rows_of = zero
    for i, x in enumerate(totals):
        rows_of = jnp.where(row == i, jnp.broadcast_to(jnp.sum(x, axis=0, keepdims=True), (8, LANES)), rows_of)
    sums[...] = jnp.broadcast_to(jnp.sum(rows_of, axis=1, keepdims=True), (8, LANES))


def energy_kernel(base, second, edges, phase, energy):
    nodes = base.shape[0] // 3
    layers = nodes - 1
    rows = phase.shape[0] // layers
    lane = lanes()

    def layer(field, first_edge, k):
        out = []
        for c in range(3):
            fill = lane_roll(edges[first_edge + c], LANES - 1 - (SLOTS * k + 5))
            out.append(
                in_plane(
                    field[c * nodes + k],
                    lambda t: jnp.where(lane == LANES - 1, fill, lane_roll(t, -1)),
                    lambda t: pltpu.roll(t, 7, 0),
                )
            )
        return out

    low = layer(base, 0, 0), layer(second, 3, 0)
    for k in range(layers):
        high = layer(base, 0, k + 1), layer(second, 3, k + 1)
        m, n = split_layers(low[0], high[0]), split_layers(low[1], high[1])
        g, h = stress(m), stress(n)
        slope = -table(element_rows(phase, k, layers), PHASE_SLOPE)
        for which, value in enumerate((inner(g, m), inner(h, m), inner(h, n))):
            energy[which, pl.ds(k, rows, stride=layers), :] = slope * value[0:rows]
        low = high


def combine_kernel(base, second, energy, sums, displacement, sensitivity):
    a, curve, plain, shifted, cross, bend = (sums[i : i + 1, :] for i in range(6))
    slope = curve / a
    alpha = a / curve
    less = 1.0 - slope
    rest = jnp.where(slope < 0.5, plain - slope * curve, shifted - less * less * a)
    bend = bend + 2.0 * less * cross + less * less * curve
    alpha_next = rest / (bend - rest * rest / curve)
    beta = alpha * alpha * rest / a
    first = alpha + alpha_next * beta - alpha * alpha_next * less
    other = -alpha * alpha_next
    comps, nodes, rows, width = displacement.shape
    for c in range(comps):
        for k in range(nodes):
            q = c * nodes + k
            displacement[c, k] = (first * base[q] + other * second[q])[0:rows]
    sensitivity[...] = (first * first) * energy[0] + (2.0 * first * other) * energy[1] + (other * other) * energy[2]


def exchange_pairs(one, two, axis):
    count = lax.axis_size(axis)
    far = lax.ppermute(two, axis, [(i, (i - 1) % count if i % 2 == 0 else (i + 1) % count) for i in range(count)])
    near = lax.ppermute(one, axis, [(i, i ^ 1) for i in range(count)])
    return near, far


def exchange(down, up, axis):
    count = lax.axis_size(axis)
    low = lax.ppermute(up, axis, [(i, (i + 1) % count) for i in range(count)])
    high = lax.ppermute(down, axis, [((i + 1) % count, i) for i in range(count)])
    return high, low


def total_over(x, axis):
    count = lax.axis_size(axis)
    if count & (count - 1):
        return lax.psum(x, axis)
    step = 1
    while step < count:
        width = 4 if count // step >= 4 else 2
        if axis == "gx" and count == 4:
            to = [[(i, (i + by) % 4) for i in range(4)] for by in (3, 2, 1)]
        else:
            to = [[(i, i ^ (step * by)) for i in range(count)] for by in range(1, width)]
        x = functools.reduce(jnp.add, [lax.ppermute(x, axis, pairs) for pairs in to], x)
        step *= width
    return x


def body(force, phase, fixed):
    comps, nodes, rows, width = force.shape
    layers = nodes - 1
    phase = phase.transpose(1, 0, 2).reshape(rows * layers, width)
    rhs = [(1 - fixed).astype(jnp.float32) * force[c] for c in range(comps)]
    f32 = jnp.float32
    paired = lax.axis_size("gy") % 2 == 0
    column = jax.ShapeDtypeStruct((2, 8, LANES), f32)
    messages = (jax.ShapeDtypeStruct((DOWN, LANES), f32), jax.ShapeDtypeStruct((UP, LANES), f32))
    strips = jax.ShapeDtypeStruct((6, 8, LANES), f32)

    def call(kernel, out_shape, scratch=()):
        return pl.pallas_call(kernel, out_shape=out_shape, scratch_shapes=scratch, compiler_params=PARAMS)

    own, col1, col2 = call(
        functools.partial(column_kernel, paired),
        (jax.ShapeDtypeStruct((5, 8, LANES), f32), column, column),
        [pltpu.VMEM((5, 8, LANES), f32)],
    )(*rhs, phase, fixed)
    down, up, pair = call(row_kernel, messages + (jax.ShapeDtypeStruct((layers, LANES), f32),))(*rhs, phase, fixed)
    near, far = (exchange_pairs if paired else exchange)(col1, col2, "gy")
    strip, down, up = call(
        functools.partial(strip_kernel, nodes, paired),
        (strips,) + messages,
        [pltpu.VMEM((32, LANES), f32)],
    )(own, far, near, down, up, pair)
    high, low = exchange(down, up, "gx")
    field = jax.ShapeDtypeStruct((comps * nodes, 8, LANES), f32)
    base, second, edges, sums = call(
        operator_kernel,
        (
            field,
            field,
            strips,
            jax.ShapeDtypeStruct((8, LANES), f32),
        ),
        [
            pltpu.VMEM((3, 8, LANES), f32),
            pltpu.VMEM((comps * nodes, 8, LANES), f32),
            pltpu.VMEM((nodes, 8, LANES), f32),
            pltpu.VMEM((DOWN - (comps * nodes + layers + nodes) // 8 * 8, LANES), f32),
        ],
    )(*rhs, phase, fixed, strip, low, high)
    energy = call(energy_kernel, jax.ShapeDtypeStruct((3,) + phase.shape, f32))(base, second, edges, phase)
    sums = total_over(total_over(sums, "gx"), "gy")
    displacement, sensitivity = call(
        combine_kernel,
        (jax.ShapeDtypeStruct(force.shape, f32), jax.ShapeDtypeStruct(phase.shape, f32)),
    )(base, second, energy, sums)
    return displacement, sensitivity.reshape(rows, layers, width).transpose(1, 0, 2)


def solution(mesh):
    return jax.shard_map(
        body,
        mesh=mesh,
        in_specs=(
            P(None, None, ("parts", "gx"), "gy"),
            P(None, ("parts", "gx"), "gy"),
            P(None, ("parts", "gx"), "gy"),
        ),
        out_specs=(P(None, None, ("parts", "gx"), "gy"), P(None, ("parts", "gx"), "gy")),
        check_vma=False,
    )
```

```python
import functools

import jax
import jax.numpy as jnp
import numpy as np
from jax import lax
from jax.experimental import pallas as pl
from jax.experimental.pallas import tpu as pltpu
from jax.sharding import PartitionSpec as P

PHASE_STIFFNESS = (0.125, 0.343, 0.614, 1.0)
PHASE_SLOPE = (0.75, 1.47, 2.17, 3.0)
POISSON = 0.3
LAME = POISSON / ((1.0 + POISSON) * (1.0 - 2.0 * POISSON))
SHEAR = 1.0 / (2.0 * (1.0 + POISSON))
KE_DIAGONAL = (LAME + 4.0 * SHEAR) / 9.0

SLOTS = 7
LANES = 128
DOWN, DOWN_CORNERS = 144, 135
UP, UP_CORNERS = 144, 83

VMEM = pl.BlockSpec(memory_space=pltpu.VMEM)
PARAMS = pltpu.CompilerParams(vmem_limit_bytes=32 * 1024 * 1024)


def lanes():
    return lax.broadcasted_iota(jnp.int32, (8, LANES), 1)


def sublanes():
    return lax.broadcasted_iota(jnp.int32, (8, LANES), 0)


def table(phase, values):
    out = jnp.full(phase.shape, values[3], jnp.float32)
    for index in (2, 1, 0):
        out = jnp.where(phase == index, jnp.float32(values[index]), out)
    return out


def element_rows(ref, k, layers):
    return ref[pl.ds(k, ref.shape[0] // layers, stride=layers), :]


def lane_roll(x, by):
    if isinstance(by, int):
        by = by % LANES
        return x if by == 0 else pltpu.roll(x, by, 1)
    return pltpu.roll(x, lax.rem(by + LANES, LANES), 1)


def is_even(axis):
    return lax.rem(lax.axis_index(axis), 2) == 0


def gather(nodes, *items):
    lane = lanes()
    slot = jnp.where(lane < nodes * SLOTS, lax.rem(lane, SLOTS), SLOTS)
    out = jnp.zeros((8, LANES), jnp.float32)
    for plane, by, first, count in items:
        out = jnp.where((slot >= first) & (slot < first + count), lane_roll(plane, by), out)
    return out


def column_kernel(paired, rhs_0, rhs_1, rhs_2, phase, fixed, own, col1, col2, pad):
    rhs = (rhs_0, rhs_1, rhs_2)
    nodes, rows, width = rhs_0.shape
    layers = nodes - 1
    lane = lax.broadcasted_iota(jnp.int32, (rows, LANES), 1)
    even = is_even("gy") if paired else True
    pad[...] = jnp.zeros(pad.shape, jnp.float32)
    planes = [jnp.zeros((rows, LANES), jnp.float32)] * 5
    for k in range(nodes):
        here = (lane >= k * SLOTS) & (lane < k * SLOTS + 5)
        values = [rhs[c][k] for c in range(3)]
        values.append(table(element_rows(phase, k, layers), PHASE_STIFFNESS) if k < layers else None)
        values.append((1 - fixed[k]).astype(jnp.float32))
        for p, value in enumerate(values):
            if value is not None:
                planes[p] = jnp.where(here, lane_roll(value, k * SLOTS + 3), planes[p])
    for p in range(5):
        pad[p, 0:rows, :] = planes[p]
        planes[p] = pad[p]
        own[p] = planes[p]
    high = [
        gather(nodes, (planes[0], -2, 0, 1), (planes[1], -1, 1, 1), (planes[2], 0, 2, 1), (planes[3], 2, 3, 2)),
        jnp.zeros((8, LANES), jnp.float32),
    ]
    low = [
        gather(nodes, (planes[0], -3, 0, 2), (planes[1], -1, 2, 2), (planes[2], 1, 4, 2), (planes[4], 3, 6, 1)),
        planes[3],
    ]
    for p in range(2):
        if paired:
            col1[p] = jnp.where(even, high[p], low[p])
            col2[p] = jnp.where(even, low[p], high[p])
        else:
            col1[p] = low[p]
            col2[p] = high[p]


def row_kernel(rhs_0, rhs_1, rhs_2, phase, fixed, down, up, pair):
    rhs = (rhs_0, rhs_1, rhs_2)
    nodes, rows, width = rhs_0.shape
    layers, cn = nodes - 1, 3 * nodes
    for k in range(nodes):
        for c in range(3):
            q = c * nodes + k
            down[q : q + 1, :] = rhs[c][k, 0:1]
            down[cn + layers + nodes + q : cn + layers + nodes + q + 1, :] = rhs[c][k, 1:2]
            up[q : q + 1, :] = rhs[c][k, rows - 1 : rows]
        at = cn + layers + k
        down[at : at + 1, :] = (1 - fixed[k, 0:1]).astype(jnp.float32)
    scale = [table(phase[i * layers : (i + 1) * layers], PHASE_STIFFNESS) for i in (0, 1, rows - 2, rows - 1)]
    down[cn : cn + layers, :] = scale[0]
    up[cn : cn + layers, :] = scale[2]
    up[cn + layers : cn + 2 * layers, :] = scale[3]
    pair[...] = scale[0] + scale[1]
    down[DOWN_CORNERS:, :] = jnp.zeros((DOWN - DOWN_CORNERS, LANES), jnp.float32)
    up[UP_CORNERS:, :] = jnp.zeros((UP - UP_CORNERS, LANES), jnp.float32)


def strip_kernel(nodes, paired, own, got2, got1, down, up, pair, strip, down_out, up_out, dense):
    even_y = is_even("gy") if paired else True
    if paired:
        from_low = jnp.where(even_y, got2[0], got1[0])
        from_high = [jnp.where(even_y, got1[p], got2[p]) for p in range(2)]
    else:
        from_low, from_high = got2[0], [got1[p] for p in range(2)]
    planes = [
        gather(nodes, (from_low, -c, 0, 1), (own[c], -2, 1, 2), (own[c], 2, 3, 2), (from_high[0], 5 - 2 * c, 5, 2))
        for c in range(3)
    ]
    scale = own[3]
    planes.append(gather(nodes, (from_low, -3, 0, 2), (scale, -1, 2, 1), (scale, 3, 3, 3), (from_high[1], 3, 6, 1)))
    planes.append(gather(nodes, (from_low, -4, 0, 1), (scale, -2, 1, 2), (scale, 2, 3, 2), (from_high[1], 2, 5, 2)))
    planes.append(gather(nodes, (own[4], -2, 1, 1), (own[4], 2, 4, 1), (from_high[0], -1, 5, 1)))
    rows = 6
    down_out[...] = down[...]
    up_out[...] = up[...]
    for p, plane in enumerate(planes):
        strip[p] = plane
        up_out[UP_CORNERS + 2 * p : UP_CORNERS + 2 * p + 2, :] = plane[rows - 2 : rows]
    around = planes[3] + planes[4]
    around = around + pltpu.roll(around, 1, 0)
    around = KE_DIAGONAL * (around + lane_roll(around, SLOTS))
    inv = jnp.where(around > 0.0, 1.0 / around, 0.0)
    corners = [plane[0:1] for plane in planes[0:3]]
    corners += [(plane * inv)[1:2] for plane in planes[0:3]]
    corners += [plane[0:1] for plane in planes[3:6]]
    for p, value in enumerate(corners):
        down_out[DOWN_CORNERS + p : DOWN_CORNERS + p + 1, :] = value
    layers, cn = nodes - 1, 3 * nodes
    tall = lax.broadcasted_iota(jnp.int32, (layers, LANES), 0)
    wide = lax.broadcasted_iota(jnp.int32, (layers, LANES), 1)
    edge = jnp.broadcast_to(planes[4][0:1] + planes[4][1:2], (layers, LANES))
    edge = jnp.sum(jnp.where(wide == SLOTS * tall, edge, 0.0), axis=1, keepdims=True)
    dense[...] = jnp.zeros(dense.shape, jnp.float32)
    dense[1 : layers + 1, :] = pair[...] + jnp.where(wide == 0, edge, pltpu.roll(pair[...], 1, 1))
    inv = 1.0 / (KE_DIAGONAL * (dense[0:nodes, :] + dense[1 : nodes + 1, :]))
    for c in range(3):
        at = cn + layers + nodes + c * nodes
        down_out[at : at + nodes, :] = down[at : at + nodes, :] * inv


PLANE = ("", "1", "2", "12")


def split_layers(lo, hi):
    sums = [{m: lo[c][m] + hi[c][m] for m in ("1", "2", "12")} for c in range(3)]
    diffs = [{m: hi[c][m] - lo[c][m] for m in PLANE} for c in range(3)]
    u, v, w = range(3)
    return (
        diffs[u][""], sums[v]["1"], sums[w]["2"],
        sums[u]["1"] + diffs[v][""], sums[u]["2"] + diffs[w][""], sums[v]["2"] + sums[w]["1"],
        diffs[u]["1"], sums[w]["12"], diffs[u]["2"], sums[v]["12"], diffs[v]["1"], diffs[w]["2"],
        sums[u]["12"], diffs[v]["2"], diffs[w]["1"],
        diffs[u]["12"], diffs[v]["12"], diffs[w]["12"],
    )


def stress(m):
    one, two, three = 1.0 / 16.0, 1.0 / 48.0, 1.0 / 144.0
    trace = (LAME * one) * (m[0] + m[1] + m[2])
    out = [trace + (2.0 * SHEAR * one) * m[i] for i in range(3)]
    out += [(SHEAR * one) * m[i] for i in (3, 4, 5)]
    own, other = (LAME + 3.0 * SHEAR) * two, LAME * two
    for i in (6, 8, 10):
        out += [own * m[i] + other * m[i + 1], own * m[i + 1] + other * m[i]]
    total = m[12] + m[13] + m[14]
    out += [(SHEAR * two) * (m[i] + total) for i in (12, 13, 14)]
    out += [((LAME + 4.0 * SHEAR) * three) * m[i] for i in (15, 16, 17)]
    return out


def inner(g, m):
    parts = [g[i] * m[i] for i in range(18)]
    while len(parts) > 1:
        parts = [parts[i] + parts[i + 1] if i + 1 < len(parts) else parts[i] for i in range(0, len(parts), 2)]
    return parts[0]


def join_layers(g):
    sums = [
        {"1": g[3], "2": g[4], "12": g[12]},
        {"1": g[1], "2": g[5], "12": g[9]},
        {"1": g[5], "2": g[2], "12": g[7]},
    ]
    diffs = [
        {"": g[0], "1": g[6], "2": g[8], "12": g[15]},
        {"": g[3], "1": g[10], "2": g[13], "12": g[16]},
        {"": g[4], "1": g[14], "2": g[11], "12": g[17]},
    ]
    lower = [{m: (sums[c][m] - diffs[c][m] if m else -diffs[c][m]) for m in PLANE} for c in range(3)]
    upper = [{m: (sums[c][m] + diffs[c][m] if m else diffs[c][m]) for m in PLANE} for c in range(3)]
    return lower, upper


def in_plane(x, right, up):
    y = right(x)
    near, far = x + y, y - x
    near_up, far_up = up(near), up(far)
    return {"": near + near_up, "1": near_up - near, "2": far + far_up, "12": far_up - far}


def out_of_plane(f, right, up):
    plain = (f[""] - f["2"]) + right(f[""] + f["2"])
    steep = (f["1"] - f["12"]) + right(f["1"] + f["12"])
    return (plain - steep) + up(plain + steep)


def operator_kernel(
    rhs_0, rhs_1, rhs_2, phase, fixed, strip, lo, hi,
    base, second, edges, sums,
    scales, frees, residual, inverse, turned,
):
    rhs, comps = (rhs_0, rhs_1, rhs_2), 3
    nodes, rows, width = rhs_0.shape
    layers = nodes - 1
    lane, row = lanes(), sublanes()
    last_row, below = row == 6, row == 7
    cn = comps * nodes
    def spread(ref, at):
        return jnp.broadcast_to(ref[pl.ds(at, 1), :], (8, LANES))

    def roll_up(x):
        return pltpu.roll(x, 7, 0)

    def roll_down(x):
        return pltpu.roll(x, 1, 0)

    def node_rows(x, x_m2):
        return x + jnp.where(below, x_m2, roll_down(x))

    def plane_modes(x, y, x_up, y_up):
        near, far, near_up, far_up = x + y, y - x, x_up + y_up, y_up - x_up
        return {"": near + near_up, "1": near_up - near, "2": far + far_up, "12": far_up - far}

    def node_forces(f, by):
        sides = []
        for sign in (-1, 1):
            plain = f[""] + f["2"] if sign > 0 else f[""] - f["2"]
            steep = f["1"] + f["12"] if sign > 0 else f["1"] - f["12"]
            sides.append((plain - steep) + roll_down(plain + steep))
        return sides[0] + lane_roll(sides[1], by)

    def products(totals, d0, image, z, s, v):
        return tuple(t + x for t, x in zip(totals, (d0 * image, image * z, s * v, v * image)))

    def above(p):
        return spread(hi, DOWN_CORNERS + p)

    def under(p, which):
        return spread(lo, UP_CORNERS + 2 * p + which)

    tiles = [
        jnp.where(row < 6, strip[p], jnp.where(last_row, above(p if p < 3 else p + 3), under(p, 1))) for p in range(6)
    ]
    left, right = tiles[3], tiles[4]
    edge_rows = node_rows(right, under(4, 0))
    row_7 = cn + layers + nodes
    first_7 = row_7 // 8 * 8
    turned[...] = pltpu.roll(hi[first_7:DOWN, :], LANES - 1, 1)

    def strip_diagonal(x):
        return KE_DIAGONAL * (x + lane_roll(x, SLOTS))

    strip_diag = strip_diagonal(node_rows(left + right, under(3, 0) + under(4, 0)))
    strip_inv = jnp.where(strip_diag > 0.0, 1.0 / strip_diag, 0.0)
    slot = lax.rem(lane, SLOTS)
    strip_scale = jnp.where((slot == 2) | (slot == 6), 0.0, right)
    strip_base = [tiles[c] * strip_inv for c in range(3)]

    def strip_layers(modes):
        return [{m: lane_roll(modes[c][m], -SLOTS) for m in PLANE} for c in range(3)]

    lower = []
    for c in range(3):
        x, x_7 = strip_base[c], above(3 + c)
        y, y_7 = lane_roll(x, -1), lane_roll(x_7, -1)
        lower.append(plane_modes(x, y, jnp.where(last_row, x_7, roll_up(x)), jnp.where(last_row, y_7, roll_up(y))))
    f_low, f_up = join_layers([strip_scale * x for x in stress(split_layers(lower, strip_layers(lower)))])
    strip_second, strip_sums = [], (0.0,) * 4
    for c in range(3):
        f = node_forces({m: f_low[c][m] + lane_roll(f_up[c][m], SLOTS) for m in PLANE}, 1)
        image = jnp.where(tiles[5] > 0.0, f, 0.0)
        s = jnp.where(tiles[5] > 0.0, f - tiles[c], 0.0)
        strip_second.append(s * strip_inv)
        strip_sums = products(strip_sums, strip_base[c], image, image * strip_inv, s, strip_second[c])
        edges[c] = strip_base[c]
        edges[3 + c] = strip_second[c]
    ends = [jnp.where(slot == 4, x, lane_roll(x, 4)) for x in strip_second]
    lower = [plane_modes(x, lane_roll(x, -1), roll_up(x), roll_up(lane_roll(x, -1))) for x in strip_second]
    m = split_layers(lower, strip_layers(lower))
    strip_e = strip_scale * inner(stress(m), m)

    def box(k):
        scales[k, 0:rows, :] = table(element_rows(phase, k, layers), PHASE_STIFFNESS)
        scales[k, 6:7, :] = hi[pl.ds(cn + k, 1), :]
        scales[k, 7:8, :] = lo[pl.ds(cn + layers + k, 1), :]
        x = scales[k]
        r = node_rows(x, spread(lo, cn + k))
        return x, r + jnp.where(lane == 0, lane_roll(edge_rows, -SLOTS * k), lane_roll(r, 1))

    def first_layer(k, around_node):
        inv = 1.0 / (KE_DIAGONAL * around_node)
        inverse[k] = inv
        out = []
        for c in range(3):
            q = c * nodes + k
            residual[q, 0:rows, :] = rhs[c][k]
            residual[q, 6:7, :] = hi[pl.ds(q, 1), :]
            residual[q, 7:8, :] = lo[pl.ds(q, 1), :]
            x = residual[q] * inv
            base[q] = x
            y = lane_roll(x, -1)
            x_up = jnp.where(last_row, spread(hi, row_7 + q), roll_up(x))
            y_up = jnp.where(last_row, spread(turned, row_7 - first_7 + q), roll_up(y))
            out.append(plane_modes(x, y, x_up, y_up))
        return out

    def finish_layer(k, f, totals):
        inv = inverse[k]
        frees[k, 0:rows, :] = 1.0 - fixed[k].astype(jnp.float32)
        frees[k, 6:7, :] = hi[pl.ds(cn + layers + k, 1), :]
        frees[k, 7:8, :] = jnp.zeros((1, LANES), jnp.float32)
        free = frees[k] > 0.0
        inv = jnp.where(free, inv, 1.0)
        a, rest = totals[0], totals[1:]
        for c in range(3):
            q = c * nodes + k
            r0 = residual[q]
            d0 = r0 * inv
            image = jnp.where(free, node_forces(f[c], 1), d0)
            s = image - r0
            v = s * inv
            ends_now = lane_roll(ends[c], LANES - 1 - (SLOTS * k + 4))
            second[q] = jnp.where((lane == 0) | (lane == LANES - 1), ends_now, v)
            a, rest = a + r0 * d0, products(rest, d0, image, image * inv, s, v)
        return (a,) + rest

    def flat(x):
        return tuple(x[c][m] for c in range(3) for m in PLANE)

    def unflat(x):
        return [{m: x[4 * c + i] for i, m in enumerate(PLANE)} for c in range(3)]

    zero = jnp.zeros((8, LANES), jnp.float32)

    def element(k, low_modes, high_modes, scale, pending, totals):
        g = stress(split_layers(low_modes, high_modes))
        f_lower, f_upper = join_layers([scale * x for x in g])
        done = [{m: pending[c][m] + f_lower[c][m] for m in PLANE} for c in range(3)]
        return f_upper, finish_layer(k, done, totals)

    def forward(k, carry):
        low_modes, pending, totals, scale, b = carry
        next_scale, next_b = box(k + 1)
        high = first_layer(k + 1, b + next_b)
        f_upper, totals = element(k, unflat(low_modes), high, scale, unflat(pending), totals)
        return flat(high), flat(f_upper), totals, next_scale, next_b

    scale, b = box(0)
    carry = (flat(first_layer(0, b)), (zero,) * 12, (zero,) * 5, scale, b)
    low_modes, pending, totals, scale, b = lax.fori_loop(0, layers - 1, forward, carry, unroll=True)
    high = first_layer(layers, b)
    f_upper, totals = element(layers - 1, unflat(low_modes), high, scale, unflat(pending), totals)
    totals = finish_layer(layers, f_upper, totals)

    def second_layer(k):
        out = []
        for c in range(3):
            x = second[c * nodes + k]
            y = lane_roll(x, -1)
            out.append(plane_modes(x, y, roll_up(x), roll_up(y)))
        return out

    def again(k, carry):
        low_modes, total = carry
        high = second_layer(k + 1)
        m = split_layers(unflat(low_modes), high)
        return flat(high), total + scales[k] * inner(stress(m), m)

    _, total = lax.fori_loop(0, layers, again, (flat(second_layer(0)), zero), unroll=True)
    mine = row < rows
    inside = mine & (lane > 0) & (lane < LANES - 1)
    at_ends = mine & ((slot == 1) | (slot == 4))
    totals = [jnp.where(mine, totals[0], 0.0)] + [
        jnp.where(inside, x, 0.0) + jnp.where(at_ends, y, 0.0) for x, y in zip(totals[1:], strip_sums)
    ]
    totals.append(
        jnp.where(mine & (lane < LANES - 1), total, 0.0) + jnp.where(mine & (slot == 4), strip_e, 0.0)
    )
    rows_of = zero
    for i, x in enumerate(totals):
        rows_of = jnp.where(row == i, jnp.broadcast_to(jnp.sum(x, axis=0, keepdims=True), (8, LANES)), rows_of)
    sums[...] = jnp.broadcast_to(jnp.sum(rows_of, axis=1, keepdims=True), (8, LANES))


def energy_kernel(base, second, edges, phase, energy):
    nodes = base.shape[0] // 3
    layers = nodes - 1
    rows = phase.shape[0] // layers
    lane = lanes()

    def layer(field, first_edge, k):
        out = []
        for c in range(3):
            fill = lane_roll(edges[first_edge + c], LANES - 1 - (SLOTS * k + 5))
            out.append(
                in_plane(
                    field[c * nodes + k],
                    lambda t: jnp.where(lane == LANES - 1, fill, lane_roll(t, -1)),
                    lambda t: pltpu.roll(t, 7, 0),
                )
            )
        return out

    low = layer(base, 0, 0), layer(second, 3, 0)
    for k in range(layers):
        high = layer(base, 0, k + 1), layer(second, 3, k + 1)
        m, n = split_layers(low[0], high[0]), split_layers(low[1], high[1])
        g, h = stress(m), stress(n)
        slope = -table(element_rows(phase, k, layers), PHASE_SLOPE)
        for which, value in enumerate((inner(g, m), inner(h, m), inner(h, n))):
            energy[which, pl.ds(k, rows, stride=layers), :] = slope * value[0:rows]
        low = high


def combine_kernel(base, second, energy, sums, displacement, sensitivity):
    a, curve, plain, shifted, cross, bend = (sums[i : i + 1, :] for i in range(6))
    slope = curve / a
    alpha = a / curve
    less = 1.0 - slope
    rest = jnp.where(slope < 0.5, plain - slope * curve, shifted - less * less * a)
    bend = bend + 2.0 * less * cross + less * less * curve
    alpha_next = rest / (bend - rest * rest / curve)
    beta = alpha * alpha * rest / a
    first = alpha + alpha_next * beta - alpha * alpha_next * less
    other = -alpha * alpha_next
    comps, nodes, rows, width = displacement.shape
    for c in range(comps):
        for k in range(nodes):
            q = c * nodes + k
            displacement[c, k] = (first * base[q] + other * second[q])[0:rows]
    sensitivity[...] = (first * first) * energy[0] + (2.0 * first * other) * energy[1] + (other * other) * energy[2]


def exchange_pairs(one, two, axis):
    count = lax.axis_size(axis)
    far = lax.ppermute(two, axis, [(i, (i - 1) % count if i % 2 == 0 else (i + 1) % count) for i in range(count)])
    near = lax.ppermute(one, axis, [(i, i ^ 1) for i in range(count)])
    return near, far


def exchange(down, up, axis):
    count = lax.axis_size(axis)
    low = lax.ppermute(up, axis, [(i, (i + 1) % count) for i in range(count)])
    high = lax.ppermute(down, axis, [((i + 1) % count, i) for i in range(count)])
    return high, low


def total_over(x, axis):
    count = lax.axis_size(axis)
    if count & (count - 1):
        return lax.psum(x, axis)
    step = 1
    while step < count:
        width = 4 if count // step >= 4 else 2
        if axis == "gx" and count == 4:
            to = [[(i, (i + by) % 4) for i in range(4)] for by in (3, 2, 1)]
        else:
            to = [[(i, i ^ (step * by)) for i in range(count)] for by in range(1, width)]
        x = functools.reduce(jnp.add, [lax.ppermute(x, axis, pairs) for pairs in to], x)
        step *= width
    return x


def body(force, phase, fixed):
    comps, nodes, rows, width = force.shape
    layers = nodes - 1
    phase = phase.transpose(1, 0, 2).reshape(rows * layers, width)
    rhs = [(1 - fixed).astype(jnp.float32) * force[c] for c in range(comps)]
    f32 = jnp.float32
    paired = lax.axis_size("gy") % 2 == 0
    column = jax.ShapeDtypeStruct((2, 8, LANES), f32)
    messages = (jax.ShapeDtypeStruct((DOWN, LANES), f32), jax.ShapeDtypeStruct((UP, LANES), f32))
    strips = jax.ShapeDtypeStruct((6, 8, LANES), f32)

    def call(kernel, out_shape, scratch=()):
        return pl.pallas_call(kernel, out_shape=out_shape, scratch_shapes=scratch, compiler_params=PARAMS)

    own, col1, col2 = call(
        functools.partial(column_kernel, paired),
        (jax.ShapeDtypeStruct((5, 8, LANES), f32), column, column),
        [pltpu.VMEM((5, 8, LANES), f32)],
    )(*rhs, phase, fixed)
    down, up, pair = call(row_kernel, messages + (jax.ShapeDtypeStruct((layers, LANES), f32),))(*rhs, phase, fixed)
    near, far = (exchange_pairs if paired else exchange)(col1, col2, "gy")
    strip, down, up = call(
        functools.partial(strip_kernel, nodes, paired),
        (strips,) + messages,
        [pltpu.VMEM((32, LANES), f32)],
    )(own, far, near, down, up, pair)
    high, low = exchange(down, up, "gx")
    field = jax.ShapeDtypeStruct((comps * nodes, 8, LANES), f32)
    base, second, edges, sums = call(
        operator_kernel,
        (
            field,
            field,
            strips,
            jax.ShapeDtypeStruct((8, LANES), f32),
        ),
        [
            pltpu.VMEM((layers, 8, LANES), f32),
            pltpu.VMEM((nodes, 8, LANES), f32),
            pltpu.VMEM((comps * nodes, 8, LANES), f32),
            pltpu.VMEM((nodes, 8, LANES), f32),
            pltpu.VMEM((DOWN - (comps * nodes + layers + nodes) // 8 * 8, LANES), f32),
        ],
    )(*rhs, phase, fixed, strip, low, high)
    energy = call(energy_kernel, jax.ShapeDtypeStruct((3,) + phase.shape, f32))(base, second, edges, phase)
    sums = total_over(total_over(sums, "gx"), "gy")
    displacement, sensitivity = call(
        combine_kernel,
        (jax.ShapeDtypeStruct(force.shape, f32), jax.ShapeDtypeStruct(phase.shape, f32)),
    )(base, second, energy, sums)
    return displacement, sensitivity.reshape(rows, layers, width).transpose(1, 0, 2)


def solution(mesh):
    return jax.shard_map(
        body,
        mesh=mesh,
        in_specs=(
            P(None, None, ("parts", "gx"), "gy"),
            P(None, ("parts", "gx"), "gy"),
            P(None, ("parts", "gx"), "gy"),
        ),
        out_specs=(P(None, None, ("parts", "gx"), "gy"), P(None, ("parts", "gx"), "gy")),
        check_vma=False,
    )
```

```python
import functools

import jax
import jax.numpy as jnp
import numpy as np
from jax import lax
from jax.experimental import pallas as pl
from jax.experimental.pallas import tpu as pltpu
from jax.sharding import PartitionSpec as P

PHASE_STIFFNESS = (0.125, 0.343, 0.614, 1.0)
PHASE_SLOPE = (0.75, 1.47, 2.17, 3.0)
POISSON = 0.3
LAME = POISSON / ((1.0 + POISSON) * (1.0 - 2.0 * POISSON))
SHEAR = 1.0 / (2.0 * (1.0 + POISSON))
KE_DIAGONAL = (LAME + 4.0 * SHEAR) / 9.0

SLOTS = 7
LANES = 128
DOWN, DOWN_CORNERS = 144, 135
UP, UP_CORNERS = 144, 83

PARAMS = pltpu.CompilerParams(vmem_limit_bytes=32 * 1024 * 1024)


def lanes():
    return lax.broadcasted_iota(jnp.int32, (8, LANES), 1)


def sublanes():
    return lax.broadcasted_iota(jnp.int32, (8, LANES), 0)


def table(phase, values):
    out = jnp.full(phase.shape, values[3], jnp.float32)
    for index in (2, 1, 0):
        out = jnp.where(phase == index, jnp.float32(values[index]), out)
    return out


def element_rows(ref, k, layers):
    return ref[pl.ds(k, ref.shape[0] // layers, stride=layers), :]


def lane_roll(x, by):
    if isinstance(by, int):
        by = by % LANES
        return x if by == 0 else pltpu.roll(x, by, 1)
    return pltpu.roll(x, lax.rem(by + LANES, LANES), 1)


def is_even(axis):
    return lax.rem(lax.axis_index(axis), 2) == 0


def gather(nodes, *items):
    lane = lanes()
    slot = jnp.where(lane < nodes * SLOTS, lax.rem(lane, SLOTS), SLOTS)
    out = jnp.zeros((8, LANES), jnp.float32)
    for plane, by, first, count in items:
        out = jnp.where((slot >= first) & (slot < first + count), lane_roll(plane, by), out)
    return out


def column_kernel(paired, rhs_0, rhs_1, rhs_2, phase, fixed, own, col1, col2, pad):
    rhs = (rhs_0, rhs_1, rhs_2)
    nodes, rows, width = rhs_0.shape
    layers = nodes - 1
    lane = lax.broadcasted_iota(jnp.int32, (rows, LANES), 1)
    even = is_even("gy") if paired else True
    pad[...] = jnp.zeros(pad.shape, jnp.float32)
    planes = [jnp.zeros((rows, LANES), jnp.float32)] * 5
    for k in range(nodes):
        here = (lane >= k * SLOTS) & (lane < k * SLOTS + 5)
        values = [rhs[c][k] for c in range(3)]
        values.append(table(element_rows(phase, k, layers), PHASE_STIFFNESS) if k < layers else None)
        values.append((1 - fixed[k]).astype(jnp.float32))
        for p, value in enumerate(values):
            if value is not None:
                planes[p] = jnp.where(here, lane_roll(value, k * SLOTS + 3), planes[p])
    for p in range(5):
        pad[p, 0:rows, :] = planes[p]
        planes[p] = pad[p]
        own[p] = planes[p]
    high = [
        gather(nodes, (planes[0], -2, 0, 1), (planes[1], -1, 1, 1), (planes[2], 0, 2, 1), (planes[3], 2, 3, 2)),
        jnp.zeros((8, LANES), jnp.float32),
    ]
    low = [
        gather(nodes, (planes[0], -3, 0, 2), (planes[1], -1, 2, 2), (planes[2], 1, 4, 2), (planes[4], 3, 6, 1)),
        planes[3],
    ]
    for p in range(2):
        if paired:
            col1[p] = jnp.where(even, high[p], low[p])
            col2[p] = jnp.where(even, low[p], high[p])
        else:
            col1[p] = low[p]
            col2[p] = high[p]


def row_kernel(rhs_0, rhs_1, rhs_2, phase, fixed, down, up, pair):
    rhs = (rhs_0, rhs_1, rhs_2)
    nodes, rows, width = rhs_0.shape
    layers, cn = nodes - 1, 3 * nodes
    for k in range(nodes):
        for c in range(3):
            q = c * nodes + k
            down[q : q + 1, :] = rhs[c][k, 0:1]
            down[cn + layers + nodes + q : cn + layers + nodes + q + 1, :] = rhs[c][k, 1:2]
            up[q : q + 1, :] = rhs[c][k, rows - 1 : rows]
        at = cn + layers + k
        down[at : at + 1, :] = (1 - fixed[k, 0:1]).astype(jnp.float32)
    scale = [table(phase[i * layers : (i + 1) * layers], PHASE_STIFFNESS) for i in (0, 1, rows - 2, rows - 1)]
    down[cn : cn + layers, :] = scale[0]
    up[cn : cn + layers, :] = scale[2]
    up[cn + layers : cn + 2 * layers, :] = scale[3]
    pair[...] = scale[0] + scale[1]
    down[DOWN_CORNERS:, :] = jnp.zeros((DOWN - DOWN_CORNERS, LANES), jnp.float32)
    up[UP_CORNERS:, :] = jnp.zeros((UP - UP_CORNERS, LANES), jnp.float32)


def strip_kernel(nodes, paired, own, got2, got1, down, up, pair, strip, down_out, up_out, dense):
    even_y = is_even("gy") if paired else True
    if paired:
        from_low = jnp.where(even_y, got2[0], got1[0])
        from_high = [jnp.where(even_y, got1[p], got2[p]) for p in range(2)]
    else:
        from_low, from_high = got2[0], [got1[p] for p in range(2)]
    planes = [
        gather(nodes, (from_low, -c, 0, 1), (own[c], -2, 1, 2), (own[c], 2, 3, 2), (from_high[0], 5 - 2 * c, 5, 2))
        for c in range(3)
    ]
    scale = own[3]
    planes.append(gather(nodes, (from_low, -3, 0, 2), (scale, -1, 2, 1), (scale, 3, 3, 3), (from_high[1], 3, 6, 1)))
    planes.append(gather(nodes, (from_low, -4, 0, 1), (scale, -2, 1, 2), (scale, 2, 3, 2), (from_high[1], 2, 5, 2)))
    planes.append(gather(nodes, (own[4], -2, 1, 1), (own[4], 2, 4, 1), (from_high[0], -1, 5, 1)))
    rows = 6
    down_out[...] = down[...]
    up_out[...] = up[...]
    for p, plane in enumerate(planes):
        strip[p] = plane
        up_out[UP_CORNERS + 2 * p : UP_CORNERS + 2 * p + 2, :] = plane[rows - 2 : rows]
    around = planes[3] + planes[4]
    around = around + pltpu.roll(around, 1, 0)
    around = KE_DIAGONAL * (around + lane_roll(around, SLOTS))
    inv = jnp.where(around > 0.0, 1.0 / around, 0.0)
    corners = [plane[0:1] for plane in planes[0:3]]
    corners += [(plane * inv)[1:2] for plane in planes[0:3]]
    corners += [plane[0:1] for plane in planes[3:6]]
    for p, value in enumerate(corners):
        down_out[DOWN_CORNERS + p : DOWN_CORNERS + p + 1, :] = value
    layers, cn = nodes - 1, 3 * nodes
    tall = lax.broadcasted_iota(jnp.int32, (layers, LANES), 0)
    wide = lax.broadcasted_iota(jnp.int32, (layers, LANES), 1)
    edge = jnp.broadcast_to(planes[4][0:1] + planes[4][1:2], (layers, LANES))
    edge = jnp.sum(jnp.where(wide == SLOTS * tall, edge, 0.0), axis=1, keepdims=True)
    dense[...] = jnp.zeros(dense.shape, jnp.float32)
    dense[1 : layers + 1, :] = pair[...] + jnp.where(wide == 0, edge, pltpu.roll(pair[...], 1, 1))
    inv = 1.0 / (KE_DIAGONAL * (dense[0:nodes, :] + dense[1 : nodes + 1, :]))
    for c in range(3):
        at = cn + layers + nodes + c * nodes
        down_out[at : at + nodes, :] = down[at : at + nodes, :] * inv


PLANE = ("", "1", "2", "12")


def split_layers(lo, hi):
    sums = [{m: lo[c][m] + hi[c][m] for m in ("1", "2", "12")} for c in range(3)]
    diffs = [{m: hi[c][m] - lo[c][m] for m in PLANE} for c in range(3)]
    u, v, w = range(3)
    return (
        diffs[u][""], sums[v]["1"], sums[w]["2"],
        sums[u]["1"] + diffs[v][""], sums[u]["2"] + diffs[w][""], sums[v]["2"] + sums[w]["1"],
        diffs[u]["1"], sums[w]["12"], diffs[u]["2"], sums[v]["12"], diffs[v]["1"], diffs[w]["2"],
        sums[u]["12"], diffs[v]["2"], diffs[w]["1"],
        diffs[u]["12"], diffs[v]["12"], diffs[w]["12"],
    )


def stress(m):
    one, two, three = 1.0 / 16.0, 1.0 / 48.0, 1.0 / 144.0
    trace = (LAME * one) * (m[0] + m[1] + m[2])
    out = [trace + (2.0 * SHEAR * one) * m[i] for i in range(3)]
    out += [(SHEAR * one) * m[i] for i in (3, 4, 5)]
    own, other = (LAME + 3.0 * SHEAR) * two, LAME * two
    for i in (6, 8, 10):
        out += [own * m[i] + other * m[i + 1], own * m[i + 1] + other * m[i]]
    total = m[12] + m[13] + m[14]
    out += [(SHEAR * two) * (m[i] + total) for i in (12, 13, 14)]
    out += [((LAME + 4.0 * SHEAR) * three) * m[i] for i in (15, 16, 17)]
    return out


def inner(g, m):
    parts = [g[i] * m[i] for i in range(18)]
    while len(parts) > 1:
        parts = [parts[i] + parts[i + 1] if i + 1 < len(parts) else parts[i] for i in range(0, len(parts), 2)]
    return parts[0]


def join_layers(g):
    sums = [
        {"1": g[3], "2": g[4], "12": g[12]},
        {"1": g[1], "2": g[5], "12": g[9]},
        {"1": g[5], "2": g[2], "12": g[7]},
    ]
    diffs = [
        {"": g[0], "1": g[6], "2": g[8], "12": g[15]},
        {"": g[3], "1": g[10], "2": g[13], "12": g[16]},
        {"": g[4], "1": g[14], "2": g[11], "12": g[17]},
    ]
    lower = [{m: (sums[c][m] - diffs[c][m] if m else -diffs[c][m]) for m in PLANE} for c in range(3)]
    upper = [{m: (sums[c][m] + diffs[c][m] if m else diffs[c][m]) for m in PLANE} for c in range(3)]
    return lower, upper


def in_plane(x, right, up):
    y = right(x)
    near, far = x + y, y - x
    near_up, far_up = up(near), up(far)
    return {"": near + near_up, "1": near_up - near, "2": far + far_up, "12": far_up - far}


def out_of_plane(f, right, up):
    plain = (f[""] - f["2"]) + right(f[""] + f["2"])
    steep = (f["1"] - f["12"]) + right(f["1"] + f["12"])
    return (plain - steep) + up(plain + steep)


def operator_kernel(
    rhs_0, rhs_1, rhs_2, phase, fixed, strip, lo, hi,
    base, second, edges, sums,
    scales, frees, residual, inverse, turned,
):
    rhs, comps = (rhs_0, rhs_1, rhs_2), 3
    nodes, rows, width = rhs_0.shape
    layers = nodes - 1
    lane, row = lanes(), sublanes()
    last_row, below = row == 6, row == 7
    cn = comps * nodes
    def spread(ref, at):
        return jnp.broadcast_to(ref[pl.ds(at, 1), :], (8, LANES))

    def roll_up(x):
        return pltpu.roll(x, 7, 0)

    def roll_down(x):
        return pltpu.roll(x, 1, 0)

    def node_rows(x, x_m2):
        return x + jnp.where(below, x_m2, roll_down(x))

    def plane_modes(x, y, x_up, y_up):
        near, far, near_up, far_up = x + y, y - x, x_up + y_up, y_up - x_up
        return {"": near + near_up, "1": near_up - near, "2": far + far_up, "12": far_up - far}

    def node_forces(f, by):
        sides = []
        for sign in (-1, 1):
            plain = f[""] + f["2"] if sign > 0 else f[""] - f["2"]
            steep = f["1"] + f["12"] if sign > 0 else f["1"] - f["12"]
            sides.append((plain - steep) + roll_down(plain + steep))
        return sides[0] + lane_roll(sides[1], by)

    def products(totals, d0, image, z, s, v):
        return tuple(t + x for t, x in zip(totals, (d0 * image, image * z, s * v, v * image)))

    def above(p):
        return spread(hi, DOWN_CORNERS + p)

    def under(p, which):
        return spread(lo, UP_CORNERS + 2 * p + which)

    tiles = [
        jnp.where(row < 6, strip[p], jnp.where(last_row, above(p if p < 3 else p + 3), under(p, 1))) for p in range(6)
    ]
    left, right = tiles[3], tiles[4]
    edge_rows = node_rows(right, under(4, 0))
    row_7 = cn + layers + nodes
    first_7 = row_7 // 8 * 8
    turned[...] = pltpu.roll(hi[first_7:DOWN, :], LANES - 1, 1)

    def strip_diagonal(x):
        return KE_DIAGONAL * (x + lane_roll(x, SLOTS))

    strip_diag = strip_diagonal(node_rows(left + right, under(3, 0) + under(4, 0)))
    strip_inv = jnp.where(strip_diag > 0.0, 1.0 / strip_diag, 0.0)
    slot = lax.rem(lane, SLOTS)
    strip_scale = jnp.where((slot == 2) | (slot == 6), 0.0, right)
    strip_base = [tiles[c] * strip_inv for c in range(3)]

    def strip_layers(modes):
        return [{m: lane_roll(modes[c][m], -SLOTS) for m in PLANE} for c in range(3)]

    lower = []
    for c in range(3):
        x, x_7 = strip_base[c], above(3 + c)
        y, y_7 = lane_roll(x, -1), lane_roll(x_7, -1)
        lower.append(plane_modes(x, y, jnp.where(last_row, x_7, roll_up(x)), jnp.where(last_row, y_7, roll_up(y))))
    f_low, f_up = join_layers([strip_scale * x for x in stress(split_layers(lower, strip_layers(lower)))])
    strip_second, strip_sums = [], (0.0,) * 4
    strip_free = tiles[5] > 0.0
    free_inv = jnp.where(strip_free, strip_inv, 1.0)
    for c in range(3):
        f = node_forces({m: f_low[c][m] + lane_roll(f_up[c][m], SLOTS) for m in PLANE}, 1)
        image = jnp.where(strip_free, f, tiles[c])
        s = image - tiles[c]
        strip_second.append(s * free_inv)
        strip_sums = products(strip_sums, tiles[c] * free_inv, image, image * free_inv, s, strip_second[c])
        edges[c] = strip_base[c]
        edges[3 + c] = strip_second[c]
    ends = [jnp.where(slot == 4, x, lane_roll(x, 4)) for x in strip_second]
    lower = [plane_modes(x, lane_roll(x, -1), roll_up(x), roll_up(lane_roll(x, -1))) for x in strip_second]
    m = split_layers(lower, strip_layers(lower))
    strip_e = strip_scale * inner(stress(m), m)

    def box(k):
        scales[k, 0:rows, :] = table(element_rows(phase, k, layers), PHASE_STIFFNESS)
        scales[k, 6:7, :] = hi[pl.ds(cn + k, 1), :]
        scales[k, 7:8, :] = lo[pl.ds(cn + layers + k, 1), :]
        x = scales[k]
        r = node_rows(x, spread(lo, cn + k))
        return x, r + jnp.where(lane == 0, lane_roll(edge_rows, -SLOTS * k), lane_roll(r, 1))

    def first_layer(k, around_node):
        inv = 1.0 / (KE_DIAGONAL * around_node)
        inverse[k] = inv
        out = []
        for c in range(3):
            q = c * nodes + k
            residual[q, 0:rows, :] = rhs[c][k]
            residual[q, 6:7, :] = hi[pl.ds(q, 1), :]
            residual[q, 7:8, :] = lo[pl.ds(q, 1), :]
            x = residual[q] * inv
            base[q] = x
            y = lane_roll(x, -1)
            x_up = jnp.where(last_row, spread(hi, row_7 + q), roll_up(x))
            y_up = jnp.where(last_row, spread(turned, row_7 - first_7 + q), roll_up(y))
            out.append(plane_modes(x, y, x_up, y_up))
        return out

    def finish_layer(k, f, totals):
        inv = inverse[k]
        frees[k, 0:rows, :] = 1.0 - fixed[k].astype(jnp.float32)
        frees[k, 6:7, :] = hi[pl.ds(cn + layers + k, 1), :]
        frees[k, 7:8, :] = jnp.zeros((1, LANES), jnp.float32)
        free = frees[k] > 0.0
        inv = jnp.where(free, inv, 1.0)
        a, rest = totals[0], totals[1:]
        for c in range(3):
            q = c * nodes + k
            r0 = residual[q]
            d0 = r0 * inv
            image = jnp.where(free, node_forces(f[c], 1), d0)
            s = image - r0
            v = s * inv
            ends_now = lane_roll(ends[c], LANES - 1 - (SLOTS * k + 4))
            second[q] = jnp.where((lane == 0) | (lane == LANES - 1), ends_now, v)
            a, rest = a + r0 * d0, products(rest, d0, image, image * inv, s, v)
        return (a,) + rest

    def flat(x):
        return tuple(x[c][m] for c in range(3) for m in PLANE)

    def unflat(x):
        return [{m: x[4 * c + i] for i, m in enumerate(PLANE)} for c in range(3)]

    zero = jnp.zeros((8, LANES), jnp.float32)

    def element(k, low_modes, high_modes, scale, pending, totals):
        g = stress(split_layers(low_modes, high_modes))
        f_lower, f_upper = join_layers([scale * x for x in g])
        done = [{m: pending[c][m] + f_lower[c][m] for m in PLANE} for c in range(3)]
        return f_upper, finish_layer(k, done, totals)

    def forward(k, carry):
        low_modes, pending, totals, scale, b = carry
        next_scale, next_b = box(k + 1)
        high = first_layer(k + 1, b + next_b)
        f_upper, totals = element(k, unflat(low_modes), high, scale, unflat(pending), totals)
        return flat(high), flat(f_upper), totals, next_scale, next_b

    scale, b = box(0)
    carry = (flat(first_layer(0, b)), (zero,) * 12, (zero,) * 5, scale, b)
    low_modes, pending, totals, scale, b = lax.fori_loop(0, layers - 1, forward, carry, unroll=True)
    high = first_layer(layers, b)
    f_upper, totals = element(layers - 1, unflat(low_modes), high, scale, unflat(pending), totals)
    totals = finish_layer(layers, f_upper, totals)

    def second_layer(k):
        out = []
        for c in range(3):
            x = second[c * nodes + k]
            y = lane_roll(x, -1)
            out.append(plane_modes(x, y, roll_up(x), roll_up(y)))
        return out

    def again(k, carry):
        low_modes, total = carry
        high = second_layer(k + 1)
        m = split_layers(unflat(low_modes), high)
        return flat(high), total + scales[k] * inner(stress(m), m)

    _, total = lax.fori_loop(0, layers, again, (flat(second_layer(0)), zero), unroll=True)
    mine = row < rows
    inside = mine & (lane > 0) & (lane < LANES - 1)
    at_ends = mine & ((slot == 1) | (slot == 4))
    totals = [jnp.where(mine, totals[0], 0.0)] + [
        jnp.where(inside, x, 0.0) + jnp.where(at_ends, y, 0.0) for x, y in zip(totals[1:], strip_sums)
    ]
    totals.append(
        jnp.where(mine & (lane < LANES - 1), total, 0.0) + jnp.where(mine & (slot == 4), strip_e, 0.0)
    )
    rows_of = zero
    for i, x in enumerate(totals):
        rows_of = jnp.where(row == i, jnp.broadcast_to(jnp.sum(x, axis=0, keepdims=True), (8, LANES)), rows_of)
    sums[...] = jnp.broadcast_to(jnp.sum(rows_of, axis=1, keepdims=True), (8, LANES))


def energy_kernel(base, second, edges, phase, energy):
    nodes = base.shape[0] // 3
    layers = nodes - 1
    rows = phase.shape[0] // layers
    lane = lanes()

    def layer(field, first_edge, k):
        out = []
        for c in range(3):
            fill = lane_roll(edges[first_edge + c], LANES - 1 - (SLOTS * k + 5))
            out.append(
                in_plane(
                    field[c * nodes + k],
                    lambda t: jnp.where(lane == LANES - 1, fill, lane_roll(t, -1)),
                    lambda t: pltpu.roll(t, 7, 0),
                )
            )
        return out

    low = layer(base, 0, 0), layer(second, 3, 0)
    for k in range(layers):
        high = layer(base, 0, k + 1), layer(second, 3, k + 1)
        m, n = split_layers(low[0], high[0]), split_layers(low[1], high[1])
        g, h = stress(m), stress(n)
        slope = -table(element_rows(phase, k, layers), PHASE_SLOPE)
        for which, value in enumerate((inner(g, m), inner(h, m), inner(h, n))):
            energy[which, pl.ds(k, rows, stride=layers), :] = slope * value[0:rows]
        low = high


def combine_kernel(base, second, energy, sums, displacement, sensitivity):
    a, curve, plain, shifted, cross, bend = (sums[i : i + 1, :] for i in range(6))
    slope = curve / a
    alpha = a / curve
    less = 1.0 - slope
    rest = jnp.where(slope < 0.5, plain - slope * curve, shifted - less * less * a)
    bend = bend + 2.0 * less * cross + less * less * curve
    alpha_next = rest / (bend - rest * rest / curve)
    beta = alpha * alpha * rest / a
    first = alpha + alpha_next * beta - alpha * alpha_next * less
    other = -alpha * alpha_next
    comps, nodes, rows, width = displacement.shape
    for c in range(comps):
        for k in range(nodes):
            q = c * nodes + k
            displacement[c, k] = (first * base[q] + other * second[q])[0:rows]
    sensitivity[...] = (first * first) * energy[0] + (2.0 * first * other) * energy[1] + (other * other) * energy[2]


def exchange_pairs(one, two, axis):
    count = lax.axis_size(axis)
    far = lax.ppermute(two, axis, [(i, (i - 1) % count if i % 2 == 0 else (i + 1) % count) for i in range(count)])
    near = lax.ppermute(one, axis, [(i, i ^ 1) for i in range(count)])
    return near, far


def exchange(down, up, axis):
    count = lax.axis_size(axis)
    low = lax.ppermute(up, axis, [(i, (i + 1) % count) for i in range(count)])
    high = lax.ppermute(down, axis, [((i + 1) % count, i) for i in range(count)])
    return high, low


def total_over(x, axis):
    count = lax.axis_size(axis)
    if count & (count - 1):
        return lax.psum(x, axis)
    step = 1
    while step < count:
        width = 4 if count // step >= 4 else 2
        if axis == "gx" and count == 4:
            to = [[(i, (i + by) % 4) for i in range(4)] for by in (3, 2, 1)]
        else:
            to = [[(i, i ^ (step * by)) for i in range(count)] for by in range(1, width)]
        x = functools.reduce(jnp.add, [lax.ppermute(x, axis, pairs) for pairs in to], x)
        step *= width
    return x


def body(force, phase, fixed):
    comps, nodes, rows, width = force.shape
    layers = nodes - 1
    phase = phase.transpose(1, 0, 2).reshape(rows * layers, width)
    rhs = [(1 - fixed).astype(jnp.float32) * force[c] for c in range(comps)]
    f32 = jnp.float32
    paired = lax.axis_size("gy") % 2 == 0
    column = jax.ShapeDtypeStruct((2, 8, LANES), f32)
    messages = (jax.ShapeDtypeStruct((DOWN, LANES), f32), jax.ShapeDtypeStruct((UP, LANES), f32))
    strips = jax.ShapeDtypeStruct((6, 8, LANES), f32)

    def call(kernel, out_shape, scratch=()):
        return pl.pallas_call(kernel, out_shape=out_shape, scratch_shapes=scratch, compiler_params=PARAMS)

    own, col1, col2 = call(
        functools.partial(column_kernel, paired),
        (jax.ShapeDtypeStruct((5, 8, LANES), f32), column, column),
        [pltpu.VMEM((5, 8, LANES), f32)],
    )(*rhs, phase, fixed)
    down, up, pair = call(row_kernel, messages + (jax.ShapeDtypeStruct((layers, LANES), f32),))(*rhs, phase, fixed)
    near, far = (exchange_pairs if paired else exchange)(col1, col2, "gy")
    strip, down, up = call(
        functools.partial(strip_kernel, nodes, paired),
        (strips,) + messages,
        [pltpu.VMEM((32, LANES), f32)],
    )(own, far, near, down, up, pair)
    high, low = exchange(down, up, "gx")
    field = jax.ShapeDtypeStruct((comps * nodes, 8, LANES), f32)
    base, second, edges, sums = call(
        operator_kernel,
        (
            field,
            field,
            strips,
            jax.ShapeDtypeStruct((8, LANES), f32),
        ),
        [
            pltpu.VMEM((layers, 8, LANES), f32),
            pltpu.VMEM((nodes, 8, LANES), f32),
            pltpu.VMEM((comps * nodes, 8, LANES), f32),
            pltpu.VMEM((nodes, 8, LANES), f32),
            pltpu.VMEM((DOWN - (comps * nodes + layers + nodes) // 8 * 8, LANES), f32),
        ],
    )(*rhs, phase, fixed, strip, low, high)
    energy = call(energy_kernel, jax.ShapeDtypeStruct((3,) + phase.shape, f32))(base, second, edges, phase)
    sums = total_over(total_over(sums, "gx"), "gy")
    displacement, sensitivity = call(
        combine_kernel,
        (jax.ShapeDtypeStruct(force.shape, f32), jax.ShapeDtypeStruct(phase.shape, f32)),
    )(base, second, energy, sums)
    return displacement, sensitivity.reshape(rows, layers, width).transpose(1, 0, 2)


def solution(mesh):
    return jax.shard_map(
        body,
        mesh=mesh,
        in_specs=(
            P(None, None, ("parts", "gx"), "gy"),
            P(None, ("parts", "gx"), "gy"),
            P(None, ("parts", "gx"), "gy"),
        ),
        out_specs=(P(None, None, ("parts", "gx"), "gy"), P(None, ("parts", "gx"), "gy")),
        check_vma=False,
    )
```

```python
import functools

import jax
import jax.numpy as jnp
import numpy as np
from jax import lax
from jax.experimental import pallas as pl
from jax.experimental.pallas import tpu as pltpu
from jax.sharding import PartitionSpec as P

PHASE_STIFFNESS = (0.125, 0.343, 0.614, 1.0)
PHASE_SLOPE = (0.75, 1.47, 2.17, 3.0)
POISSON = 0.3
LAME = POISSON / ((1.0 + POISSON) * (1.0 - 2.0 * POISSON))
SHEAR = 1.0 / (2.0 * (1.0 + POISSON))
KE_DIAGONAL = (LAME + 4.0 * SHEAR) / 9.0

SLOTS = 7
LANES = 128
DOWN, DOWN_CORNERS = 144, 135
UP, UP_CORNERS = 144, 83

PARAMS = pltpu.CompilerParams(vmem_limit_bytes=32 * 1024 * 1024)


def lanes():
    return lax.broadcasted_iota(jnp.int32, (8, LANES), 1)


def sublanes():
    return lax.broadcasted_iota(jnp.int32, (8, LANES), 0)


def table(phase, values):
    out = jnp.full(phase.shape, values[3], jnp.float32)
    for index in (2, 1, 0):
        out = jnp.where(phase == index, jnp.float32(values[index]), out)
    return out


def element_rows(ref, k, layers):
    return ref[pl.ds(k, ref.shape[0] // layers, stride=layers), :]


def lane_roll(x, by):
    if isinstance(by, int):
        by = by % LANES
        return x if by == 0 else pltpu.roll(x, by, 1)
    return pltpu.roll(x, lax.rem(by + LANES, LANES), 1)


def is_even(axis):
    return lax.rem(lax.axis_index(axis), 2) == 0


def gather(nodes, *items):
    lane = lanes()
    slot = jnp.where(lane < nodes * SLOTS, lax.rem(lane, SLOTS), SLOTS)
    out = jnp.zeros((8, LANES), jnp.float32)
    for plane, by, first, count in items:
        out = jnp.where((slot >= first) & (slot < first + count), lane_roll(plane, by), out)
    return out


def column_kernel(paired, rhs_0, rhs_1, rhs_2, phase, fixed, own, col1, col2, pad):
    rhs = (rhs_0, rhs_1, rhs_2)
    nodes, rows, width = rhs_0.shape
    layers = nodes - 1
    lane = lax.broadcasted_iota(jnp.int32, (rows, LANES), 1)
    even = is_even("gy") if paired else True
    pad[...] = jnp.zeros(pad.shape, jnp.float32)
    planes = [jnp.zeros((rows, LANES), jnp.float32)] * 5
    for k in range(nodes):
        here = (lane >= k * SLOTS) & (lane < k * SLOTS + 5)
        values = [rhs[c][k] for c in range(3)]
        values.append(table(element_rows(phase, k, layers), PHASE_STIFFNESS) if k < layers else None)
        values.append((1 - fixed[k]).astype(jnp.float32))
        for p, value in enumerate(values):
            if value is not None:
                planes[p] = jnp.where(here, lane_roll(value, k * SLOTS + 3), planes[p])
    for p in range(5):
        pad[p, 0:rows, :] = planes[p]
        planes[p] = pad[p]
        own[p] = planes[p]
    high = [
        gather(nodes, (planes[0], -2, 0, 1), (planes[1], -1, 1, 1), (planes[2], 0, 2, 1), (planes[3], 2, 3, 2)),
        jnp.zeros((8, LANES), jnp.float32),
    ]
    low = [
        gather(nodes, (planes[0], -3, 0, 2), (planes[1], -1, 2, 2), (planes[2], 1, 4, 2), (planes[4], 3, 6, 1)),
        planes[3],
    ]
    for p in range(2):
        if paired:
            col1[p] = jnp.where(even, high[p], low[p])
            col2[p] = jnp.where(even, low[p], high[p])
        else:
            col1[p] = low[p]
            col2[p] = high[p]


def row_kernel(rhs_0, rhs_1, rhs_2, phase, fixed, down, up, pair):
    rhs = (rhs_0, rhs_1, rhs_2)
    nodes, rows, width = rhs_0.shape
    layers, cn = nodes - 1, 3 * nodes
    for k in range(nodes):
        for c in range(3):
            q = c * nodes + k
            down[q : q + 1, :] = rhs[c][k, 0:1]
            down[cn + layers + nodes + q : cn + layers + nodes + q + 1, :] = rhs[c][k, 1:2]
            up[q : q + 1, :] = rhs[c][k, rows - 1 : rows]
        at = cn + layers + k
        down[at : at + 1, :] = (1 - fixed[k, 0:1]).astype(jnp.float32)
    scale = [table(phase[i * layers : (i + 1) * layers], PHASE_STIFFNESS) for i in (0, 1, rows - 2, rows - 1)]
    down[cn : cn + layers, :] = scale[0]
    up[cn : cn + layers, :] = scale[2]
    up[cn + layers : cn + 2 * layers, :] = scale[3]
    pair[...] = scale[0] + scale[1]
    down[DOWN_CORNERS:, :] = jnp.zeros((DOWN - DOWN_CORNERS, LANES), jnp.float32)
    up[UP_CORNERS:, :] = jnp.zeros((UP - UP_CORNERS, LANES), jnp.float32)


def strip_kernel(nodes, paired, own, got2, got1, up, strip, up_out):
    even_y = is_even("gy") if paired else True
    if paired:
        from_low = jnp.where(even_y, got2[0], got1[0])
        from_high = [jnp.where(even_y, got1[p], got2[p]) for p in range(2)]
    else:
        from_low, from_high = got2[0], [got1[p] for p in range(2)]
    planes = [
        gather(nodes, (from_low, -c, 0, 1), (own[c], -2, 1, 2), (own[c], 2, 3, 2), (from_high[0], 5 - 2 * c, 5, 2))
        for c in range(3)
    ]
    scale = own[3]
    planes.append(gather(nodes, (from_low, -3, 0, 2), (scale, -1, 2, 1), (scale, 3, 3, 3), (from_high[1], 3, 6, 1)))
    planes.append(gather(nodes, (from_low, -4, 0, 1), (scale, -2, 1, 2), (scale, 2, 3, 2), (from_high[1], 2, 5, 2)))
    planes.append(gather(nodes, (own[4], -2, 1, 1), (own[4], 2, 4, 1), (from_high[0], -1, 5, 1)))
    rows = 6
    up_out[...] = up[...]
    for p, plane in enumerate(planes):
        strip[p] = plane
        up_out[UP_CORNERS + 2 * p : UP_CORNERS + 2 * p + 2, :] = plane[rows - 2 : rows]


def lower_kernel(nodes, strip, down, pair, down_out, dense):
    planes = [strip[p] for p in range(6)]
    down_out[...] = down[...]
    around = planes[3] + planes[4]
    around = around + pltpu.roll(around, 1, 0)
    around = KE_DIAGONAL * (around + lane_roll(around, SLOTS))
    inv = jnp.where(around > 0.0, 1.0 / around, 0.0)
    corners = [plane[0:1] for plane in planes[0:3]]
    corners += [(plane * inv)[1:2] for plane in planes[0:3]]
    corners += [plane[0:1] for plane in planes[3:6]]
    for p, value in enumerate(corners):
        down_out[DOWN_CORNERS + p : DOWN_CORNERS + p + 1, :] = value
    layers, cn = nodes - 1, 3 * nodes
    tall = lax.broadcasted_iota(jnp.int32, (layers, LANES), 0)
    wide = lax.broadcasted_iota(jnp.int32, (layers, LANES), 1)
    edge = jnp.broadcast_to(planes[4][0:1] + planes[4][1:2], (layers, LANES))
    edge = jnp.sum(jnp.where(wide == SLOTS * tall, edge, 0.0), axis=1, keepdims=True)
    dense[...] = jnp.zeros(dense.shape, jnp.float32)
    dense[1 : layers + 1, :] = pair[...] + jnp.where(wide == 0, edge, pltpu.roll(pair[...], 1, 1))
    inv = 1.0 / (KE_DIAGONAL * (dense[0:nodes, :] + dense[1 : nodes + 1, :]))
    for c in range(3):
        at = cn + layers + nodes + c * nodes
        down_out[at : at + nodes, :] = down[at : at + nodes, :] * inv


PLANE = ("", "1", "2", "12")


def split_layers(lo, hi):
    sums = [{m: lo[c][m] + hi[c][m] for m in ("1", "2", "12")} for c in range(3)]
    diffs = [{m: hi[c][m] - lo[c][m] for m in PLANE} for c in range(3)]
    u, v, w = range(3)
    return (
        diffs[u][""], sums[v]["1"], sums[w]["2"],
        sums[u]["1"] + diffs[v][""], sums[u]["2"] + diffs[w][""], sums[v]["2"] + sums[w]["1"],
        diffs[u]["1"], sums[w]["12"], diffs[u]["2"], sums[v]["12"], diffs[v]["1"], diffs[w]["2"],
        sums[u]["12"], diffs[v]["2"], diffs[w]["1"],
        diffs[u]["12"], diffs[v]["12"], diffs[w]["12"],
    )


def stress(m):
    one, two, three = 1.0 / 16.0, 1.0 / 48.0, 1.0 / 144.0
    trace = (LAME * one) * (m[0] + m[1] + m[2])
    out = [trace + (2.0 * SHEAR * one) * m[i] for i in range(3)]
    out += [(SHEAR * one) * m[i] for i in (3, 4, 5)]
    own, other = (LAME + 3.0 * SHEAR) * two, LAME * two
    for i in (6, 8, 10):
        out += [own * m[i] + other * m[i + 1], own * m[i + 1] + other * m[i]]
    total = m[12] + m[13] + m[14]
    out += [(SHEAR * two) * (m[i] + total) for i in (12, 13, 14)]
    out += [((LAME + 4.0 * SHEAR) * three) * m[i] for i in (15, 16, 17)]
    return out


def inner(g, m):
    parts = [g[i] * m[i] for i in range(18)]
    while len(parts) > 1:
        parts = [parts[i] + parts[i + 1] if i + 1 < len(parts) else parts[i] for i in range(0, len(parts), 2)]
    return parts[0]


def join_layers(g):
    sums = [
        {"1": g[3], "2": g[4], "12": g[12]},
        {"1": g[1], "2": g[5], "12": g[9]},
        {"1": g[5], "2": g[2], "12": g[7]},
    ]
    diffs = [
        {"": g[0], "1": g[6], "2": g[8], "12": g[15]},
        {"": g[3], "1": g[10], "2": g[13], "12": g[16]},
        {"": g[4], "1": g[14], "2": g[11], "12": g[17]},
    ]
    lower = [{m: (sums[c][m] - diffs[c][m] if m else -diffs[c][m]) for m in PLANE} for c in range(3)]
    upper = [{m: (sums[c][m] + diffs[c][m] if m else diffs[c][m]) for m in PLANE} for c in range(3)]
    return lower, upper


def in_plane(x, right, up):
    y = right(x)
    near, far = x + y, y - x
    near_up, far_up = up(near), up(far)
    return {"": near + near_up, "1": near_up - near, "2": far + far_up, "12": far_up - far}


def out_of_plane(f, right, up):
    plain = (f[""] - f["2"]) + right(f[""] + f["2"])
    steep = (f["1"] - f["12"]) + right(f["1"] + f["12"])
    return (plain - steep) + up(plain + steep)


def operator_kernel(
    rhs_0, rhs_1, rhs_2, phase, fixed, strip, lo, hi,
    base, second, edges, sums,
    scales, frees, residual, inverse, turned,
):
    rhs, comps = (rhs_0, rhs_1, rhs_2), 3
    nodes, rows, width = rhs_0.shape
    layers = nodes - 1
    lane, row = lanes(), sublanes()
    last_row, below = row == 6, row == 7
    cn = comps * nodes
    def spread(ref, at):
        return jnp.broadcast_to(ref[pl.ds(at, 1), :], (8, LANES))

    def roll_up(x):
        return pltpu.roll(x, 7, 0)

    def roll_down(x):
        return pltpu.roll(x, 1, 0)

    def node_rows(x, x_m2):
        return x + jnp.where(below, x_m2, roll_down(x))

    def plane_modes(x, y, x_up, y_up):
        near, far, near_up, far_up = x + y, y - x, x_up + y_up, y_up - x_up
        return {"": near + near_up, "1": near_up - near, "2": far + far_up, "12": far_up - far}

    def node_forces(f, by):
        sides = []
        for sign in (-1, 1):
            plain = f[""] + f["2"] if sign > 0 else f[""] - f["2"]
            steep = f["1"] + f["12"] if sign > 0 else f["1"] - f["12"]
            sides.append((plain - steep) + roll_down(plain + steep))
        return sides[0] + lane_roll(sides[1], by)

    def products(totals, d0, image, z, s, v):
        return tuple(t + x for t, x in zip(totals, (d0 * image, image * z, s * v, v * image)))

    def above(p):
        return spread(hi, DOWN_CORNERS + p)

    def under(p, which):
        return spread(lo, UP_CORNERS + 2 * p + which)

    tiles = [
        jnp.where(row < 6, strip[p], jnp.where(last_row, above(p if p < 3 else p + 3), under(p, 1))) for p in range(6)
    ]
    left, right = tiles[3], tiles[4]
    edge_rows = node_rows(right, under(4, 0))
    row_7 = cn + layers + nodes
    first_7 = row_7 // 8 * 8
    turned[...] = pltpu.roll(hi[first_7:DOWN, :], LANES - 1, 1)

    def strip_diagonal(x):
        return KE_DIAGONAL * (x + lane_roll(x, SLOTS))

    strip_diag = strip_diagonal(node_rows(left + right, under(3, 0) + under(4, 0)))
    strip_inv = jnp.where(strip_diag > 0.0, 1.0 / strip_diag, 0.0)
    slot = lax.rem(lane, SLOTS)
    strip_scale = jnp.where((slot == 2) | (slot == 6), 0.0, right)
    strip_base = [tiles[c] * strip_inv for c in range(3)]

    def strip_layers(modes):
        return [{m: lane_roll(modes[c][m], -SLOTS) for m in PLANE} for c in range(3)]

    lower = []
    for c in range(3):
        x, x_7 = strip_base[c], above(3 + c)
        y, y_7 = lane_roll(x, -1), lane_roll(x_7, -1)
        lower.append(plane_modes(x, y, jnp.where(last_row, x_7, roll_up(x)), jnp.where(last_row, y_7, roll_up(y))))
    f_low, f_up = join_layers([strip_scale * x for x in stress(split_layers(lower, strip_layers(lower)))])
    strip_second, strip_sums = [], (0.0,) * 4
    strip_free = tiles[5] > 0.0
    free_inv = jnp.where(strip_free, strip_inv, 1.0)
    for c in range(3):
        f = node_forces({m: f_low[c][m] + lane_roll(f_up[c][m], SLOTS) for m in PLANE}, 1)
        image = jnp.where(strip_free, f, tiles[c])
        s = image - tiles[c]
        strip_second.append(s * free_inv)
        strip_sums = products(strip_sums, tiles[c] * free_inv, image, image * free_inv, s, strip_second[c])
        edges[c] = strip_base[c]
        edges[3 + c] = strip_second[c]
    ends = [jnp.where(slot == 4, x, lane_roll(x, 4)) for x in strip_second]
    lower = [plane_modes(x, lane_roll(x, -1), roll_up(x), roll_up(lane_roll(x, -1))) for x in strip_second]
    m = split_layers(lower, strip_layers(lower))
    strip_e = strip_scale * inner(stress(m), m)

    def box(k):
        scales[k, 0:rows, :] = table(element_rows(phase, k, layers), PHASE_STIFFNESS)
        scales[k, 6:7, :] = hi[pl.ds(cn + k, 1), :]
        scales[k, 7:8, :] = lo[pl.ds(cn + layers + k, 1), :]
        x = scales[k]
        r = node_rows(x, spread(lo, cn + k))
        return x, r + jnp.where(lane == 0, lane_roll(edge_rows, -SLOTS * k), lane_roll(r, 1))

    def first_layer(k, around_node):
        inv = 1.0 / (KE_DIAGONAL * around_node)
        inverse[k] = inv
        out = []
        for c in range(3):
            q = c * nodes + k
            residual[q, 0:rows, :] = rhs[c][k]
            residual[q, 6:7, :] = hi[pl.ds(q, 1), :]
            residual[q, 7:8, :] = lo[pl.ds(q, 1), :]
            x = residual[q] * inv
            base[q] = x
            y = lane_roll(x, -1)
            x_up = jnp.where(last_row, spread(hi, row_7 + q), roll_up(x))
            y_up = jnp.where(last_row, spread(turned, row_7 - first_7 + q), roll_up(y))
            out.append(plane_modes(x, y, x_up, y_up))
        return out

    def finish_layer(k, f, totals):
        inv = inverse[k]
        frees[k, 0:rows, :] = 1.0 - fixed[k].astype(jnp.float32)
        frees[k, 6:7, :] = hi[pl.ds(cn + layers + k, 1), :]
        frees[k, 7:8, :] = jnp.zeros((1, LANES), jnp.float32)
        free = frees[k] > 0.0
        inv = jnp.where(free, inv, 1.0)
        a, rest = totals[0], totals[1:]
        for c in range(3):
            q = c * nodes + k
            r0 = residual[q]
            d0 = r0 * inv
            image = jnp.where(free, node_forces(f[c], 1), d0)
            s = image - r0
            v = s * inv
            ends_now = lane_roll(ends[c], LANES - 1 - (SLOTS * k + 4))
            second[q] = jnp.where((lane == 0) | (lane == LANES - 1), ends_now, v)
            a, rest = a + r0 * d0, products(rest, d0, image, image * inv, s, v)
        return (a,) + rest

    def flat(x):
        return tuple(x[c][m] for c in range(3) for m in PLANE)

    def unflat(x):
        return [{m: x[4 * c + i] for i, m in enumerate(PLANE)} for c in range(3)]

    zero = jnp.zeros((8, LANES), jnp.float32)

    def element(k, low_modes, high_modes, scale, pending, totals):
        g = stress(split_layers(low_modes, high_modes))
        f_lower, f_upper = join_layers([scale * x for x in g])
        done = [{m: pending[c][m] + f_lower[c][m] for m in PLANE} for c in range(3)]
        return f_upper, finish_layer(k, done, totals)

    def forward(k, carry):
        low_modes, pending, totals, scale, b = carry
        next_scale, next_b = box(k + 1)
        high = first_layer(k + 1, b + next_b)
        f_upper, totals = element(k, unflat(low_modes), high, scale, unflat(pending), totals)
        return flat(high), flat(f_upper), totals, next_scale, next_b

    scale, b = box(0)
    carry = (flat(first_layer(0, b)), (zero,) * 12, (zero,) * 5, scale, b)
    low_modes, pending, totals, scale, b = lax.fori_loop(0, layers - 1, forward, carry, unroll=True)
    high = first_layer(layers, b)
    f_upper, totals = element(layers - 1, unflat(low_modes), high, scale, unflat(pending), totals)
    totals = finish_layer(layers, f_upper, totals)

    def second_layer(k):
        out = []
        for c in range(3):
            x = second[c * nodes + k]
            y = lane_roll(x, -1)
            out.append(plane_modes(x, y, roll_up(x), roll_up(y)))
        return out

    def again(k, carry):
        low_modes, total = carry
        high = second_layer(k + 1)
        m = split_layers(unflat(low_modes), high)
        return flat(high), total + scales[k] * inner(stress(m), m)

    _, total = lax.fori_loop(0, layers, again, (flat(second_layer(0)), zero), unroll=True)
    mine = row < rows
    inside = mine & (lane > 0) & (lane < LANES - 1)
    at_ends = mine & ((slot == 1) | (slot == 4))
    totals = [jnp.where(mine, totals[0], 0.0)] + [
        jnp.where(inside, x, 0.0) + jnp.where(at_ends, y, 0.0) for x, y in zip(totals[1:], strip_sums)
    ]
    totals.append(
        jnp.where(mine & (lane < LANES - 1), total, 0.0) + jnp.where(mine & (slot == 4), strip_e, 0.0)
    )
    rows_of = zero
    for i, x in enumerate(totals):
        rows_of = jnp.where(row == i, jnp.broadcast_to(jnp.sum(x, axis=0, keepdims=True), (8, LANES)), rows_of)
    sums[...] = jnp.broadcast_to(jnp.sum(rows_of, axis=1, keepdims=True), (8, LANES))


def energy_kernel(base, second, edges, phase, energy):
    nodes = base.shape[0] // 3
    layers = nodes - 1
    rows = phase.shape[0] // layers
    lane = lanes()

    def layer(field, first_edge, k):
        out = []
        for c in range(3):
            fill = lane_roll(edges[first_edge + c], LANES - 1 - (SLOTS * k + 5))
            out.append(
                in_plane(
                    field[c * nodes + k],
                    lambda t: jnp.where(lane == LANES - 1, fill, lane_roll(t, -1)),
                    lambda t: pltpu.roll(t, 7, 0),
                )
            )
        return out

    low = layer(base, 0, 0), layer(second, 3, 0)
    for k in range(layers):
        high = layer(base, 0, k + 1), layer(second, 3, k + 1)
        m, n = split_layers(low[0], high[0]), split_layers(low[1], high[1])
        g, h = stress(m), stress(n)
        slope = -table(element_rows(phase, k, layers), PHASE_SLOPE)
        for which, value in enumerate((inner(g, m), inner(h, m), inner(h, n))):
            energy[which, pl.ds(k, rows, stride=layers), :] = slope * value[0:rows]
        low = high


def combine_kernel(base, second, energy, sums, displacement, sensitivity):
    a, curve, plain, shifted, cross, bend = (sums[i : i + 1, :] for i in range(6))
    slope = curve / a
    alpha = a / curve
    less = 1.0 - slope
    rest = jnp.where(slope < 0.5, plain - slope * curve, shifted - less * less * a)
    bend = bend + 2.0 * less * cross + less * less * curve
    alpha_next = rest / (bend - rest * rest / curve)
    beta = alpha * alpha * rest / a
    first = alpha + alpha_next * beta - alpha * alpha_next * less
    other = -alpha * alpha_next
    comps, nodes, rows, width = displacement.shape
    for c in range(comps):
        for k in range(nodes):
            q = c * nodes + k
            displacement[c, k] = (first * base[q] + other * second[q])[0:rows]
    sensitivity[...] = (first * first) * energy[0] + (2.0 * first * other) * energy[1] + (other * other) * energy[2]


def exchange_pairs(one, two, axis):
    count = lax.axis_size(axis)
    far = lax.ppermute(two, axis, [(i, (i - 1) % count if i % 2 == 0 else (i + 1) % count) for i in range(count)])
    near = lax.ppermute(one, axis, [(i, i ^ 1) for i in range(count)])
    return near, far


def exchange(down, up, axis):
    count = lax.axis_size(axis)
    low = lax.ppermute(up, axis, [(i, (i + 1) % count) for i in range(count)])
    high = lax.ppermute(down, axis, [((i + 1) % count, i) for i in range(count)])
    return high, low


def total_over(x, axis):
    count = lax.axis_size(axis)
    if count & (count - 1):
        return lax.psum(x, axis)
    step = 1
    while step < count:
        width = 4 if count // step >= 4 else 2
        if axis == "gx" and count == 4:
            to = [[(i, (i + by) % 4) for i in range(4)] for by in (3, 2, 1)]
        else:
            to = [[(i, i ^ (step * by)) for i in range(count)] for by in range(1, width)]
        x = functools.reduce(jnp.add, [lax.ppermute(x, axis, pairs) for pairs in to], x)
        step *= width
    return x


def body(force, phase, fixed):
    comps, nodes, rows, width = force.shape
    layers = nodes - 1
    phase = phase.transpose(1, 0, 2).reshape(rows * layers, width)
    rhs = [(1 - fixed).astype(jnp.float32) * force[c] for c in range(comps)]
    f32 = jnp.float32
    paired = lax.axis_size("gy") % 2 == 0
    column = jax.ShapeDtypeStruct((2, 8, LANES), f32)
    messages = (jax.ShapeDtypeStruct((DOWN, LANES), f32), jax.ShapeDtypeStruct((UP, LANES), f32))
    strips = jax.ShapeDtypeStruct((6, 8, LANES), f32)

    def call(kernel, out_shape, scratch=()):
        return pl.pallas_call(kernel, out_shape=out_shape, scratch_shapes=scratch, compiler_params=PARAMS)

    own, col1, col2 = call(
        functools.partial(column_kernel, paired),
        (jax.ShapeDtypeStruct((5, 8, LANES), f32), column, column),
        [pltpu.VMEM((5, 8, LANES), f32)],
    )(*rhs, phase, fixed)
    down, up, pair = call(row_kernel, messages + (jax.ShapeDtypeStruct((layers, LANES), f32),))(*rhs, phase, fixed)
    near, far = (exchange_pairs if paired else exchange)(col1, col2, "gy")
    strip, up = call(functools.partial(strip_kernel, nodes, paired), (strips, messages[1]))(own, far, near, up)
    down = call(
        functools.partial(lower_kernel, nodes),
        messages[0],
        [pltpu.VMEM((32, LANES), f32)],
    )(strip, down, pair)
    high, low = exchange(down, up, "gx")
    field = jax.ShapeDtypeStruct((comps * nodes, 8, LANES), f32)
    base, second, edges, sums = call(
        operator_kernel,
        (
            field,
            field,
            strips,
            jax.ShapeDtypeStruct((8, LANES), f32),
        ),
        [
            pltpu.VMEM((layers, 8, LANES), f32),
            pltpu.VMEM((nodes, 8, LANES), f32),
            pltpu.VMEM((comps * nodes, 8, LANES), f32),
            pltpu.VMEM((nodes, 8, LANES), f32),
            pltpu.VMEM((DOWN - (comps * nodes + layers + nodes) // 8 * 8, LANES), f32),
        ],
    )(*rhs, phase, fixed, strip, low, high)
    energy = call(energy_kernel, jax.ShapeDtypeStruct((3,) + phase.shape, f32))(base, second, edges, phase)
    sums = total_over(total_over(sums, "gx"), "gy")
    displacement, sensitivity = call(
        combine_kernel,
        (jax.ShapeDtypeStruct(force.shape, f32), jax.ShapeDtypeStruct(phase.shape, f32)),
    )(base, second, energy, sums)
    return displacement, sensitivity.reshape(rows, layers, width).transpose(1, 0, 2)


def solution(mesh):
    return jax.shard_map(
        body,
        mesh=mesh,
        in_specs=(
            P(None, None, ("parts", "gx"), "gy"),
            P(None, ("parts", "gx"), "gy"),
            P(None, ("parts", "gx"), "gy"),
        ),
        out_specs=(P(None, None, ("parts", "gx"), "gy"), P(None, ("parts", "gx"), "gy")),
        check_vma=False,
    )
```

```python
import functools

import jax
import jax.numpy as jnp
import numpy as np
from jax import lax
from jax.experimental import pallas as pl
from jax.experimental.pallas import tpu as pltpu
from jax.sharding import PartitionSpec as P

PHASE_STIFFNESS = (0.125, 0.343, 0.614, 1.0)
PHASE_SLOPE = (0.75, 1.47, 2.17, 3.0)
POISSON = 0.3
LAME = POISSON / ((1.0 + POISSON) * (1.0 - 2.0 * POISSON))
SHEAR = 1.0 / (2.0 * (1.0 + POISSON))
KE_DIAGONAL = (LAME + 4.0 * SHEAR) / 9.0

SLOTS = 7
LANES = 128
DOWN, DOWN_CORNERS = 144, 135
UP, UP_CORNERS = 144, 83

PARAMS = pltpu.CompilerParams(vmem_limit_bytes=32 * 1024 * 1024)


def lanes():
    return lax.broadcasted_iota(jnp.int32, (8, LANES), 1)


def sublanes():
    return lax.broadcasted_iota(jnp.int32, (8, LANES), 0)


def table(phase, values):
    out = jnp.full(phase.shape, values[3], jnp.float32)
    for index in (2, 1, 0):
        out = jnp.where(phase == index, jnp.float32(values[index]), out)
    return out


def element_rows(ref, k, layers):
    return ref[pl.ds(k, ref.shape[0] // layers, stride=layers), :]


def lane_roll(x, by):
    if isinstance(by, int):
        by = by % LANES
        return x if by == 0 else pltpu.roll(x, by, 1)
    return pltpu.roll(x, lax.rem(by + LANES, LANES), 1)


def is_even(axis):
    return lax.rem(lax.axis_index(axis), 2) == 0


def gather(nodes, *items):
    lane = lanes()
    slot = jnp.where(lane < nodes * SLOTS, lax.rem(lane, SLOTS), SLOTS)
    out = jnp.zeros((8, LANES), jnp.float32)
    for plane, by, first, count in items:
        out = jnp.where((slot >= first) & (slot < first + count), lane_roll(plane, by), out)
    return out


def column_kernel(paired, rhs_0, rhs_1, rhs_2, phase, fixed, own, col1, col2, pad):
    rhs = (rhs_0, rhs_1, rhs_2)
    nodes, rows, width = rhs_0.shape
    layers = nodes - 1
    lane = lax.broadcasted_iota(jnp.int32, (rows, LANES), 1)
    even = is_even("gy") if paired else True
    pad[...] = jnp.zeros(pad.shape, jnp.float32)
    planes = [jnp.zeros((rows, LANES), jnp.float32)] * 5
    for k in range(nodes):
        here = (lane >= k * SLOTS) & (lane < k * SLOTS + 5)
        values = [rhs[c][k] for c in range(3)]
        values.append(table(element_rows(phase, k, layers), PHASE_STIFFNESS) if k < layers else None)
        values.append((1 - fixed[k]).astype(jnp.float32))
        for p, value in enumerate(values):
            if value is not None:
                planes[p] = jnp.where(here, lane_roll(value, k * SLOTS + 3), planes[p])
    for p in range(5):
        pad[p, 0:rows, :] = planes[p]
        planes[p] = pad[p]
        own[p] = planes[p]
    high = [
        gather(nodes, (planes[0], -2, 0, 1), (planes[1], -1, 1, 1), (planes[2], 0, 2, 1), (planes[3], 2, 3, 2)),
        jnp.zeros((8, LANES), jnp.float32),
    ]
    low = [
        gather(nodes, (planes[0], -3, 0, 2), (planes[1], -1, 2, 2), (planes[2], 1, 4, 2), (planes[4], 3, 6, 1)),
        planes[3],
    ]
    for p in range(2):
        if paired:
            col1[p] = jnp.where(even, high[p], low[p])
            col2[p] = jnp.where(even, low[p], high[p])
        else:
            col1[p] = low[p]
            col2[p] = high[p]


def row_kernel(rhs_0, rhs_1, rhs_2, phase, fixed, down, up, pair):
    rhs = (rhs_0, rhs_1, rhs_2)
    nodes, rows, width = rhs_0.shape
    layers, cn = nodes - 1, 3 * nodes
    for k in range(nodes):
        for c in range(3):
            q = c * nodes + k
            down[q : q + 1, :] = rhs[c][k, 0:1]
            down[cn + layers + nodes + q : cn + layers + nodes + q + 1, :] = rhs[c][k, 1:2]
            up[q : q + 1, :] = rhs[c][k, rows - 1 : rows]
        at = cn + layers + k
        down[at : at + 1, :] = (1 - fixed[k, 0:1]).astype(jnp.float32)
    scale = [table(phase[i * layers : (i + 1) * layers], PHASE_STIFFNESS) for i in (0, 1, rows - 2, rows - 1)]
    down[cn : cn + layers, :] = scale[0]
    up[cn : cn + layers, :] = scale[2]
    up[cn + layers : cn + 2 * layers, :] = scale[3]
    pair[...] = scale[0] + scale[1]
    down[DOWN_CORNERS:, :] = jnp.zeros((DOWN - DOWN_CORNERS, LANES), jnp.float32)
    up[UP_CORNERS:, :] = jnp.zeros((UP - UP_CORNERS, LANES), jnp.float32)


def strip_kernel(nodes, paired, own, got2, got1, down, up, pair, strip, down_out, up_out, dense):
    even_y = is_even("gy") if paired else True
    if paired:
        from_low = jnp.where(even_y, got2[0], got1[0])
        from_high = [jnp.where(even_y, got1[p], got2[p]) for p in range(2)]
    else:
        from_low, from_high = got2[0], [got1[p] for p in range(2)]
    planes = [
        gather(nodes, (from_low, -c, 0, 1), (own[c], -2, 1, 2), (own[c], 2, 3, 2), (from_high[0], 5 - 2 * c, 5, 2))
        for c in range(3)
    ]
    scale = own[3]
    planes.append(gather(nodes, (from_low, -3, 0, 2), (scale, -1, 2, 1), (scale, 3, 3, 3), (from_high[1], 3, 6, 1)))
    planes.append(gather(nodes, (from_low, -4, 0, 1), (scale, -2, 1, 2), (scale, 2, 3, 2), (from_high[1], 2, 5, 2)))
    planes.append(gather(nodes, (own[4], -2, 1, 1), (own[4], 2, 4, 1), (from_high[0], -1, 5, 1)))
    rows = 6
    down_out[...] = down[...]
    up_out[...] = up[...]
    for p, plane in enumerate(planes):
        strip[p] = plane
        up_out[UP_CORNERS + 2 * p : UP_CORNERS + 2 * p + 2, :] = plane[rows - 2 : rows]
    around = planes[3] + planes[4]
    around = around + pltpu.roll(around, 1, 0)
    around = KE_DIAGONAL * (around + lane_roll(around, SLOTS))
    inv = jnp.where(around > 0.0, 1.0 / around, 0.0)
    corners = [plane[0:1] for plane in planes[0:3]]
    corners += [(plane * inv)[1:2] for plane in planes[0:3]]
    corners += [plane[0:1] for plane in planes[3:6]]
    for p, value in enumerate(corners):
        down_out[DOWN_CORNERS + p : DOWN_CORNERS + p + 1, :] = value
    layers, cn = nodes - 1, 3 * nodes
    tall = lax.broadcasted_iota(jnp.int32, (layers, LANES), 0)
    wide = lax.broadcasted_iota(jnp.int32, (layers, LANES), 1)
    edge = jnp.broadcast_to(planes[4][0:1] + planes[4][1:2], (layers, LANES))
    edge = jnp.sum(jnp.where(wide == SLOTS * tall, edge, 0.0), axis=1, keepdims=True)
    dense[...] = jnp.zeros(dense.shape, jnp.float32)
    dense[1 : layers + 1, :] = pair[...] + jnp.where(wide == 0, edge, pltpu.roll(pair[...], 1, 1))
    inv = 1.0 / (KE_DIAGONAL * (dense[0:nodes, :] + dense[1 : nodes + 1, :]))
    for c in range(3):
        at = cn + layers + nodes + c * nodes
        down_out[at : at + nodes, :] = down[at : at + nodes, :] * inv


PLANE = ("", "1", "2", "12")


def split_layers(lo, hi):
    sums = [{m: lo[c][m] + hi[c][m] for m in ("1", "2", "12")} for c in range(3)]
    diffs = [{m: hi[c][m] - lo[c][m] for m in PLANE} for c in range(3)]
    u, v, w = range(3)
    return (
        diffs[u][""], sums[v]["1"], sums[w]["2"],
        sums[u]["1"] + diffs[v][""], sums[u]["2"] + diffs[w][""], sums[v]["2"] + sums[w]["1"],
        diffs[u]["1"], sums[w]["12"], diffs[u]["2"], sums[v]["12"], diffs[v]["1"], diffs[w]["2"],
        sums[u]["12"], diffs[v]["2"], diffs[w]["1"],
        diffs[u]["12"], diffs[v]["12"], diffs[w]["12"],
    )


def stress(m):
    one, two, three = 1.0 / 16.0, 1.0 / 48.0, 1.0 / 144.0
    trace = (LAME * one) * (m[0] + m[1] + m[2])
    out = [trace + (2.0 * SHEAR * one) * m[i] for i in range(3)]
    out += [(SHEAR * one) * m[i] for i in (3, 4, 5)]
    own, other = (LAME + 3.0 * SHEAR) * two, LAME * two
    for i in (6, 8, 10):
        out += [own * m[i] + other * m[i + 1], own * m[i + 1] + other * m[i]]
    total = m[12] + m[13] + m[14]
    out += [(SHEAR * two) * (m[i] + total) for i in (12, 13, 14)]
    out += [((LAME + 4.0 * SHEAR) * three) * m[i] for i in (15, 16, 17)]
    return out


def inner(g, m):
    parts = [g[i] * m[i] for i in range(18)]
    while len(parts) > 1:
        parts = [parts[i] + parts[i + 1] if i + 1 < len(parts) else parts[i] for i in range(0, len(parts), 2)]
    return parts[0]


def join_layers(g):
    sums = [
        {"1": g[3], "2": g[4], "12": g[12]},
        {"1": g[1], "2": g[5], "12": g[9]},
        {"1": g[5], "2": g[2], "12": g[7]},
    ]
    diffs = [
        {"": g[0], "1": g[6], "2": g[8], "12": g[15]},
        {"": g[3], "1": g[10], "2": g[13], "12": g[16]},
        {"": g[4], "1": g[14], "2": g[11], "12": g[17]},
    ]
    lower = [{m: (sums[c][m] - diffs[c][m] if m else -diffs[c][m]) for m in PLANE} for c in range(3)]
    upper = [{m: (sums[c][m] + diffs[c][m] if m else diffs[c][m]) for m in PLANE} for c in range(3)]
    return lower, upper


def in_plane(x, right, up):
    y = right(x)
    near, far = x + y, y - x
    near_up, far_up = up(near), up(far)
    return {"": near + near_up, "1": near_up - near, "2": far + far_up, "12": far_up - far}


def out_of_plane(f, right, up):
    plain = (f[""] - f["2"]) + right(f[""] + f["2"])
    steep = (f["1"] - f["12"]) + right(f["1"] + f["12"])
    return (plain - steep) + up(plain + steep)


def operator_kernel(
    rhs_0, rhs_1, rhs_2, phase, fixed, strip, lo, hi,
    base, second, edges, sums,
    scales, frees, residual, inverse, turned,
):
    rhs, comps = (rhs_0, rhs_1, rhs_2), 3
    nodes, rows, width = rhs_0.shape
    layers = nodes - 1
    lane, row = lanes(), sublanes()
    last_row, below = row == 6, row == 7
    cn = comps * nodes
    def spread(ref, at):
        return jnp.broadcast_to(ref[pl.ds(at, 1), :], (8, LANES))

    def roll_up(x):
        return pltpu.roll(x, 7, 0)

    def roll_down(x):
        return pltpu.roll(x, 1, 0)

    def node_rows(x, x_m2):
        return x + jnp.where(below, x_m2, roll_down(x))

    def plane_modes(x, y, x_up, y_up):
        near, far, near_up, far_up = x + y, y - x, x_up + y_up, y_up - x_up
        return {"": near + near_up, "1": near_up - near, "2": far + far_up, "12": far_up - far}

    def node_forces(f, by):
        sides = []
        for sign in (-1, 1):
            plain = f[""] + f["2"] if sign > 0 else f[""] - f["2"]
            steep = f["1"] + f["12"] if sign > 0 else f["1"] - f["12"]
            sides.append((plain - steep) + roll_down(plain + steep))
        return sides[0] + lane_roll(sides[1], by)

    def products(totals, d0, image, z, s, v):
        return tuple(t + x for t, x in zip(totals, (d0 * image, image * z, s * v, v * image)))

    def above(p):
        return spread(hi, DOWN_CORNERS + p)

    def under(p, which):
        return spread(lo, UP_CORNERS + 2 * p + which)

    tiles = [
        jnp.where(row < 6, strip[p], jnp.where(last_row, above(p if p < 3 else p + 3), under(p, 1))) for p in range(6)
    ]
    left, right = tiles[3], tiles[4]
    edge_rows = node_rows(right, under(4, 0))
    row_7 = cn + layers + nodes
    first_7 = row_7 // 8 * 8
    turned[...] = pltpu.roll(hi[first_7:DOWN, :], LANES - 1, 1)

    def strip_diagonal(x):
        return KE_DIAGONAL * (x + lane_roll(x, SLOTS))

    strip_diag = strip_diagonal(node_rows(left + right, under(3, 0) + under(4, 0)))
    strip_inv = jnp.where(strip_diag > 0.0, 1.0 / strip_diag, 0.0)
    slot = lax.rem(lane, SLOTS)
    strip_scale = jnp.where((slot == 2) | (slot == 6), 0.0, right)
    strip_base = [tiles[c] * strip_inv for c in range(3)]

    def strip_layers(modes):
        return [{m: lane_roll(modes[c][m], -SLOTS) for m in PLANE} for c in range(3)]

    lower = []
    for c in range(3):
        x, x_7 = strip_base[c], above(3 + c)
        y, y_7 = lane_roll(x, -1), lane_roll(x_7, -1)
        lower.append(plane_modes(x, y, jnp.where(last_row, x_7, roll_up(x)), jnp.where(last_row, y_7, roll_up(y))))
    f_low, f_up = join_layers([strip_scale * x for x in stress(split_layers(lower, strip_layers(lower)))])
    strip_second, strip_sums = [], (0.0,) * 4
    strip_free = tiles[5] > 0.0
    free_inv = jnp.where(strip_free, strip_inv, 1.0)
    for c in range(3):
        f = node_forces({m: f_low[c][m] + lane_roll(f_up[c][m], SLOTS) for m in PLANE}, 1)
        image = jnp.where(strip_free, f, tiles[c])
        s = image - tiles[c]
        strip_second.append(s * free_inv)
        strip_sums = products(strip_sums, tiles[c] * free_inv, image, image * free_inv, s, strip_second[c])
        edges[c] = strip_base[c]
        edges[3 + c] = strip_second[c]
    ends = [jnp.where(slot == 4, x, lane_roll(x, 4)) for x in strip_second]
    lower = [plane_modes(x, lane_roll(x, -1), roll_up(x), roll_up(lane_roll(x, -1))) for x in strip_second]
    m = split_layers(lower, strip_layers(lower))
    strip_e = strip_scale * inner(stress(m), m)

    def box(k):
        scales[k, 0:rows, :] = table(element_rows(phase, k, layers), PHASE_STIFFNESS)
        scales[k, 6:7, :] = hi[pl.ds(cn + k, 1), :]
        scales[k, 7:8, :] = lo[pl.ds(cn + layers + k, 1), :]
        x = scales[k]
        r = node_rows(x, spread(lo, cn + k))
        return x, r + jnp.where(lane == 0, lane_roll(edge_rows, -SLOTS * k), lane_roll(r, 1))

    def first_layer(k, around_node):
        inv = 1.0 / (KE_DIAGONAL * around_node)
        inverse[k] = inv
        out = []
        for c in range(3):
            q = c * nodes + k
            residual[q, 0:rows, :] = rhs[c][k]
            residual[q, 6:7, :] = hi[pl.ds(q, 1), :]
            residual[q, 7:8, :] = lo[pl.ds(q, 1), :]
            x = residual[q] * inv
            base[q] = x
            y = lane_roll(x, -1)
            x_up = jnp.where(last_row, spread(hi, row_7 + q), roll_up(x))
            y_up = jnp.where(last_row, spread(turned, row_7 - first_7 + q), roll_up(y))
            out.append(plane_modes(x, y, x_up, y_up))
        return out

    def finish_layer(k, f, totals):
        inv = inverse[k]
        frees[k, 0:rows, :] = 1.0 - fixed[k].astype(jnp.float32)
        frees[k, 6:7, :] = hi[pl.ds(cn + layers + k, 1), :]
        frees[k, 7:8, :] = jnp.zeros((1, LANES), jnp.float32)
        free = frees[k] > 0.0
        inv = jnp.where(free, inv, 1.0)
        a, rest = totals[0], totals[1:]
        for c in range(3):
            q = c * nodes + k
            r0 = residual[q]
            d0 = r0 * inv
            image = jnp.where(free, node_forces(f[c], 1), d0)
            s = image - r0
            v = s * inv
            ends_now = lane_roll(ends[c], LANES - 1 - (SLOTS * k + 4))
            second[q] = jnp.where((lane == 0) | (lane == LANES - 1), ends_now, v)
            a, rest = a + r0 * d0, products(rest, d0, image, image * inv, s, v)
        return (a,) + rest

    def flat(x):
        return tuple(x[c][m] for c in range(3) for m in PLANE)

    def unflat(x):
        return [{m: x[4 * c + i] for i, m in enumerate(PLANE)} for c in range(3)]

    zero = jnp.zeros((8, LANES), jnp.float32)

    def element(k, low_modes, high_modes, scale, pending, totals):
        g = stress(split_layers(low_modes, high_modes))
        f_lower, f_upper = join_layers([scale * x for x in g])
        done = [{m: pending[c][m] + f_lower[c][m] for m in PLANE} for c in range(3)]
        return f_upper, finish_layer(k, done, totals)

    def forward(k, carry):
        low_modes, pending, totals, scale, b = carry
        next_scale, next_b = box(k + 1)
        high = first_layer(k + 1, b + next_b)
        f_upper, totals = element(k, unflat(low_modes), high, scale, unflat(pending), totals)
        return flat(high), flat(f_upper), totals, next_scale, next_b

    scale, b = box(0)
    carry = (flat(first_layer(0, b)), (zero,) * 12, (zero,) * 5, scale, b)
    low_modes, pending, totals, scale, b = lax.fori_loop(0, layers - 1, forward, carry, unroll=True)
    high = first_layer(layers, b)
    f_upper, totals = element(layers - 1, unflat(low_modes), high, scale, unflat(pending), totals)
    totals = finish_layer(layers, f_upper, totals)

    def second_layer(k):
        out = []
        for c in range(3):
            x = second[c * nodes + k]
            y = lane_roll(x, -1)
            out.append(plane_modes(x, y, roll_up(x), roll_up(y)))
        return out

    def again(k, carry):
        low_modes, total = carry
        high = second_layer(k + 1)
        m = split_layers(unflat(low_modes), high)
        return flat(high), total + scales[k] * inner(stress(m), m)

    _, total = lax.fori_loop(0, layers, again, (flat(second_layer(0)), zero), unroll=True)
    mine = row < rows
    inside = mine & (lane > 0) & (lane < LANES - 1)
    at_ends = mine & ((slot == 1) | (slot == 4))
    totals = [jnp.where(mine, totals[0], 0.0)] + [
        jnp.where(inside, x, 0.0) + jnp.where(at_ends, y, 0.0) for x, y in zip(totals[1:], strip_sums)
    ]
    totals.append(
        jnp.where(mine & (lane < LANES - 1), total, 0.0) + jnp.where(mine & (slot == 4), strip_e, 0.0)
    )
    rows_of = zero
    for i, x in enumerate(totals):
        rows_of = jnp.where(row == i, jnp.broadcast_to(jnp.sum(x, axis=0, keepdims=True), (8, LANES)), rows_of)
    rows_of = jnp.broadcast_to(jnp.sum(rows_of, axis=1, keepdims=True), (8, LANES))
    sums[...] = jnp.sum(jnp.where(lane == row, rows_of, 0.0), axis=0, keepdims=True)


def energy_kernel(base, second, edges, phase, energy):
    nodes = base.shape[0] // 3
    layers = nodes - 1
    rows = phase.shape[0] // layers
    lane = lanes()

    def layer(field, first_edge, k):
        out = []
        for c in range(3):
            fill = lane_roll(edges[first_edge + c], LANES - 1 - (SLOTS * k + 5))
            out.append(
                in_plane(
                    field[c * nodes + k],
                    lambda t: jnp.where(lane == LANES - 1, fill, lane_roll(t, -1)),
                    lambda t: pltpu.roll(t, 7, 0),
                )
            )
        return out

    low = layer(base, 0, 0), layer(second, 3, 0)
    for k in range(layers):
        high = layer(base, 0, k + 1), layer(second, 3, k + 1)
        m, n = split_layers(low[0], high[0]), split_layers(low[1], high[1])
        g, h = stress(m), stress(n)
        slope = -table(element_rows(phase, k, layers), PHASE_SLOPE)
        for which, value in enumerate((inner(g, m), inner(h, m), inner(h, n))):
            energy[which, pl.ds(k, rows, stride=layers), :] = slope * value[0:rows]
        low = high


def combine_kernel(base, second, energy, sums, displacement, sensitivity):
    lane = lax.broadcasted_iota(jnp.int32, (1, LANES), 1)
    a, curve, plain, shifted, cross, bend = (
        jnp.sum(jnp.where(lane == i, sums[...], 0.0), axis=1, keepdims=True) for i in range(6)
    )
    slope = curve / a
    alpha = a / curve
    less = 1.0 - slope
    rest = jnp.where(slope < 0.5, plain - slope * curve, shifted - less * less * a)
    bend = bend + 2.0 * less * cross + less * less * curve
    alpha_next = rest / (bend - rest * rest / curve)
    beta = alpha * alpha * rest / a
    first = alpha + alpha_next * beta - alpha * alpha_next * less
    other = -alpha * alpha_next
    comps, nodes, rows, width = displacement.shape
    for c in range(comps):
        for k in range(nodes):
            q = c * nodes + k
            displacement[c, k] = (first * base[q] + other * second[q])[0:rows]
    sensitivity[...] = (first * first) * energy[0] + (2.0 * first * other) * energy[1] + (other * other) * energy[2]


def exchange_pairs(one, two, axis):
    count = lax.axis_size(axis)
    far = lax.ppermute(two, axis, [(i, (i - 1) % count if i % 2 == 0 else (i + 1) % count) for i in range(count)])
    near = lax.ppermute(one, axis, [(i, i ^ 1) for i in range(count)])
    return near, far


def exchange(down, up, axis):
    count = lax.axis_size(axis)
    low = lax.ppermute(up, axis, [(i, (i + 1) % count) for i in range(count)])
    high = lax.ppermute(down, axis, [((i + 1) % count, i) for i in range(count)])
    return high, low


def total_over(x, axis):
    count = lax.axis_size(axis)
    if count & (count - 1):
        return lax.psum(x, axis)
    step = 1
    while step < count:
        width = 4 if count // step >= 4 else 2
        if axis == "gx" and count == 4:
            to = [[(i, (i + by) % 4) for i in range(4)] for by in (3, 2, 1)]
        else:
            to = [[(i, i ^ (step * by)) for i in range(count)] for by in range(1, width)]
        x = functools.reduce(jnp.add, [lax.ppermute(x, axis, pairs) for pairs in to], x)
        step *= width
    return x


def body(force, phase, fixed):
    comps, nodes, rows, width = force.shape
    layers = nodes - 1
    phase = phase.transpose(1, 0, 2).reshape(rows * layers, width)
    rhs = [(1 - fixed).astype(jnp.float32) * force[c] for c in range(comps)]
    f32 = jnp.float32
    paired = lax.axis_size("gy") % 2 == 0
    column = jax.ShapeDtypeStruct((2, 8, LANES), f32)
    messages = (jax.ShapeDtypeStruct((DOWN, LANES), f32), jax.ShapeDtypeStruct((UP, LANES), f32))
    strips = jax.ShapeDtypeStruct((6, 8, LANES), f32)

    def call(kernel, out_shape, scratch=()):
        return pl.pallas_call(kernel, out_shape=out_shape, scratch_shapes=scratch, compiler_params=PARAMS)

    own, col1, col2 = call(
        functools.partial(column_kernel, paired),
        (jax.ShapeDtypeStruct((5, 8, LANES), f32), column, column),
        [pltpu.VMEM((5, 8, LANES), f32)],
    )(*rhs, phase, fixed)
    down, up, pair = call(row_kernel, messages + (jax.ShapeDtypeStruct((layers, LANES), f32),))(*rhs, phase, fixed)
    near, far = (exchange_pairs if paired else exchange)(col1, col2, "gy")
    strip, down, up = call(
        functools.partial(strip_kernel, nodes, paired),
        (strips,) + messages,
        [pltpu.VMEM((32, LANES), f32)],
    )(own, far, near, down, up, pair)
    high, low = exchange(down, up, "gx")
    field = jax.ShapeDtypeStruct((comps * nodes, 8, LANES), f32)
    base, second, edges, sums = call(
        operator_kernel,
        (
            field,
            field,
            strips,
            jax.ShapeDtypeStruct((1, LANES), f32),
        ),
        [
            pltpu.VMEM((layers, 8, LANES), f32),
            pltpu.VMEM((nodes, 8, LANES), f32),
            pltpu.VMEM((comps * nodes, 8, LANES), f32),
            pltpu.VMEM((nodes, 8, LANES), f32),
            pltpu.VMEM((DOWN - (comps * nodes + layers + nodes) // 8 * 8, LANES), f32),
        ],
    )(*rhs, phase, fixed, strip, low, high)
    energy = call(energy_kernel, jax.ShapeDtypeStruct((3,) + phase.shape, f32))(base, second, edges, phase)
    sums = total_over(total_over(sums, "gx"), "gy")
    displacement, sensitivity = call(
        combine_kernel,
        (jax.ShapeDtypeStruct(force.shape, f32), jax.ShapeDtypeStruct(phase.shape, f32)),
    )(base, second, energy, sums)
    return displacement, sensitivity.reshape(rows, layers, width).transpose(1, 0, 2)


def solution(mesh):
    return jax.shard_map(
        body,
        mesh=mesh,
        in_specs=(
            P(None, None, ("parts", "gx"), "gy"),
            P(None, ("parts", "gx"), "gy"),
            P(None, ("parts", "gx"), "gy"),
        ),
        out_specs=(P(None, None, ("parts", "gx"), "gy"), P(None, ("parts", "gx"), "gy")),
        check_vma=False,
    )
```

```python
import functools

import jax
import jax.numpy as jnp
import numpy as np
from jax import lax
from jax.experimental import pallas as pl
from jax.experimental.pallas import tpu as pltpu
from jax.sharding import PartitionSpec as P

PHASE_STIFFNESS = (0.125, 0.343, 0.614, 1.0)
PHASE_SLOPE = (0.75, 1.47, 2.17, 3.0)
POISSON = 0.3
LAME = POISSON / ((1.0 + POISSON) * (1.0 - 2.0 * POISSON))
SHEAR = 1.0 / (2.0 * (1.0 + POISSON))
KE_DIAGONAL = (LAME + 4.0 * SHEAR) / 9.0

SLOTS = 7
LANES = 128
DOWN, DOWN_CORNERS = 144, 135
UP, UP_CORNERS = 144, 83

PARAMS = pltpu.CompilerParams(vmem_limit_bytes=32 * 1024 * 1024)


def lanes():
    return lax.broadcasted_iota(jnp.int32, (8, LANES), 1)


def sublanes():
    return lax.broadcasted_iota(jnp.int32, (8, LANES), 0)


def table(phase, values):
    out = jnp.full(phase.shape, values[3], jnp.float32)
    for index in (2, 1, 0):
        out = jnp.where(phase == index, jnp.float32(values[index]), out)
    return out


def element_rows(ref, k, layers):
    return ref[pl.ds(k, ref.shape[0] // layers, stride=layers), :]


def lane_roll(x, by):
    if isinstance(by, int):
        by = by % LANES
        return x if by == 0 else pltpu.roll(x, by, 1)
    return pltpu.roll(x, lax.rem(by + LANES, LANES), 1)


def is_even(axis):
    return lax.rem(lax.axis_index(axis), 2) == 0


def gather(nodes, *items):
    lane = lanes()
    slot = jnp.where(lane < nodes * SLOTS, lax.rem(lane, SLOTS), SLOTS)
    out = jnp.zeros((8, LANES), jnp.float32)
    for plane, by, first, count in items:
        out = jnp.where((slot >= first) & (slot < first + count), lane_roll(plane, by), out)
    return out


def column_kernel(paired, rhs_0, rhs_1, rhs_2, phase, fixed, own, col1, col2, pad):
    rhs = (rhs_0, rhs_1, rhs_2)
    nodes, rows, width = rhs_0.shape
    layers = nodes - 1
    lane = lax.broadcasted_iota(jnp.int32, (rows, LANES), 1)
    even = is_even("gy") if paired else True
    pad[...] = jnp.zeros(pad.shape, jnp.float32)
    planes = [jnp.zeros((rows, LANES), jnp.float32)] * 5
    for k in range(nodes):
        here = (lane >= k * SLOTS) & (lane < k * SLOTS + 5)
        values = [rhs[c][k] for c in range(3)]
        values.append(table(element_rows(phase, k, layers), PHASE_STIFFNESS) if k < layers else None)
        values.append((1 - fixed[k]).astype(jnp.float32))
        for p, value in enumerate(values):
            if value is not None:
                planes[p] = jnp.where(here, lane_roll(value, k * SLOTS + 3), planes[p])
    for p in range(5):
        pad[p, 0:rows, :] = planes[p]
        planes[p] = pad[p]
        own[p] = planes[p]
    high = [
        gather(nodes, (planes[0], -2, 0, 1), (planes[1], -1, 1, 1), (planes[2], 0, 2, 1), (planes[3], 2, 3, 2)),
        jnp.zeros((8, LANES), jnp.float32),
    ]
    low = [
        gather(nodes, (planes[0], -3, 0, 2), (planes[1], -1, 2, 2), (planes[2], 1, 4, 2), (planes[4], 3, 6, 1)),
        planes[3],
    ]
    for p in range(2):
        if paired:
            col1[p] = jnp.where(even, high[p], low[p])
            col2[p] = jnp.where(even, low[p], high[p])
        else:
            col1[p] = low[p]
            col2[p] = high[p]


def row_kernel(rhs_0, rhs_1, rhs_2, phase, fixed, down, up, pair):
    rhs = (rhs_0, rhs_1, rhs_2)
    nodes, rows, width = rhs_0.shape
    layers, cn = nodes - 1, 3 * nodes
    for k in range(nodes):
        for c in range(3):
            q = c * nodes + k
            down[q : q + 1, :] = rhs[c][k, 0:1]
            down[cn + layers + nodes + q : cn + layers + nodes + q + 1, :] = rhs[c][k, 1:2]
            up[q : q + 1, :] = rhs[c][k, rows - 1 : rows]
        at = cn + layers + k
        down[at : at + 1, :] = (1 - fixed[k, 0:1]).astype(jnp.float32)
    scale = [table(phase[i * layers : (i + 1) * layers], PHASE_STIFFNESS) for i in (0, 1, rows - 2, rows - 1)]
    down[cn : cn + layers, :] = scale[0]
    up[cn : cn + layers, :] = scale[2]
    up[cn + layers : cn + 2 * layers, :] = scale[3]
    pair[...] = scale[0] + scale[1]
    down[DOWN_CORNERS:, :] = jnp.zeros((DOWN - DOWN_CORNERS, LANES), jnp.float32)
    up[UP_CORNERS:, :] = jnp.zeros((UP - UP_CORNERS, LANES), jnp.float32)


def strip_kernel(nodes, paired, own, got2, got1, up, strip, up_out):
    even_y = is_even("gy") if paired else True
    if paired:
        from_low = jnp.where(even_y, got2[0], got1[0])
        from_high = [jnp.where(even_y, got1[p], got2[p]) for p in range(2)]
    else:
        from_low, from_high = got2[0], [got1[p] for p in range(2)]
    planes = [
        gather(nodes, (from_low, -c, 0, 1), (own[c], -2, 1, 2), (own[c], 2, 3, 2), (from_high[0], 5 - 2 * c, 5, 2))
        for c in range(3)
    ]
    scale = own[3]
    planes.append(gather(nodes, (from_low, -3, 0, 2), (scale, -1, 2, 1), (scale, 3, 3, 3), (from_high[1], 3, 6, 1)))
    planes.append(gather(nodes, (from_low, -4, 0, 1), (scale, -2, 1, 2), (scale, 2, 3, 2), (from_high[1], 2, 5, 2)))
    planes.append(gather(nodes, (own[4], -2, 1, 1), (own[4], 2, 4, 1), (from_high[0], -1, 5, 1)))
    rows = 6
    up_out[...] = up[...]
    for p, plane in enumerate(planes):
        strip[p] = plane
        up_out[UP_CORNERS + 2 * p : UP_CORNERS + 2 * p + 2, :] = plane[rows - 2 : rows]


def lower_kernel(nodes, strip, down, pair, down_out, dense):
    planes = [strip[p] for p in range(6)]
    down_out[...] = down[...]
    around = planes[3] + planes[4]
    around = around + pltpu.roll(around, 1, 0)
    around = KE_DIAGONAL * (around + lane_roll(around, SLOTS))
    inv = jnp.where(around > 0.0, 1.0 / around, 0.0)
    corners = [plane[0:1] for plane in planes[0:3]]
    corners += [(plane * inv)[1:2] for plane in planes[0:3]]
    corners += [plane[0:1] for plane in planes[3:6]]
    for p, value in enumerate(corners):
        down_out[DOWN_CORNERS + p : DOWN_CORNERS + p + 1, :] = value
    layers, cn = nodes - 1, 3 * nodes
    tall = lax.broadcasted_iota(jnp.int32, (layers, LANES), 0)
    wide = lax.broadcasted_iota(jnp.int32, (layers, LANES), 1)
    edge = jnp.broadcast_to(planes[4][0:1] + planes[4][1:2], (layers, LANES))
    edge = jnp.sum(jnp.where(wide == SLOTS * tall, edge, 0.0), axis=1, keepdims=True)
    dense[...] = jnp.zeros(dense.shape, jnp.float32)
    dense[1 : layers + 1, :] = pair[...] + jnp.where(wide == 0, edge, pltpu.roll(pair[...], 1, 1))
    inv = 1.0 / (KE_DIAGONAL * (dense[0:nodes, :] + dense[1 : nodes + 1, :]))
    for c in range(3):
        at = cn + layers + nodes + c * nodes
        down_out[at : at + nodes, :] = down[at : at + nodes, :] * inv


PLANE = ("", "1", "2", "12")


def split_layers(lo, hi):
    sums = [{m: lo[c][m] + hi[c][m] for m in ("1", "2", "12")} for c in range(3)]
    diffs = [{m: hi[c][m] - lo[c][m] for m in PLANE} for c in range(3)]
    u, v, w = range(3)
    return (
        diffs[u][""], sums[v]["1"], sums[w]["2"],
        sums[u]["1"] + diffs[v][""], sums[u]["2"] + diffs[w][""], sums[v]["2"] + sums[w]["1"],
        diffs[u]["1"], sums[w]["12"], diffs[u]["2"], sums[v]["12"], diffs[v]["1"], diffs[w]["2"],
        sums[u]["12"], diffs[v]["2"], diffs[w]["1"],
        diffs[u]["12"], diffs[v]["12"], diffs[w]["12"],
    )


def stress(m):
    one, two, three = 1.0 / 16.0, 1.0 / 48.0, 1.0 / 144.0
    trace = (LAME * one) * (m[0] + m[1] + m[2])
    out = [trace + (2.0 * SHEAR * one) * m[i] for i in range(3)]
    out += [(SHEAR * one) * m[i] for i in (3, 4, 5)]
    own, other = (LAME + 3.0 * SHEAR) * two, LAME * two
    for i in (6, 8, 10):
        out += [own * m[i] + other * m[i + 1], own * m[i + 1] + other * m[i]]
    total = m[12] + m[13] + m[14]
    out += [(SHEAR * two) * (m[i] + total) for i in (12, 13, 14)]
    out += [((LAME + 4.0 * SHEAR) * three) * m[i] for i in (15, 16, 17)]
    return out


def inner(g, m):
    parts = [g[i] * m[i] for i in range(18)]
    while len(parts) > 1:
        parts = [parts[i] + parts[i + 1] if i + 1 < len(parts) else parts[i] for i in range(0, len(parts), 2)]
    return parts[0]


def join_layers(g):
    sums = [
        {"1": g[3], "2": g[4], "12": g[12]},
        {"1": g[1], "2": g[5], "12": g[9]},
        {"1": g[5], "2": g[2], "12": g[7]},
    ]
    diffs = [
        {"": g[0], "1": g[6], "2": g[8], "12": g[15]},
        {"": g[3], "1": g[10], "2": g[13], "12": g[16]},
        {"": g[4], "1": g[14], "2": g[11], "12": g[17]},
    ]
    lower = [{m: (sums[c][m] - diffs[c][m] if m else -diffs[c][m]) for m in PLANE} for c in range(3)]
    upper = [{m: (sums[c][m] + diffs[c][m] if m else diffs[c][m]) for m in PLANE} for c in range(3)]
    return lower, upper


def in_plane(x, right, up):
    y = right(x)
    near, far = x + y, y - x
    near_up, far_up = up(near), up(far)
    return {"": near + near_up, "1": near_up - near, "2": far + far_up, "12": far_up - far}


def out_of_plane(f, right, up):
    plain = (f[""] - f["2"]) + right(f[""] + f["2"])
    steep = (f["1"] - f["12"]) + right(f["1"] + f["12"])
    return (plain - steep) + up(plain + steep)


def operator_kernel(
    rhs_0, rhs_1, rhs_2, phase, fixed, strip, lo, hi,
    base, second, edges, sums,
    scales, frees, residual, inverse, turned,
):
    rhs, comps = (rhs_0, rhs_1, rhs_2), 3
    nodes, rows, width = rhs_0.shape
    layers = nodes - 1
    lane, row = lanes(), sublanes()
    last_row, below = row == 6, row == 7
    cn = comps * nodes
    def spread(ref, at):
        return jnp.broadcast_to(ref[pl.ds(at, 1), :], (8, LANES))

    def roll_up(x):
        return pltpu.roll(x, 7, 0)

    def roll_down(x):
        return pltpu.roll(x, 1, 0)

    def node_rows(x, x_m2):
        return x + jnp.where(below, x_m2, roll_down(x))

    def plane_modes(x, y, x_up, y_up):
        near, far, near_up, far_up = x + y, y - x, x_up + y_up, y_up - x_up
        return {"": near + near_up, "1": near_up - near, "2": far + far_up, "12": far_up - far}

    def node_forces(f, by):
        sides = []
        for sign in (-1, 1):
            plain = f[""] + f["2"] if sign > 0 else f[""] - f["2"]
            steep = f["1"] + f["12"] if sign > 0 else f["1"] - f["12"]
            sides.append((plain - steep) + roll_down(plain + steep))
        return sides[0] + lane_roll(sides[1], by)

    def products(totals, d0, image, z, s, v):
        return tuple(t + x for t, x in zip(totals, (d0 * image, image * z, s * v, v * image)))

    def above(p):
        return spread(hi, DOWN_CORNERS + p)

    def under(p, which):
        return spread(lo, UP_CORNERS + 2 * p + which)

    tiles = [
        jnp.where(row < 6, strip[p], jnp.where(last_row, above(p if p < 3 else p + 3), under(p, 1))) for p in range(6)
    ]
    left, right = tiles[3], tiles[4]
    edge_rows = node_rows(right, under(4, 0))
    row_7 = cn + layers + nodes
    first_7 = row_7 // 8 * 8
    turned[...] = pltpu.roll(hi[first_7:DOWN, :], LANES - 1, 1)

    def strip_diagonal(x):
        return KE_DIAGONAL * (x + lane_roll(x, SLOTS))

    strip_diag = strip_diagonal(node_rows(left + right, under(3, 0) + under(4, 0)))
    strip_inv = jnp.where(strip_diag > 0.0, 1.0 / strip_diag, 0.0)
    slot = lax.rem(lane, SLOTS)
    strip_scale = jnp.where((slot == 2) | (slot == 6), 0.0, right)
    strip_base = [tiles[c] * strip_inv for c in range(3)]

    def strip_layers(modes):
        return [{m: lane_roll(modes[c][m], -SLOTS) for m in PLANE} for c in range(3)]

    lower = []
    for c in range(3):
        x, x_7 = strip_base[c], above(3 + c)
        y, y_7 = lane_roll(x, -1), lane_roll(x_7, -1)
        lower.append(plane_modes(x, y, jnp.where(last_row, x_7, roll_up(x)), jnp.where(last_row, y_7, roll_up(y))))
    f_low, f_up = join_layers([strip_scale * x for x in stress(split_layers(lower, strip_layers(lower)))])
    strip_second, strip_sums = [], (0.0,) * 4
    strip_free = tiles[5] > 0.0
    free_inv = jnp.where(strip_free, strip_inv, 1.0)
    for c in range(3):
        f = node_forces({m: f_low[c][m] + lane_roll(f_up[c][m], SLOTS) for m in PLANE}, 1)
        image = jnp.where(strip_free, f, tiles[c])
        s = image - tiles[c]
        strip_second.append(s * free_inv)
        strip_sums = products(strip_sums, tiles[c] * free_inv, image, image * free_inv, s, strip_second[c])
        edges[c] = strip_base[c]
        edges[3 + c] = strip_second[c]
    ends = [jnp.where(slot == 4, x, lane_roll(x, 4)) for x in strip_second]
    lower = [plane_modes(x, lane_roll(x, -1), roll_up(x), roll_up(lane_roll(x, -1))) for x in strip_second]
    m = split_layers(lower, strip_layers(lower))
    strip_e = strip_scale * inner(stress(m), m)

    def box(k):
        scales[k, 0:rows, :] = table(element_rows(phase, k, layers), PHASE_STIFFNESS)
        scales[k, 6:7, :] = hi[pl.ds(cn + k, 1), :]
        scales[k, 7:8, :] = lo[pl.ds(cn + layers + k, 1), :]
        x = scales[k]
        r = node_rows(x, spread(lo, cn + k))
        return x, r + jnp.where(lane == 0, lane_roll(edge_rows, -SLOTS * k), lane_roll(r, 1))

    def first_layer(k, around_node):
        inv = 1.0 / (KE_DIAGONAL * around_node)
        inverse[k] = inv
        out = []
        for c in range(3):
            q = c * nodes + k
            residual[q, 0:rows, :] = rhs[c][k]
            residual[q, 6:7, :] = hi[pl.ds(q, 1), :]
            residual[q, 7:8, :] = lo[pl.ds(q, 1), :]
            x = residual[q] * inv
            base[q] = x
            y = lane_roll(x, -1)
            x_up = jnp.where(last_row, spread(hi, row_7 + q), roll_up(x))
            y_up = jnp.where(last_row, spread(turned, row_7 - first_7 + q), roll_up(y))
            out.append(plane_modes(x, y, x_up, y_up))
        return out

    def finish_layer(k, f, totals):
        inv = inverse[k]
        frees[k, 0:rows, :] = 1.0 - fixed[k].astype(jnp.float32)
        frees[k, 6:7, :] = hi[pl.ds(cn + layers + k, 1), :]
        frees[k, 7:8, :] = jnp.zeros((1, LANES), jnp.float32)
        free = frees[k] > 0.0
        inv = jnp.where(free, inv, 1.0)
        a, rest = totals[0], totals[1:]
        for c in range(3):
            q = c * nodes + k
            r0 = residual[q]
            d0 = r0 * inv
            image = jnp.where(free, node_forces(f[c], 1), d0)
            s = image - r0
            v = s * inv
            ends_now = lane_roll(ends[c], LANES - 1 - (SLOTS * k + 4))
            second[q] = jnp.where((lane == 0) | (lane == LANES - 1), ends_now, v)
            a, rest = a + r0 * d0, products(rest, d0, image, image * inv, s, v)
        return (a,) + rest

    def flat(x):
        return tuple(x[c][m] for c in range(3) for m in PLANE)

    def unflat(x):
        return [{m: x[4 * c + i] for i, m in enumerate(PLANE)} for c in range(3)]

    zero = jnp.zeros((8, LANES), jnp.float32)

    def element(k, low_modes, high_modes, scale, pending, totals):
        g = stress(split_layers(low_modes, high_modes))
        f_lower, f_upper = join_layers([scale * x for x in g])
        done = [{m: pending[c][m] + f_lower[c][m] for m in PLANE} for c in range(3)]
        return f_upper, finish_layer(k, done, totals)

    def forward(k, carry):
        low_modes, pending, totals, scale, b = carry
        next_scale, next_b = box(k + 1)
        high = first_layer(k + 1, b + next_b)
        f_upper, totals = element(k, unflat(low_modes), high, scale, unflat(pending), totals)
        return flat(high), flat(f_upper), totals, next_scale, next_b

    scale, b = box(0)
    carry = (flat(first_layer(0, b)), (zero,) * 12, (zero,) * 5, scale, b)
    low_modes, pending, totals, scale, b = lax.fori_loop(0, layers - 1, forward, carry, unroll=True)
    high = first_layer(layers, b)
    f_upper, totals = element(layers - 1, unflat(low_modes), high, scale, unflat(pending), totals)
    totals = finish_layer(layers, f_upper, totals)

    def second_layer(k):
        out = []
        for c in range(3):
            x = second[c * nodes + k]
            y = lane_roll(x, -1)
            out.append(plane_modes(x, y, roll_up(x), roll_up(y)))
        return out

    def again(k, carry):
        low_modes, total = carry
        high = second_layer(k + 1)
        m = split_layers(unflat(low_modes), high)
        return flat(high), total + scales[k] * inner(stress(m), m)

    _, total = lax.fori_loop(0, layers, again, (flat(second_layer(0)), zero), unroll=True)
    mine = row < rows
    inside = mine & (lane > 0) & (lane < LANES - 1)
    at_ends = mine & ((slot == 1) | (slot == 4))
    totals = [jnp.where(mine, totals[0], 0.0)] + [
        jnp.where(inside, x, 0.0) + jnp.where(at_ends, y, 0.0) for x, y in zip(totals[1:], strip_sums)
    ]
    totals.append(
        jnp.where(mine & (lane < LANES - 1), total, 0.0) + jnp.where(mine & (slot == 4), strip_e, 0.0)
    )
    rows_of = zero
    for i, x in enumerate(totals):
        rows_of = jnp.where(row == i, jnp.broadcast_to(jnp.sum(x, axis=0, keepdims=True), (8, LANES)), rows_of)
    rows_of = jnp.broadcast_to(jnp.sum(rows_of, axis=1, keepdims=True), (8, LANES))
    sums[...] = jnp.sum(jnp.where(lane == row, rows_of, 0.0), axis=0, keepdims=True)


def energy_kernel(base, second, edges, phase, energy):
    nodes = base.shape[0] // 3
    layers = nodes - 1
    rows = phase.shape[0] // layers
    lane = lanes()

    def layer(field, first_edge, k):
        out = []
        for c in range(3):
            fill = lane_roll(edges[first_edge + c], LANES - 1 - (SLOTS * k + 5))
            out.append(
                in_plane(
                    field[c * nodes + k],
                    lambda t: jnp.where(lane == LANES - 1, fill, lane_roll(t, -1)),
                    lambda t: pltpu.roll(t, 7, 0),
                )
            )
        return out

    low = layer(base, 0, 0), layer(second, 3, 0)
    for k in range(layers):
        high = layer(base, 0, k + 1), layer(second, 3, k + 1)
        m, n = split_layers(low[0], high[0]), split_layers(low[1], high[1])
        g, h = stress(m), stress(n)
        slope = -table(element_rows(phase, k, layers), PHASE_SLOPE)
        for which, value in enumerate((inner(g, m), inner(h, m), inner(h, n))):
            energy[which, pl.ds(k, rows, stride=layers), :] = slope * value[0:rows]
        low = high


def combine_kernel(base, second, energy, sums, displacement, sensitivity):
    lane = lax.broadcasted_iota(jnp.int32, (1, LANES), 1)
    a, curve, plain, shifted, cross, bend = (
        jnp.sum(jnp.where(lane == i, sums[...], 0.0), axis=1, keepdims=True) for i in range(6)
    )
    slope = curve / a
    alpha = a / curve
    less = 1.0 - slope
    rest = jnp.where(slope < 0.5, plain - slope * curve, shifted - less * less * a)
    bend = bend + 2.0 * less * cross + less * less * curve
    alpha_next = rest / (bend - rest * rest / curve)
    beta = alpha * alpha * rest / a
    first = alpha + alpha_next * beta - alpha * alpha_next * less
    other = -alpha * alpha_next
    comps, nodes, rows, width = displacement.shape
    for c in range(comps):
        for k in range(nodes):
            q = c * nodes + k
            displacement[c, k] = (first * base[q] + other * second[q])[0:rows]
    sensitivity[...] = (first * first) * energy[0] + (2.0 * first * other) * energy[1] + (other * other) * energy[2]


def exchange_pairs(one, two, axis):
    count = lax.axis_size(axis)
    far = lax.ppermute(two, axis, [(i, (i - 1) % count if i % 2 == 0 else (i + 1) % count) for i in range(count)])
    near = lax.ppermute(one, axis, [(i, i ^ 1) for i in range(count)])
    return near, far


def exchange(down, up, axis):
    count = lax.axis_size(axis)
    low = lax.ppermute(up, axis, [(i, (i + 1) % count) for i in range(count)])
    high = lax.ppermute(down, axis, [((i + 1) % count, i) for i in range(count)])
    return high, low


def total_over(x, axis):
    count = lax.axis_size(axis)
    if count & (count - 1):
        return lax.psum(x, axis)
    step = 1
    while step < count:
        width = 4 if count // step >= 4 else 2
        if axis == "gx" and count == 4:
            to = [[(i, (i + by) % 4) for i in range(4)] for by in (3, 2, 1)]
        else:
            to = [[(i, i ^ (step * by)) for i in range(count)] for by in range(1, width)]
        x = functools.reduce(jnp.add, [lax.ppermute(x, axis, pairs) for pairs in to], x)
        step *= width
    return x


def body(force, phase, fixed):
    comps, nodes, rows, width = force.shape
    layers = nodes - 1
    phase = phase.transpose(1, 0, 2).reshape(rows * layers, width)
    rhs = [(1 - fixed).astype(jnp.float32) * force[c] for c in range(comps)]
    f32 = jnp.float32
    paired = lax.axis_size("gy") % 2 == 0
    column = jax.ShapeDtypeStruct((2, 8, LANES), f32)
    messages = (jax.ShapeDtypeStruct((DOWN, LANES), f32), jax.ShapeDtypeStruct((UP, LANES), f32))
    strips = jax.ShapeDtypeStruct((6, 8, LANES), f32)

    def call(kernel, out_shape, scratch=()):
        return pl.pallas_call(kernel, out_shape=out_shape, scratch_shapes=scratch, compiler_params=PARAMS)

    own, col1, col2 = call(
        functools.partial(column_kernel, paired),
        (jax.ShapeDtypeStruct((5, 8, LANES), f32), column, column),
        [pltpu.VMEM((5, 8, LANES), f32)],
    )(*rhs, phase, fixed)
    down, up, pair = call(row_kernel, messages + (jax.ShapeDtypeStruct((layers, LANES), f32),))(*rhs, phase, fixed)
    near, far = (exchange_pairs if paired else exchange)(col1, col2, "gy")
    strip, up = call(functools.partial(strip_kernel, nodes, paired), (strips, messages[1]))(own, far, near, up)
    down = call(
        functools.partial(lower_kernel, nodes),
        messages[0],
        [pltpu.VMEM((32, LANES), f32)],
    )(strip, down, pair)
    high, low = exchange(down, up, "gx")
    field = jax.ShapeDtypeStruct((comps * nodes, 8, LANES), f32)
    base, second, edges, sums = call(
        operator_kernel,
        (
            field,
            field,
            strips,
            jax.ShapeDtypeStruct((1, LANES), f32),
        ),
        [
            pltpu.VMEM((layers, 8, LANES), f32),
            pltpu.VMEM((nodes, 8, LANES), f32),
            pltpu.VMEM((comps * nodes, 8, LANES), f32),
            pltpu.VMEM((nodes, 8, LANES), f32),
            pltpu.VMEM((DOWN - (comps * nodes + layers + nodes) // 8 * 8, LANES), f32),
        ],
    )(*rhs, phase, fixed, strip, low, high)
    energy = call(energy_kernel, jax.ShapeDtypeStruct((3,) + phase.shape, f32))(base, second, edges, phase)
    sums = total_over(total_over(sums, "gx"), "gy")
    displacement, sensitivity = call(
        combine_kernel,
        (jax.ShapeDtypeStruct(force.shape, f32), jax.ShapeDtypeStruct(phase.shape, f32)),
    )(base, second, energy, sums)
    return displacement, sensitivity.reshape(rows, layers, width).transpose(1, 0, 2)


def solution(mesh):
    return jax.shard_map(
        body,
        mesh=mesh,
        in_specs=(
            P(None, None, ("parts", "gx"), "gy"),
            P(None, ("parts", "gx"), "gy"),
            P(None, ("parts", "gx"), "gy"),
        ),
        out_specs=(P(None, None, ("parts", "gx"), "gy"), P(None, ("parts", "gx"), "gy")),
        check_vma=False,
    )
```
